32 devices in a mesh: mic: 4 (over x, core), bin: 8 (over z, y).
Axes of the slice: x: 2, y: 2, z: 4, core: 2. Of those that a mesh axis runs over, the one named last changes fastest.
Arguments:
- images: bfloat16 [128, 256, 256], P(('mic', 'bin')), may hold values from -6 to 6
- offsets: int32 [2, 128], P(None, ('mic', 'bin')), may hold values from 0 to 255
- ctf_group: int32 [128], P(('mic', 'bin')), may hold values from 0 to 63
- particle_bin: int32 [128], P(('mic', 'bin')), may hold values from 0 to 255, as said below
- bin_place: int32 [256], replicated, may hold values from 0 to 255, as said below
- defocus: float32 [64], replicated, may hold values from 40 to 160
- bfactor: float32 [64], replicated, may hold values from 0.2 to 2
- references: bfloat16 [256, 256, 256], P(('mic', 'bin')), may hold values from -6 to 6
Outputs:
- refined: bfloat16 [256, 256, 256], P(('mic', 'bin'))
- scores: float32 [128], P(('mic', 'bin'))
The draws below stay inside these ranges and needn't reach their ends.
Inputs may be any that keep to these rules, and one draw needn't show every extreme that they name: bin_place is a permutation. A particle's owner is bin_place[particle_bin] // 8, with bin index owner % 8 and mic index owner // 8. Of the 4 particles of one device, at most 1 have owners with one bin index, and some device of every mic row reaches it. `particle_bin`: within one mic row exactly 4 particles have owners with each bin index, and at most 2 have the same owner; in every mic row some owner has exactly 2. Several particles may share one bin.
All inputs are finite; a program needn't handle non-finite values.
Results may differ from the reference program's by a relative error of at most 0.0055.
Values may be sent and summed in bfloat16 or wider, within the bound.
No kernel may reach another device: no remote copies, remote signals or barrier semaphores. Data moves between devices by JAX's collectives and lax.ppermute only.
A program may use at most 64 MiB of HBM per device.

```python
import math
import jax
import jax.numpy as jnp
from jax import lax

IMAGE_SIDE = 256
PARTICLE_DEV = 4
BIN_DEV = 8
CTF_GROUPS = 64
ITERS = 2
PARTICLES = 128
BINS = 256
N_MIC = 4
N_BIN = 8


def routing(key):
    cap_first = (PARTICLE_DEV + N_BIN - 1) // N_BIN
    cap_second = (3 * PARTICLE_DEV + 2 * N_MIC - 1) // (2 * N_MIC)
    first_slots = N_BIN * cap_first
    second_slots = N_MIC * cap_second
    key_forced = jax.random.fold_in(key, 101)
    key_order = jax.random.fold_in(key, 102)
    key_mic = jax.random.fold_in(key, 103)
    key_second = jax.random.fold_in(key, 104)
    key_local = jax.random.fold_in(key, 105)
    key_other = jax.random.fold_in(key, 106)
    key_perm = jax.random.fold_in(key, 107)
    key_half = jax.random.fold_in(key, 108)
    slot_ids = jnp.arange(first_slots, dtype=jnp.int32)
    forced_bin = jax.random.randint(key_forced, (N_MIC, 1), 0, N_BIN)
    half_row = jax.random.randint(key_half, (), 0, N_MIC)
    row_ids = jnp.arange(N_MIC, dtype=jnp.int32)[:, None]
    forced_bin = jnp.where(row_ids == half_row, N_BIN // 2, forced_bin)
    scores_first = jax.random.randint(key_order, (N_MIC, first_slots), 0, 1 << 16) * first_slots + slot_ids[None, :]
    scores_first = jnp.where(slot_ids[None, :] // cap_first == forced_bin, slot_ids[None, :] - first_slots, scores_first)
    chosen = jnp.argsort(scores_first, axis=1)[:, :PARTICLE_DEV]
    rotation = chosen // cap_first
    device_ids = jnp.arange(N_BIN, dtype=jnp.int32)
    target_bin = (device_ids[None, :, None] + rotation[:, None, :]) % N_BIN
    mic_ids = jnp.arange(second_slots, dtype=jnp.int32)
    forced_mic = jax.random.randint(key_mic, (N_MIC, N_BIN, 1), 0, N_MIC)
    scores_second = jax.random.randint(key_second, (N_MIC, N_BIN, second_slots), 0, 1 << 16) * second_slots + mic_ids
    scores_second = jnp.where(mic_ids // cap_second == forced_mic, mic_ids - second_slots, scores_second)
    mic_slot = jnp.argsort(scores_second, axis=2)[:, :, :PARTICLE_DEV] // cap_second
    target_mic = jnp.take_along_axis(mic_slot, target_bin, axis=1)
    local_one = jax.random.randint(key_local, (N_MIC, N_BIN, PARTICLE_DEV), 0, BIN_DEV)
    local_two = jax.random.randint(key_other, (N_MIC, N_BIN, PARTICLE_DEV), 0, BIN_DEV)
    local_bin = jnp.minimum(local_one, local_two)
    places = ((target_mic * N_BIN + target_bin) * BIN_DEV + local_bin).reshape(-1)
    bin_scores = jax.random.randint(key_perm, (BINS,), 0, 1 << 12) * BINS + jnp.arange(BINS, dtype=jnp.int32)
    bin_place = jnp.argsort(bin_scores).astype(jnp.int32)
    bin_at_place = jnp.argsort(bin_place).astype(jnp.int32)
    particle_bin = jnp.take(bin_at_place, places).astype(jnp.int32)
    return (bin_place, particle_bin)


def draw_bin_place(key, part):
    return routing(key)[0]


def draw_particle_bin(key, part):
    return routing(key)[1]


def touch_ends(drawn, own_key, low, top_value):
    extent = drawn.shape
    place = [jax.random.randint(jax.random.fold_in(own_key, axis), (), 0, extent[axis]) for axis in range(len(extent))]
    drawn = drawn.at[tuple(place)].set(low)
    longest = extent.index(max(extent))
    place[longest] = (place[longest] + 1) % extent[longest]
    return drawn.at[tuple(place)].set(top_value)


def steps_of(rng, shape, pieces, smallest, high):
    def one(dim, parts):
        steps = jax.random.uniform(jax.random.fold_in(jax.random.fold_in(rng, 6), dim), (parts,), jnp.float32, smallest / len(pieces), high / len(pieces))
        return jnp.repeat(jnp.exp(steps), shape[dim] // parts).reshape((-1,) + (1,) * (len(shape) - dim - 1))

    factor_of = one(*pieces[0])
    for cut in pieces[1:]:
        factor_of = factor_of * one(*cut)
    return factor_of


def noise(key, extent, width, most, pieces=(), held_as=jnp.bfloat16):
    drawn = jax.random.normal(key, extent, jnp.float32) * width
    if len(pieces) > 0:
        drawn = steps_of(key, extent, pieces, -0.22, 0.18) * drawn
    return jnp.clip(drawn, min=-most, max=most).astype(held_as)


def setup_inputs(seed: int = 0) -> dict:
    seeds = jax.random.split(jax.random.key(seed), 9)
    return {
        "images": noise(seeds[0], (PARTICLES, IMAGE_SIDE, IMAGE_SIDE), 1.0, 6.0, ((0, 32),)),
        "offsets": touch_ends(jax.random.randint(seeds[1], (2, PARTICLES), 0, IMAGE_SIDE), jax.random.fold_in(seeds[1], 1), 0, IMAGE_SIDE - 1).astype(jnp.int32),
        "ctf_group": touch_ends(jax.random.randint(seeds[2], (PARTICLES,), 0, CTF_GROUPS), jax.random.fold_in(seeds[2], 1), 0, CTF_GROUPS - 1).astype(jnp.int32),
        "particle_bin": draw_particle_bin(jax.random.fold_in(seeds[8], 71), 0),
        "bin_place": draw_bin_place(jax.random.fold_in(seeds[8], 71), 0),
        "defocus": jnp.clip(jnp.exp(jax.random.uniform(seeds[5], (CTF_GROUPS,), jnp.float32, math.log(40.0), math.log(160.0))), 40.0, 160.0),
        "bfactor": jnp.clip(jnp.exp(jax.random.uniform(seeds[6], (CTF_GROUPS,), jnp.float32, math.log(0.2), math.log(2.0))), 0.2, 2.0),
        "references": noise(seeds[7], (BINS, IMAGE_SIDE, IMAGE_SIDE), 1.0, 6.0, ((0, 32),)),
    }


PRIOR_WEIGHT = 0.5
EPSILON = 1e-06
CONTRAST = 0.1
AMPLITUDE = math.sqrt(1.0 - CONTRAST * CONTRAST)

def hartley(image_side):
    row_index = lax.broadcasted_iota(jnp.int32, (image_side, image_side), 0)
    column_index = lax.broadcasted_iota(jnp.int32, (image_side, image_side), 1)
    phases = row_index * column_index % image_side
    angles = phases.astype(jnp.float32) * (2.0 * math.pi / image_side)
    return ((jnp.cos(angles) + jnp.sin(angles)) / math.sqrt(image_side)).astype(jnp.bfloat16)

def radius_square(image_side):
    frequency = jnp.arange(image_side, dtype=jnp.int32)
    folded = jnp.minimum(frequency, image_side - frequency).astype(jnp.float32)
    nyquist = image_side / 2.0
    square = (folded[:, None] * folded[:, None] + folded[None, :] * folded[None, :]) / (nyquist * nyquist)
    return square.reshape(image_side * image_side)

def ctf_rows(focus, damping, image_side):
    radial = radius_square(image_side)
    aberration = focus[:, None] * radial[None, :]
    envelope = jnp.exp(-damping[:, None] * radial[None, :])
    return -(AMPLITUDE * jnp.sin(aberration) + CONTRAST * jnp.cos(aberration)) * envelope

def shifted(picture, shift_pair):
    image_side = picture.shape[0]
    doubled = jnp.concatenate([picture, picture], axis=0)
    rows_moved = lax.dynamic_slice_in_dim(doubled, shift_pair[0], image_side, 0)
    doubled = jnp.concatenate([rows_moved, rows_moved], axis=1)
    return lax.dynamic_slice_in_dim(doubled, shift_pair[1], image_side, 1)

def compare(ref_rows, ctf_table, spectra, image_side):
    predicted = ctf_table * ref_rows.astype(jnp.float32)
    values = spectra.astype(jnp.float32)
    cross_term = lax.optimization_barrier(jnp.mean(predicted * values, axis=1))
    model_power = lax.optimization_barrier(jnp.mean(predicted * predicted, axis=1)) + EPSILON
    data_power = lax.optimization_barrier(jnp.mean(values * values, axis=1)) + EPSILON
    correlation = cross_term / jnp.sqrt(model_power * data_power)
    weights = jax.nn.sigmoid(image_side * correlation).astype(jnp.bfloat16)
    weighted = (weights.astype(jnp.float32)[:, None] * ctf_table * values).astype(jnp.bfloat16)
    return (correlation, weights, weighted)

def reference(images, offsets, ctf_group, particle_bin, bin_place, defocus, bfactor, references):
    blocks = PARTICLES // PARTICLE_DEV
    pixel_count = IMAGE_SIDE * IMAGE_SIDE
    basis = lax.optimization_barrier(hartley(IMAGE_SIDE)).astype(jnp.float32)

    def spectra_block(inputs):
        pictures, shift_pairs = inputs
        moved = jax.vmap(shifted)(pictures, shift_pairs).astype(jnp.float32)
        partial_rows = jnp.einsum('kx,pxy->pky', basis, moved).astype(jnp.bfloat16)
        partial_rows = lax.optimization_barrier(partial_rows).astype(jnp.float32)
        return jnp.einsum('pky,ly->pkl', partial_rows, basis).astype(jnp.bfloat16)
    spectra = lax.map(spectra_block, (images.reshape(blocks, PARTICLE_DEV, IMAGE_SIDE, IMAGE_SIDE), offsets.T.reshape(blocks, PARTICLE_DEV, 2)))
    spectra = spectra.reshape(blocks, PARTICLE_DEV, pixel_count)
    places = bin_place[particle_bin].astype(jnp.int32).reshape(blocks, PARTICLE_DEV)
    focus = defocus[ctf_group].reshape(blocks, PARTICLE_DEV)
    damping = bfactor[ctf_group].reshape(blocks, PARTICLE_DEV)
    current = references.reshape(BINS, pixel_count)
    scores = jnp.zeros((PARTICLES,), jnp.float32)
    for iteration in range(ITERS):
        frozen = current

        def one_block(carry, inputs):
            numerator, denominator = carry
            block_spectra, block_places, block_focus, block_damping = inputs
            ctf_table = ctf_rows(block_focus, block_damping, IMAGE_SIDE)
            ref_rows = frozen[block_places]
            correlation, weights, weighted = compare(ref_rows, ctf_table, block_spectra, IMAGE_SIDE)
            numerator = numerator.at[block_places].add(weighted.astype(jnp.float32))
            denominator = denominator.at[block_places].add(weights.astype(jnp.float32)[:, None] * ctf_table * ctf_table)
            return ((numerator, denominator), correlation)
        start = (jnp.zeros((BINS, pixel_count), jnp.float32), jnp.zeros((BINS, pixel_count), jnp.float32))
        (numerator, denominator), correlation = lax.scan(one_block, start, (spectra, places, focus, damping))
        current = ((numerator + PRIOR_WEIGHT * frozen.astype(jnp.float32)) / (denominator + PRIOR_WEIGHT)).astype(jnp.bfloat16)
        scores = correlation.reshape(PARTICLES)
    return (current.reshape(BINS, IMAGE_SIDE, IMAGE_SIDE), scores)
```

```python
import functools
import math

import jax
import jax.numpy as jnp
import numpy as np
from jax import lax
from jax.experimental import pallas as pl
from jax.experimental.pallas import tpu as pltpu
from jax.sharding import PartitionSpec as P

ITERS = 2
PRIOR_WEIGHT = 0.5
EPSILON = 1e-06
CONTRAST = 0.1
AMPLITUDE = math.sqrt(1.0 - CONTRAST * CONTRAST)

LABEL_ROWS = 16
CHUNK = 32
VMEM_BYTES = 48 * 1024 * 1024

F32 = jnp.float32
BF16 = jnp.bfloat16
VMEM = pl.BlockSpec(memory_space=pltpu.VMEM)
SMEM = pl.BlockSpec(memory_space=pltpu.SMEM)


def hartley(side):
    index = np.arange(side)
    angles = (np.outer(index, index) % side).astype(np.float32) * np.float32(2.0 * math.pi / side)
    return (np.cos(angles) + np.sin(angles)) / np.float32(math.sqrt(side))


def label_block(values, side):
    row = lax.broadcasted_iota(jnp.int32, (LABEL_ROWS, side), 0)
    block = jnp.zeros((LABEL_ROWS, side), jnp.int32)
    for number, value in enumerate(values):
        block = jnp.where(row == number, value, block)
    return block.astype(F32).astype(BF16)


def read_rows(block, weights):
    labels = block.astype(F32)
    total = sum(labels[r : r + 1, :128] * float(w) for r, w in enumerate(weights) if w)
    return jnp.max(total).astype(jnp.int32)


def home_kernel(
    bin_count, own_bins, place_ref, bin_ref, group_ref, offset_ref, image_ref, basis_ref, *rest
):
    outs, (spectra,) = rest[:bin_count], rest[bin_count:]
    particles, side = image_ref.shape[0], image_ref.shape[1]
    here = lax.axis_index("bin")
    empty = jnp.zeros((LABEL_ROWS, side), BF16)
    for out in outs:
        out[side : side + LABEL_ROWS, :] = empty

    @pl.loop(0, particles)
    def _(i):
        moved = pltpu.roll(image_ref[i].astype(F32), side - offset_ref[0, i], 0).astype(BF16)
        columns = pltpu.roll(basis_ref[...].astype(F32), offset_ref[1, i], 0).astype(BF16)
        half = jnp.dot(basis_ref[...], moved, preferred_element_type=F32).astype(BF16)
        spectra[...] = jnp.dot(half, columns, preferred_element_type=F32).astype(BF16)
        place = place_ref[bin_ref[i]]
        owner = place // own_bins
        target = lax.rem(owner, bin_count)
        labels = label_block(
            (1 + owner // bin_count, lax.rem(place, own_bins), group_ref[i], i * bin_count + here),
            side,
        )
        for step in range(bin_count):

            @pl.when((target ^ here) == step)
            def _():
                outs[step][0:side, :] = spectra[...]
                outs[step][side : side + LABEL_ROWS, :] = labels


def middle_kernel(mic_count, capacity, *rest):
    arrived, outs = rest[: len(rest) - mic_count], rest[len(rest) - mic_count :]
    rows, side = arrived[0].shape
    here = lax.axis_index("mic")
    empty = jnp.zeros((LABEL_ROWS, side), BF16)
    for out in outs:
        for j in range(capacity):
            out[j, rows - LABEL_ROWS : rows, :] = empty
    targets = [read_rows(block[rows - LABEL_ROWS : rows, :], (1,)) for block in arrived]
    counts = [jnp.int32(0)] * mic_count
    for block, target in zip(arrived, targets):
        step_of = (target - 1) ^ here
        for step in range(mic_count):
            chosen = (target > 0) & (step_of == step)

            @pl.when(chosen)
            def _(block=block, step=step, slot=counts[step]):
                outs[step][slot] = block[...]

            counts[step] = counts[step] + chosen.astype(jnp.int32)


def owner_kernel(
    bin_count, mic_count, capacity, focus_ref, damping_ref, current_ref, *rest
):
    arrived, (refined_ref, score_ref) = rest[:mic_count], rest[mic_count : mic_count + 2]
    spectra, ctf, middle, sums, weight, number, active, place, home, particle = rest[mic_count + 2 :]
    own_bins, side, _ = current_ref.shape
    slots = mic_count * capacity
    steps = side // CHUNK
    here = lax.axis_index("mic")
    pixels = float(side * side)

    row = lax.broadcasted_iota(jnp.int32, (slots, side), 0)
    focus = jnp.zeros((slots, side), F32)
    damping = jnp.zeros((slots, side), F32)
    for step in range(mic_count):
        for j in range(capacity):
            s = step * capacity + j
            block = arrived[step][j, side : side + LABEL_ROWS, :]
            code = read_rows(block, (0, 1, 256, 65536))
            valid = read_rows(block, (1,)) > 0
            code = jnp.where(valid, code, 0)
            group = (code // 256) % 256
            sender = code // 65536
            active[s] = valid.astype(jnp.int32)
            place[s] = code % 256
            home[s] = (here ^ step) * bin_count + sender % bin_count
            particle[s] = sender // bin_count
            focus = jnp.where(row == s, focus_ref[group], focus)
            damping = jnp.where(row == s, damping_ref[group], damping)

    frequency = lax.broadcasted_iota(jnp.int32, (slots, side), 1)
    folded = jnp.minimum(frequency, side - frequency).astype(F32) / (side / 2.0)
    square = folded * folded
    envelope = jnp.exp(-damping * square)
    sine = jnp.sin(focus * square) * envelope
    cosine = jnp.cos(focus * square) * envelope
    by_sine = jnp.transpose(CONTRAST * sine - AMPLITUDE * cosine)
    by_cosine = jnp.transpose(-(AMPLITUDE * sine + CONTRAST * cosine))
    sums[...] = jnp.zeros(sums.shape, F32)

    def rows_of(c):
        return pl.ds(pl.multiple_of(c * CHUNK, CHUNK), CHUNK)

    def fold(values):
        return jnp.sum(values.reshape(CHUNK // 8, 8, side), axis=0)

    for s in range(slots):

        @pl.when(active[s] > 0)
        def _(s=s):
            for c in range(steps):
                rows = slice(c * CHUNK, (c + 1) * CHUNK)
                ctf[s, rows, :] = (
                    by_sine[rows, s : s + 1] * sine[s : s + 1, :]
                    + by_cosine[rows, s : s + 1] * cosine[s : s + 1, :]
                )
                spectra[s, rows, :] = arrived[s // capacity][s % capacity, rows, :]

    def compare(source):
        @pl.loop(0, slots)
        def _(s):
            @pl.when(active[s] > 0)
            def _():
                def add(c, totals):
                    cross, model, data = totals
                    rows = rows_of(c)
                    values = spectra[s, rows, :].astype(F32)
                    predicted = ctf[s, rows, :] * source[place[s], rows, :].astype(F32)
                    return (
                        cross + fold(predicted * values),
                        model + fold(predicted * predicted),
                        data + fold(values * values),
                    )

                zero = jnp.zeros((8, side), F32)
                totals = lax.fori_loop(0, steps, add, (zero, zero, zero))
                for k in range(3):
                    sums[k, pl.ds(s, 1), :] = jnp.sum(totals[k], axis=0, keepdims=True)

        cross, model, data = (
            jnp.sum(sums[k], axis=1, keepdims=True) / pixels for k in range(3)
        )
        correlation = cross / jnp.sqrt((model + EPSILON) * (data + EPSILON))
        weights = 1.0 / (1.0 + jnp.exp(-float(side) * correlation))
        weight[...] = jnp.broadcast_to(weights.astype(BF16).astype(F32), (slots, side))
        return correlation

    def update(source, target):
        @pl.loop(0, own_bins)
        def _(p):
            members = jnp.int32(0)
            member = jnp.int32(0)
            for s in range(slots):
                match = (active[s] > 0) & (place[s] == p)
                members = members + match.astype(jnp.int32)
                member = jnp.where(match, s, member)

            def shares(s, rows):
                table = ctf[s, rows, :]
                scaled = weight[pl.ds(s, 1), :] * table
                term = (scaled * spectra[s, rows, :].astype(F32)).astype(BF16).astype(F32)
                return term, scaled * table

            def finish(rows, numerator, denominator):
                previous = source[p, rows, :].astype(F32)
                target[p, rows, :] = (
                    (numerator + PRIOR_WEIGHT * previous) / (denominator + PRIOR_WEIGHT)
                ).astype(BF16)

            @pl.when(members == 0)
            def _():
                target[p] = source[p]

            @pl.when(members == 1)
            def _():
                @pl.loop(0, steps)
                def _(c):
                    rows = rows_of(c)
                    finish(rows, *shares(member, rows))

            @pl.when(members > 1)
            def _():
                @pl.loop(0, steps)
                def _(c):
                    rows = rows_of(c)
                    number[0, rows, :] = jnp.zeros((CHUNK, side), F32)
                    number[1, rows, :] = jnp.zeros((CHUNK, side), F32)

                @pl.loop(0, slots)
                def _(s):
                    @pl.when((active[s] > 0) & (place[s] == p))
                    def _():
                        @pl.loop(0, steps)
                        def _(c):
                            rows = rows_of(c)
                            term, power = shares(s, rows)
                            number[0, rows, :] += term
                            number[1, rows, :] += power

                @pl.loop(0, steps)
                def _(c):
                    rows = rows_of(c)
                    finish(rows, number[0, rows, :], number[1, rows, :])

    source = current_ref
    for iteration in range(ITERS):
        correlation = compare(source)
        target = refined_ref if iteration == ITERS - 1 else middle
        update(source, target)
        source = target

    devices = score_ref.shape[0]
    device = lax.broadcasted_iota(jnp.int32, (devices, 1, 128), 0)
    lane = lax.broadcasted_iota(jnp.int32, (devices, 1, 128), 2)
    board = jnp.zeros((devices, 1, 128), F32)
    for s in range(slots):
        hit = (active[s] > 0) & (device == home[s]) & (lane == particle[s])
        board = jnp.where(hit, correlation[s : s + 1, :].reshape(1, 1, 1), board)
    score_ref[...] = board


def exchange(blocks, axis):
    size = lax.axis_size(axis)
    return [blocks[0]] + [
        lax.ppermute(blocks[k], axis, [(i, i ^ k) for i in range(size)]) for k in range(1, size)
    ]


def body(images, offsets, ctf_group, particle_bin, bin_place, defocus, bfactor, references):
    mic_count = lax.axis_size("mic")
    bin_count = lax.axis_size("bin")
    particles, side, _ = images.shape
    own_bins = references.shape[0]
    capacity = (3 * particles + 2 * mic_count - 1) // (2 * mic_count)
    slots = mic_count * capacity
    rows = side + LABEL_ROWS
    params = pltpu.CompilerParams(vmem_limit_bytes=VMEM_BYTES)

    sent = pl.pallas_call(
        functools.partial(home_kernel, bin_count, own_bins),
        out_shape=[jax.ShapeDtypeStruct((rows, side), BF16)] * bin_count,
        in_specs=[SMEM] * 4 + [VMEM] * 2,
        out_specs=[VMEM] * bin_count,
        scratch_shapes=[pltpu.VMEM((side, side), BF16)],
        compiler_params=params,
        name="home",
    )(bin_place, particle_bin, ctf_group, offsets, images, jnp.asarray(hartley(side), BF16))
    arrived = exchange(sent, "bin")

    sent = pl.pallas_call(
        functools.partial(middle_kernel, mic_count, capacity),
        out_shape=[jax.ShapeDtypeStruct((capacity, rows, side), BF16)] * mic_count,
        in_specs=[VMEM] * bin_count,
        out_specs=[VMEM] * mic_count,
        compiler_params=params,
        name="middle",
    )(*arrived)
    arrived = exchange(sent, "mic")

    refined, board = pl.pallas_call(
        functools.partial(owner_kernel, bin_count, mic_count, capacity),
        out_shape=[
            jax.ShapeDtypeStruct(references.shape, BF16),
            jax.ShapeDtypeStruct((mic_count * bin_count, 1, 128), F32),
        ],
        in_specs=[SMEM] * 2 + [VMEM] * (1 + mic_count),
        out_specs=[VMEM] * 2,
        scratch_shapes=[
            pltpu.VMEM((slots, side, side), BF16),
            pltpu.VMEM((slots, side, side), F32),
            pltpu.VMEM((own_bins, side, side), BF16),
            pltpu.VMEM((3, slots, side), F32),
            pltpu.VMEM((slots, side), F32),
            pltpu.VMEM((2, side, side), F32),
        ]
        + [pltpu.SMEM((slots,), jnp.int32)] * 4,
        compiler_params=params,
        name="owner",
    )(defocus, bfactor, references, *arrived)
    back = lax.all_to_all(board, ("mic", "bin"), split_axis=0, concat_axis=0, tiled=True)
    return (refined, jnp.sum(back, axis=(0, 1))[:particles])


def solution(mesh):
    in_specs = (
        P(("mic", "bin"), None, None),
        P(None, ("mic", "bin")),
        P(("mic", "bin")),
        P(("mic", "bin")),
        P(),
        P(),
        P(),
        P(("mic", "bin"), None, None),
    )
    out_specs = (P(("mic", "bin"), None, None), P(("mic", "bin")))
    return jax.shard_map(body, mesh=mesh, in_specs=in_specs, out_specs=out_specs, check_vma=False)
```

```python
import functools
import math

import jax
import jax.numpy as jnp
import numpy as np
from jax import lax
from jax.experimental import pallas as pl
from jax.experimental.pallas import tpu as pltpu
from jax.sharding import PartitionSpec as P

ITERS = 2
PRIOR_WEIGHT = 0.5
EPSILON = 1e-06
CONTRAST = 0.1
AMPLITUDE = math.sqrt(1.0 - CONTRAST * CONTRAST)

LABEL_ROWS = 16
CHUNK = 32
VMEM_BYTES = 48 * 1024 * 1024

F32 = jnp.float32
BF16 = jnp.bfloat16
VMEM = pl.BlockSpec(memory_space=pltpu.VMEM)
SMEM = pl.BlockSpec(memory_space=pltpu.SMEM)
HBM = pl.BlockSpec(memory_space=pltpu.HBM)


def in_hbm(x):
    return pltpu.with_memory_space_constraint(x, pltpu.HBM)


def hartley(side):
    index = np.arange(side)
    angles = (np.outer(index, index) % side).astype(np.float32) * np.float32(2.0 * math.pi / side)
    return (np.cos(angles) + np.sin(angles)) / np.float32(math.sqrt(side))


def label_block(values, side):
    row = lax.broadcasted_iota(jnp.int32, (LABEL_ROWS, side), 0)
    block = jnp.zeros((LABEL_ROWS, side), jnp.int32)
    for number, value in enumerate(values):
        block = jnp.where(row == number, value, block)
    return block.astype(F32).astype(BF16)


def read_rows(block, weights):
    labels = block.astype(F32)
    total = sum(labels[r : r + 1, :128] * float(w) for r, w in enumerate(weights) if w)
    return jnp.max(total).astype(jnp.int32)


def home_kernel(
    bin_count, own_bins, place_hbm, bin_hbm, group_hbm, offset_hbm, image_hbm, basis_hbm, *rest
):
    outs, rest = rest[:bin_count], rest[bin_count:]
    spectra, image_ref, basis_ref, place_ref, bin_ref, group_ref, offset_ref, image_sem, sem = rest
    particles, side = image_ref.shape[0], image_ref.shape[1]
    here = lax.axis_index("bin")
    pairs = (
        (basis_hbm, basis_ref),
        (place_hbm, place_ref),
        (bin_hbm, bin_ref),
        (group_hbm, group_ref),
        (offset_hbm, offset_ref),
    )
    copies = [pltpu.make_async_copy(a, b, sem.at[k]) for k, (a, b) in enumerate(pairs)]
    for copy in copies:
        copy.start()

    def image_copy(i):
        return pltpu.make_async_copy(image_hbm.at[i], image_ref.at[i], image_sem.at[i])

    for i in range(particles):
        image_copy(i).start()
    empty = jnp.zeros((LABEL_ROWS, side), BF16)
    for out in outs:
        out[side : side + LABEL_ROWS, :] = empty
    for copy in copies:
        copy.wait()

    @pl.loop(0, particles)
    def _(i):
        image_copy(i).wait()
        moved = pltpu.roll(image_ref[i].astype(F32), side - offset_ref[0, i], 0).astype(BF16)
        columns = pltpu.roll(basis_ref[...].astype(F32), offset_ref[1, i], 0).astype(BF16)
        half = jnp.dot(basis_ref[...], moved, preferred_element_type=F32).astype(BF16)
        spectra[...] = jnp.dot(half, columns, preferred_element_type=F32).astype(BF16)
        place = place_ref[bin_ref[i]]
        owner = place // own_bins
        target = lax.rem(owner, bin_count)
        labels = label_block(
            (1 + owner // bin_count, lax.rem(place, own_bins), group_ref[i], i * bin_count + here),
            side,
        )
        for step in range(bin_count):

            @pl.when((target ^ here) == step)
            def _():
                outs[step][0:side, :] = spectra[...]
                outs[step][side : side + LABEL_ROWS, :] = labels


def middle_kernel(mic_count, capacity, *rest):
    arrived, outs = rest[: len(rest) - mic_count], rest[len(rest) - mic_count :][::-1]
    rows, side = arrived[0].shape
    here = lax.axis_index("mic")
    empty = jnp.zeros((LABEL_ROWS, side), BF16)
    for out in outs:
        for j in range(capacity):
            out[j, rows - LABEL_ROWS : rows, :] = empty
    targets = [read_rows(block[rows - LABEL_ROWS : rows, :], (1,)) for block in arrived]
    counts = [jnp.int32(0)] * mic_count
    for block, target in zip(arrived, targets):
        step_of = (target - 1) ^ here
        for step in range(mic_count):
            chosen = (target > 0) & (step_of == step)

            @pl.when(chosen)
            def _(block=block, step=step, slot=counts[step]):
                outs[step][slot] = block[...]

            counts[step] = counts[step] + chosen.astype(jnp.int32)


def owner_kernel(
    bin_count, mic_count, capacity, focus_ref, damping_ref, current_ref, *rest
):
    arrived, (refined_ref, score_ref) = rest[:mic_count][::-1], rest[mic_count : mic_count + 2]
    spectra, ctf, middle, sums, weight, number, active, place, home, particle = rest[mic_count + 2 :]
    own_bins, side, _ = current_ref.shape
    slots = mic_count * capacity
    steps = side // CHUNK
    here = lax.axis_index("mic")
    pixels = float(side * side)

    row = lax.broadcasted_iota(jnp.int32, (slots, side), 0)
    focus = jnp.zeros((slots, side), F32)
    damping = jnp.zeros((slots, side), F32)
    for step in range(mic_count):
        for j in range(capacity):
            s = step * capacity + j
            block = arrived[step][j, side : side + LABEL_ROWS, :]
            code = read_rows(block, (0, 1, 256, 65536))
            valid = read_rows(block, (1,)) > 0
            code = jnp.where(valid, code, 0)
            group = (code // 256) % 256
            sender = code // 65536
            active[s] = valid.astype(jnp.int32)
            place[s] = code % 256
            home[s] = (here ^ step) * bin_count + sender % bin_count
            particle[s] = sender // bin_count
            focus = jnp.where(row == s, focus_ref[group], focus)
            damping = jnp.where(row == s, damping_ref[group], damping)

    frequency = lax.broadcasted_iota(jnp.int32, (slots, side), 1)
    folded = jnp.minimum(frequency, side - frequency).astype(F32) / (side / 2.0)
    square = folded * folded
    envelope = jnp.exp(-damping * square)
    sine = jnp.sin(focus * square) * envelope
    cosine = jnp.cos(focus * square) * envelope
    by_sine = jnp.transpose(CONTRAST * sine - AMPLITUDE * cosine)
    by_cosine = jnp.transpose(-(AMPLITUDE * sine + CONTRAST * cosine))
    sums[...] = jnp.zeros(sums.shape, F32)

    def rows_of(c):
        return pl.ds(pl.multiple_of(c * CHUNK, CHUNK), CHUNK)

    def fold(values):
        return jnp.sum(values.reshape(CHUNK // 8, 8, side), axis=0)

    for s in range(slots):

        @pl.when(active[s] > 0)
        def _(s=s):
            for c in range(steps):
                rows = slice(c * CHUNK, (c + 1) * CHUNK)
                ctf[s, rows, :] = (
                    by_sine[rows, s : s + 1] * sine[s : s + 1, :]
                    + by_cosine[rows, s : s + 1] * cosine[s : s + 1, :]
                )
                spectra[s, rows, :] = arrived[s // capacity][s % capacity, rows, :]

    def compare(source):
        @pl.loop(0, slots)
        def _(s):
            @pl.when(active[s] > 0)
            def _():
                def add(c, totals):
                    cross, model, data = totals
                    rows = rows_of(c)
                    values = spectra[s, rows, :].astype(F32)
                    predicted = ctf[s, rows, :] * source[place[s], rows, :].astype(F32)
                    return (
                        cross + fold(predicted * values),
                        model + fold(predicted * predicted),
                        data + fold(values * values),
                    )

                zero = jnp.zeros((8, side), F32)
                totals = lax.fori_loop(0, steps, add, (zero, zero, zero))
                for k in range(3):
                    sums[k, pl.ds(s, 1), :] = jnp.sum(totals[k], axis=0, keepdims=True)

        cross, model, data = (
            jnp.sum(sums[k], axis=1, keepdims=True) / pixels for k in range(3)
        )
        correlation = cross / jnp.sqrt((model + EPSILON) * (data + EPSILON))
        weights = 1.0 / (1.0 + jnp.exp(-float(side) * correlation))
        weight[...] = jnp.broadcast_to(weights.astype(BF16).astype(F32), (slots, side))
        return correlation

    def update(source, target):
        @pl.loop(0, own_bins)
        def _(p):
            members = jnp.int32(0)
            member = jnp.int32(0)
            for s in range(slots):
                match = (active[s] > 0) & (place[s] == p)
                members = members + match.astype(jnp.int32)
                member = jnp.where(match, s, member)

            def shares(s, rows):
                table = ctf[s, rows, :]
                scaled = weight[pl.ds(s, 1), :] * table
                term = (scaled * spectra[s, rows, :].astype(F32)).astype(BF16).astype(F32)
                return term, scaled * table

            def finish(rows, numerator, denominator):
                previous = source[p, rows, :].astype(F32)
                target[p, rows, :] = (
                    (numerator + PRIOR_WEIGHT * previous) / (denominator + PRIOR_WEIGHT)
                ).astype(BF16)

            @pl.when(members == 0)
            def _():
                target[p] = source[p]

            @pl.when(members == 1)
            def _():
                @pl.loop(0, steps)
                def _(c):
                    rows = rows_of(c)
                    finish(rows, *shares(member, rows))

            @pl.when(members > 1)
            def _():
                @pl.loop(0, steps)
                def _(c):
                    rows = rows_of(c)
                    number[0, rows, :] = jnp.zeros((CHUNK, side), F32)
                    number[1, rows, :] = jnp.zeros((CHUNK, side), F32)

                @pl.loop(0, slots)
                def _(s):
                    @pl.when((active[s] > 0) & (place[s] == p))
                    def _():
                        @pl.loop(0, steps)
                        def _(c):
                            rows = rows_of(c)
                            term, power = shares(s, rows)
                            number[0, rows, :] += term
                            number[1, rows, :] += power

                @pl.loop(0, steps)
                def _(c):
                    rows = rows_of(c)
                    finish(rows, number[0, rows, :], number[1, rows, :])

    source = current_ref
    for iteration in range(ITERS):
        correlation = compare(source)
        target = refined_ref if iteration == ITERS - 1 else middle
        update(source, target)
        source = target

    devices = score_ref.shape[0]
    device = lax.broadcasted_iota(jnp.int32, (devices, 1, 128), 0)
    lane = lax.broadcasted_iota(jnp.int32, (devices, 1, 128), 2)
    board = jnp.zeros((devices, 1, 128), F32)
    for s in range(slots):
        hit = (active[s] > 0) & (device == home[s]) & (lane == particle[s])
        board = jnp.where(hit, correlation[s : s + 1, :].reshape(1, 1, 1), board)
    score_ref[...] = board


def exchange(blocks, axis):
    size = lax.axis_size(axis)
    return [blocks[0]] + [
        lax.ppermute(blocks[k], axis, [(i, i ^ k) for i in range(size)]) for k in range(1, size)
    ]


def body(images, offsets, ctf_group, particle_bin, bin_place, defocus, bfactor, references):
    mic_count = lax.axis_size("mic")
    bin_count = lax.axis_size("bin")
    particles, side, _ = images.shape
    own_bins = references.shape[0]
    capacity = (3 * particles + 2 * mic_count - 1) // (2 * mic_count)
    slots = mic_count * capacity
    rows = side + LABEL_ROWS
    params = pltpu.CompilerParams(vmem_limit_bytes=VMEM_BYTES)

    sent = pl.pallas_call(
        functools.partial(home_kernel, bin_count, own_bins),
        out_shape=[jax.ShapeDtypeStruct((rows, side), BF16)] * bin_count,
        in_specs=[HBM] * 6,
        out_specs=[VMEM] * bin_count,
        scratch_shapes=[
            pltpu.VMEM((side, side), BF16),
            pltpu.VMEM(images.shape, BF16),
            pltpu.VMEM((side, side), BF16),
            pltpu.SMEM(bin_place.shape, jnp.int32),
            pltpu.SMEM(particle_bin.shape, jnp.int32),
            pltpu.SMEM(ctf_group.shape, jnp.int32),
            pltpu.SMEM(offsets.shape, jnp.int32),
            pltpu.SemaphoreType.DMA((particles,)),
            pltpu.SemaphoreType.DMA((5,)),
        ],
        compiler_params=params,
        name="home",
    )(*map(in_hbm, (bin_place, particle_bin, ctf_group, offsets, images, jnp.asarray(hartley(side), BF16))))
    arrived = exchange(sent, "bin")

    sent = pl.pallas_call(
        functools.partial(middle_kernel, mic_count, capacity),
        out_shape=[jax.ShapeDtypeStruct((capacity, rows, side), BF16)] * mic_count,
        in_specs=[VMEM] * bin_count,
        out_specs=[VMEM] * mic_count,
        compiler_params=params,
        name="middle",
    )(*arrived[::-1])
    arrived = exchange(sent[::-1], "mic")

    refined, board = pl.pallas_call(
        functools.partial(owner_kernel, bin_count, mic_count, capacity),
        out_shape=[
            jax.ShapeDtypeStruct(references.shape, BF16),
            jax.ShapeDtypeStruct((mic_count * bin_count, 1, 128), F32),
        ],
        in_specs=[SMEM] * 2 + [VMEM] * (1 + mic_count),
        out_specs=[VMEM] * 2,
        scratch_shapes=[
            pltpu.VMEM((slots, side, side), BF16),
            pltpu.VMEM((slots, side, side), F32),
            pltpu.VMEM((own_bins, side, side), BF16),
            pltpu.VMEM((3, slots, side), F32),
            pltpu.VMEM((slots, side), F32),
            pltpu.VMEM((2, side, side), F32),
        ]
        + [pltpu.SMEM((slots,), jnp.int32)] * 4,
        compiler_params=params,
        name="owner",
    )(defocus, bfactor, references, *arrived[::-1])
    back = lax.all_to_all(board, ("mic", "bin"), split_axis=0, concat_axis=0, tiled=True)
    return (refined, jnp.sum(back, axis=(0, 1))[:particles])


def solution(mesh):
    in_specs = (
        P(("mic", "bin"), None, None),
        P(None, ("mic", "bin")),
        P(("mic", "bin")),
        P(("mic", "bin")),
        P(),
        P(),
        P(),
        P(("mic", "bin"), None, None),
    )
    out_specs = (P(("mic", "bin"), None, None), P(("mic", "bin")))
    return jax.shard_map(body, mesh=mesh, in_specs=in_specs, out_specs=out_specs, check_vma=False)
```

```python
import functools
import math

import jax
import jax.numpy as jnp
import numpy as np
from jax import lax
from jax.experimental import pallas as pl
from jax.experimental.pallas import tpu as pltpu
from jax.sharding import PartitionSpec as P

ITERS = 2
PRIOR_WEIGHT = 0.5
EPSILON = 1e-06
CONTRAST = 0.1
AMPLITUDE = math.sqrt(1.0 - CONTRAST * CONTRAST)

LABEL_ROWS = 16
CHUNK = 32
VMEM_BYTES = 48 * 1024 * 1024

F32 = jnp.float32
BF16 = jnp.bfloat16
VMEM = pl.BlockSpec(memory_space=pltpu.VMEM)
SMEM = pl.BlockSpec(memory_space=pltpu.SMEM)
HBM = pl.BlockSpec(memory_space=pltpu.HBM)


def in_hbm(x):
    return pltpu.with_memory_space_constraint(x, pltpu.HBM)


def hartley(side):
    index = np.arange(side)
    angles = (np.outer(index, index) % side).astype(np.float32) * np.float32(2.0 * math.pi / side)
    return (np.cos(angles) + np.sin(angles)) / np.float32(math.sqrt(side))


def label_block(values, side):
    row = lax.broadcasted_iota(jnp.int32, (LABEL_ROWS, side), 0)
    block = jnp.zeros((LABEL_ROWS, side), jnp.int32)
    for number, value in enumerate(values):
        block = jnp.where(row == number, value, block)
    return block.astype(F32).astype(BF16)


def read_target(block):
    return jnp.max(block[0:1, :128].astype(F32)).astype(jnp.int32)


def read_labels(block):
    labels = block[:, :128].astype(F32)
    code = labels[1:2] + 256.0 * labels[2:3] + 65536.0 * labels[3:4]
    return jnp.max(jnp.where(labels[0:1] > 0, code, -1.0)).astype(jnp.int32)


def home_kernel(
    bin_count, own_bins, place_hbm, bin_hbm, group_hbm, offset_hbm, image_hbm, basis_hbm, *rest
):
    outs, rest = rest[:bin_count], rest[bin_count:]
    spectra, image_ref, basis_ref, place_ref, bin_ref, group_ref, offset_ref, image_sem, sem = rest
    particles, side = image_ref.shape[0], image_ref.shape[1]
    here = lax.axis_index("bin")
    pairs = (
        (basis_hbm, basis_ref),
        (place_hbm, place_ref),
        (bin_hbm, bin_ref),
        (group_hbm, group_ref),
        (offset_hbm, offset_ref),
    )
    copies = [pltpu.make_async_copy(a, b, sem.at[k]) for k, (a, b) in enumerate(pairs)]
    for copy in copies:
        copy.start()

    def image_copy(i):
        return pltpu.make_async_copy(image_hbm.at[i], image_ref.at[i], image_sem.at[i])

    for i in range(particles):
        image_copy(i).start()
    empty = jnp.zeros((LABEL_ROWS, side), BF16)
    for out in outs:
        out[side : side + LABEL_ROWS, :] = empty
    for copy in copies:
        copy.wait()

    @pl.loop(0, particles)
    def _(i):
        image_copy(i).wait()
        moved = pltpu.roll(image_ref[i].astype(F32), side - offset_ref[0, i], 0).astype(BF16)
        columns = pltpu.roll(basis_ref[...].astype(F32), offset_ref[1, i], 0).astype(BF16)
        half = jnp.dot(basis_ref[...], moved, preferred_element_type=F32).astype(BF16)
        spectra[...] = jnp.dot(half, columns, preferred_element_type=F32).astype(BF16)
        place = place_ref[bin_ref[i]]
        owner = place // own_bins
        target = lax.rem(owner, bin_count)
        labels = label_block(
            (1 + owner // bin_count, lax.rem(place, own_bins), group_ref[i], i * bin_count + here),
            side,
        )
        for step in range(bin_count):

            @pl.when((target ^ here) == step)
            def _():
                outs[step][0:side, :] = spectra[...]
                outs[step][side : side + LABEL_ROWS, :] = labels


def home_call(bin_count, own_bins, bin_place, particle_bin, ctf_group, offsets, images):
    particles, side, _ = images.shape
    rows = side + LABEL_ROWS
    return pl.pallas_call(
        functools.partial(home_kernel, bin_count, own_bins),
        out_shape=[jax.ShapeDtypeStruct((rows, side), BF16)] * bin_count,
        in_specs=[HBM] * 6,
        out_specs=[VMEM] * bin_count,
        scratch_shapes=[
            pltpu.VMEM((side, side), BF16),
            pltpu.VMEM(images.shape, BF16),
            pltpu.VMEM((side, side), BF16),
            pltpu.SMEM(bin_place.shape, jnp.int32),
            pltpu.SMEM(particle_bin.shape, jnp.int32),
            pltpu.SMEM(ctf_group.shape, jnp.int32),
            pltpu.SMEM(offsets.shape, jnp.int32),
            pltpu.SemaphoreType.DMA((particles,)),
            pltpu.SemaphoreType.DMA((5,)),
        ],
        compiler_params=pltpu.CompilerParams(vmem_limit_bytes=VMEM_BYTES),
        name="home",
    )(*map(in_hbm, (bin_place, particle_bin, ctf_group, offsets, images, jnp.asarray(hartley(side), BF16))))


def middle_kernel(mic_count, capacity, *rest):
    arrived, outs = rest[: len(rest) - mic_count], rest[len(rest) - mic_count :][::-1]
    rows, side = arrived[0].shape
    here = lax.axis_index("mic")
    empty = jnp.zeros((LABEL_ROWS, side), BF16)
    for out in outs:
        for j in range(capacity):
            out[j, rows - LABEL_ROWS : rows, :] = empty
    targets = [read_target(block[rows - LABEL_ROWS : rows, :]) for block in arrived]
    counts = [jnp.int32(0)] * mic_count
    for block, target in zip(arrived, targets):
        step_of = (target - 1) ^ here
        for step in range(mic_count):
            chosen = (target > 0) & (step_of == step)

            @pl.when(chosen)
            def _(block=block, step=step, slot=counts[step]):
                outs[step][slot] = block[...]

            counts[step] = counts[step] + chosen.astype(jnp.int32)


def owner_kernel(
    bin_count, mic_count, capacity, focus_ref, damping_ref, current_ref, *rest
):
    arrived, (refined_ref, score_ref) = rest[:mic_count][::-1], rest[mic_count : mic_count + 2]
    spectra, ctf, middle, sums, weight, number, active, place, alone, home, particle = rest[
        mic_count + 2 :
    ]
    own_bins, side, _ = current_ref.shape
    slots = mic_count * capacity
    here = lax.axis_index("mic")
    pixels = float(side * side)
    chunks = [slice(c, c + CHUNK) for c in range(0, side, CHUNK)]
    zero = jnp.zeros((8, side), F32)

    row = lax.broadcasted_iota(jnp.int32, (slots, side), 0)
    focus = jnp.zeros((slots, side), F32)
    damping = jnp.zeros((slots, side), F32)
    for s in range(slots):
        step = s // capacity
        code = read_labels(arrived[step][s % capacity, side : side + LABEL_ROWS, :])
        active[s] = (code >= 0).astype(jnp.int32)
        code = jnp.maximum(code, 0)
        group = (code >> 8) & 255
        sender = code >> 16
        place[s] = code & 255
        home[s] = (here ^ step) * bin_count + lax.rem(sender, bin_count)
        particle[s] = sender // bin_count
        focus = jnp.where(row == s, focus_ref[group], focus)
        damping = jnp.where(row == s, damping_ref[group], damping)
    members = [jnp.int32(0)] * own_bins
    for s in range(slots):
        same = jnp.int32(0)
        for t in range(slots):
            same = same + ((active[t] > 0) & (place[t] == place[s])).astype(jnp.int32)
        alone[s] = ((active[s] > 0) & (same == 1)).astype(jnp.int32)
    for p in range(own_bins):
        for s in range(slots):
            members[p] = members[p] + ((active[s] > 0) & (place[s] == p)).astype(jnp.int32)

    frequency = lax.broadcasted_iota(jnp.int32, (slots, side), 1)
    folded = jnp.minimum(frequency, side - frequency).astype(F32) / (side / 2.0)
    square = folded * folded
    envelope = jnp.exp(-damping * square)
    sine = jnp.sin(focus * square) * envelope
    cosine = jnp.cos(focus * square) * envelope
    by_sine = jnp.transpose(CONTRAST * sine - AMPLITUDE * cosine)
    by_cosine = jnp.transpose(-(AMPLITUDE * sine + CONTRAST * cosine))
    sums[...] = jnp.zeros(sums.shape, F32)

    def fold(values):
        return jnp.sum(values.reshape(CHUNK // 8, 8, side), axis=0)

    def keep(k, s, total):
        sums[k, pl.ds(s, 1), :] = jnp.sum(total, axis=0, keepdims=True)

    def correlate():
        cross, model, data = (
            jnp.sum(sums[k], axis=1, keepdims=True) / pixels for k in range(3)
        )
        correlation = cross / jnp.sqrt((model + EPSILON) * (data + EPSILON))
        weights = 1.0 / (1.0 + jnp.exp(-float(side) * correlation))
        weight[...] = jnp.broadcast_to(weights.astype(BF16).astype(F32), (slots, side))
        return correlation

    def shares(s, rows, values):
        table = ctf[s, rows, :]
        scaled = weight[pl.ds(s, 1), :] * table
        return (scaled * values).astype(BF16).astype(F32), scaled * table, table

    def renew(previous, numerator, denominator):
        return (
            (numerator + PRIOR_WEIGHT * previous.astype(F32)) / (denominator + PRIOR_WEIGHT)
        ).astype(BF16)

    def update_shared(source, target):
        for p in range(own_bins):

            @pl.when(members[p] > 1)
            def _(p=p):
                number[...] = jnp.zeros(number.shape, F32)

                @pl.loop(0, slots)
                def _(s):
                    @pl.when((active[s] > 0) & (place[s] == p))
                    def _():
                        for rows in chunks:
                            term, power, _ = shares(s, rows, spectra[s, rows, :].astype(F32))
                            number[0, rows, :] += term
                            number[1, rows, :] += power

                for rows in chunks:
                    target[p, rows, :] = renew(
                        source[p, rows, :], number[0, rows, :], number[1, rows, :]
                    )

    for s in range(slots):

        @pl.when(active[s] > 0)
        def _(s=s):
            cross, model, data = zero, zero, zero
            p = place[s]
            for rows in chunks:
                table = (
                    by_sine[rows, s : s + 1] * sine[s : s + 1, :]
                    + by_cosine[rows, s : s + 1] * cosine[s : s + 1, :]
                )
                held = arrived[s // capacity][s % capacity, rows, :]
                spectra[s, rows, :] = held
                ctf[s, rows, :] = table
                values = held.astype(F32)
                predicted = table * current_ref[p, rows, :].astype(F32)
                cross = cross + fold(predicted * values)
                model = model + fold(predicted * predicted)
                data = data + fold(values * values)
            keep(0, s, cross)
            keep(1, s, model)
            keep(2, s, data)

    correlate()
    update_shared(current_ref, middle)

    @pl.loop(0, slots)
    def _(s):
        p = place[s]

        def compare(rows, values, table, reference, cross, model):
            predicted = table * reference.astype(F32)
            return cross + fold(predicted * values), model + fold(predicted * predicted)

        @pl.when(alone[s] > 0)
        def _():
            cross, model = zero, zero
            for rows in chunks:
                values = spectra[s, rows, :].astype(F32)
                term, power, table = shares(s, rows, values)
                reference = renew(current_ref[p, rows, :], term, power)
                middle[p, rows, :] = reference
                cross, model = compare(rows, values, table, reference, cross, model)
            keep(0, s, cross)
            keep(1, s, model)

        @pl.when((active[s] > 0) & (alone[s] == 0))
        def _():
            cross, model = zero, zero
            for rows in chunks:
                values = spectra[s, rows, :].astype(F32)
                cross, model = compare(
                    rows, values, ctf[s, rows, :], middle[p, rows, :], cross, model
                )
            keep(0, s, cross)
            keep(1, s, model)

    correlation = correlate()
    update_shared(middle, refined_ref)

    @pl.loop(0, slots)
    def _(s):
        @pl.when(alone[s] > 0)
        def _():
            p = place[s]
            for rows in chunks:
                term, power, _ = shares(s, rows, spectra[s, rows, :].astype(F32))
                refined_ref[p, rows, :] = renew(middle[p, rows, :], term, power)

    for p in range(own_bins):

        @pl.when(members[p] == 0)
        def _(p=p):
            refined_ref[p] = current_ref[p]

    devices = score_ref.shape[0]
    device = lax.broadcasted_iota(jnp.int32, (devices, 1, 128), 0)
    lane = lax.broadcasted_iota(jnp.int32, (devices, 1, 128), 2)
    board = jnp.zeros((devices, 1, 128), F32)
    for s in range(slots):
        hit = (active[s] > 0) & (device == home[s]) & (lane == particle[s])
        board = jnp.where(hit, correlation[s : s + 1, :].reshape(1, 1, 1), board)
    score_ref[...] = board


def owner_call(bin_count, mic_count, capacity, defocus, bfactor, references, arrived):
    own_bins, side, _ = references.shape
    slots = mic_count * capacity
    return pl.pallas_call(
        functools.partial(owner_kernel, bin_count, mic_count, capacity),
        out_shape=[
            jax.ShapeDtypeStruct(references.shape, BF16),
            jax.ShapeDtypeStruct((mic_count * bin_count, 1, 128), F32),
        ],
        in_specs=[SMEM] * 2 + [VMEM] * (1 + mic_count),
        out_specs=[VMEM] * 2,
        scratch_shapes=[
            pltpu.VMEM((slots, side, side), BF16),
            pltpu.VMEM((slots, side, side), F32),
            pltpu.VMEM((own_bins, side, side), BF16),
            pltpu.VMEM((3, slots, side), F32),
            pltpu.VMEM((slots, side), F32),
            pltpu.VMEM((2, side, side), F32),
        ]
        + [pltpu.SMEM((slots,), jnp.int32)] * 5,
        compiler_params=pltpu.CompilerParams(vmem_limit_bytes=VMEM_BYTES),
        name="owner",
    )(defocus, bfactor, references, *arrived[::-1])


def exchange(blocks, axis):
    size = lax.axis_size(axis)
    return [blocks[0]] + [
        lax.ppermute(blocks[k], axis, [(i, i ^ k) for i in range(size)]) for k in range(1, size)
    ]


def body(images, offsets, ctf_group, particle_bin, bin_place, defocus, bfactor, references):
    mic_count = lax.axis_size("mic")
    bin_count = lax.axis_size("bin")
    particles, side, _ = images.shape
    own_bins = references.shape[0]
    capacity = (3 * particles + 2 * mic_count - 1) // (2 * mic_count)
    rows = side + LABEL_ROWS
    params = pltpu.CompilerParams(vmem_limit_bytes=VMEM_BYTES)

    sent = home_call(
        bin_count, own_bins, bin_place, particle_bin, ctf_group, offsets, images
    )
    arrived = exchange(sent, "bin")

    sent = pl.pallas_call(
        functools.partial(middle_kernel, mic_count, capacity),
        out_shape=[jax.ShapeDtypeStruct((capacity, rows, side), BF16)] * mic_count,
        in_specs=[VMEM] * bin_count,
        out_specs=[VMEM] * mic_count,
        compiler_params=params,
        name="middle",
    )(*arrived[::-1])
    arrived = exchange(sent[::-1], "mic")

    refined, board = owner_call(
        bin_count, mic_count, capacity, defocus, bfactor, references, arrived
    )
    back = lax.all_to_all(board, ("mic", "bin"), split_axis=0, concat_axis=0, tiled=True)
    return (refined, jnp.sum(back, axis=(0, 1))[:particles])


def solution(mesh):
    in_specs = (
        P(("mic", "bin"), None, None),
        P(None, ("mic", "bin")),
        P(("mic", "bin")),
        P(("mic", "bin")),
        P(),
        P(),
        P(),
        P(("mic", "bin"), None, None),
    )
    out_specs = (P(("mic", "bin"), None, None), P(("mic", "bin")))
    return jax.shard_map(body, mesh=mesh, in_specs=in_specs, out_specs=out_specs, check_vma=False)
```

```python
import functools
import math

import jax
import jax.numpy as jnp
import numpy as np
from jax import lax
from jax.experimental import pallas as pl
from jax.experimental.pallas import tpu as pltpu
from jax.sharding import PartitionSpec as P

ITERS = 2
PRIOR_WEIGHT = 0.5
EPSILON = 1e-06
CONTRAST = 0.1
AMPLITUDE = math.sqrt(1.0 - CONTRAST * CONTRAST)

LABEL_ROWS = 8
CHUNK = 32
VMEM_BYTES = 24 * 1024 * 1024

ACTIVE, PLACE, ALONE, HOME, PARTICLE, MEMBERS = range(6)
INFOS = 6

F32 = jnp.float32
BF16 = jnp.bfloat16
VMEM = pl.BlockSpec(memory_space=pltpu.VMEM)
SMEM = pl.BlockSpec(memory_space=pltpu.SMEM)
HBM = pl.BlockSpec(memory_space=pltpu.HBM)
ANY = pl.BlockSpec(memory_space=pl.ANY)


def in_hbm(x):
    return pltpu.with_memory_space_constraint(x, pltpu.HBM)


def hartley(side):
    index = np.arange(side)
    angles = (np.outer(index, index) % side).astype(np.float32) * np.float32(2.0 * math.pi / side)
    return (np.cos(angles) + np.sin(angles)) / np.float32(math.sqrt(side))


def label_block(values, side):
    row = lax.broadcasted_iota(jnp.int32, (LABEL_ROWS, side), 0)
    block = jnp.zeros((LABEL_ROWS, side), jnp.int32)
    for number, value in enumerate(values):
        block = jnp.where(row == number, value, block)
    return block.astype(F32).astype(BF16)


def home_kernel(
    bin_count, own_bins, first, count, place_hbm, bin_hbm, group_hbm, offset_hbm, image_hbm, basis_hbm, *rest
):
    rest = rest[len(rest) - count - 9 :]
    outs, rest = rest[:count], rest[count:]
    spectra, image_ref, basis_ref, place_ref, bin_ref, group_ref, offset_ref, image_sem, sem = rest
    particles, side = image_ref.shape[0], image_ref.shape[1]
    here = lax.axis_index("bin")
    pairs = (
        (basis_hbm, basis_ref),
        (place_hbm, place_ref),
        (bin_hbm, bin_ref),
        (group_hbm, group_ref),
        (offset_hbm, offset_ref),
    )
    copies = [pltpu.make_async_copy(a, b, sem.at[k]) for k, (a, b) in enumerate(pairs)]
    for copy in copies:
        copy.start()

    def image_copy(i):
        return pltpu.make_async_copy(image_hbm.at[i], image_ref.at[i], image_sem.at[i])

    for i in range(particles):
        image_copy(i).start()
    empty = jnp.zeros((LABEL_ROWS, side), BF16)
    for out in outs:
        out[side : side + LABEL_ROWS, :] = empty
    for copy in copies:
        copy.wait()

    @pl.loop(0, particles)
    def _(i):
        image_copy(i).wait()
        place = place_ref[bin_ref[i]]
        owner = place // own_bins
        step_of = lax.rem(owner, bin_count) ^ here

        @pl.when((step_of >= first) & (step_of < first + count))
        def _():
            moved = pltpu.roll(image_ref[i].astype(F32), side - offset_ref[0, i], 0).astype(BF16)
            columns = pltpu.roll(basis_ref[...].astype(F32), offset_ref[1, i], 0).astype(BF16)
            half = jnp.dot(basis_ref[...], moved, preferred_element_type=F32).astype(BF16)
            spectra[...] = jnp.dot(half, columns, preferred_element_type=F32).astype(BF16)
            labels = label_block(
                (
                    1 + owner // bin_count,
                    lax.rem(place, own_bins),
                    group_ref[i],
                    i * bin_count + here,
                ),
                side,
            )
            for k in range(count):

                @pl.when(step_of == first + k)
                def _():
                    outs[k][0:side, :] = spectra[...]
                    outs[k][side : side + LABEL_ROWS, :] = labels


def home_call(bin_count, own_bins, first, count, operands, after=()):
    images, particles, side = operands[4], operands[4].shape[0], operands[4].shape[1]
    return pl.pallas_call(
        functools.partial(home_kernel, bin_count, own_bins, first, count),
        out_shape=[jax.ShapeDtypeStruct((side + LABEL_ROWS, side), BF16)] * count,
        in_specs=[HBM] * 6 + [ANY] * len(after),
        out_specs=[VMEM] * count,
        scratch_shapes=[
            pltpu.VMEM((side, side), BF16),
            pltpu.VMEM(images.shape, BF16),
            pltpu.VMEM((side, side), BF16),
        ]
        + [pltpu.SMEM(x.shape, jnp.int32) for x in operands[:4]]
        + [pltpu.SemaphoreType.DMA((particles,)), pltpu.SemaphoreType.DMA((5,))],
        compiler_params=pltpu.CompilerParams(vmem_limit_bytes=VMEM_BYTES),
        name="home",
    )(*operands, *after)


def middle_kernel(mic_count, capacity, *rest):
    arrived, outs = rest[: len(rest) - 2 * mic_count], rest[len(rest) - 2 * mic_count :]
    outs, label_outs = outs[:mic_count], outs[mic_count:]
    side = arrived[0].shape[1]
    here = lax.axis_index("mic")
    for out in label_outs:
        out[...] = jnp.zeros(out.shape, F32)
    labels = [block[side : side + LABEL_ROWS, :128].astype(F32) for block in arrived]
    targets = [jnp.max(block[0:1]).astype(jnp.int32) for block in labels]
    counts = [jnp.int32(0)] * mic_count
    for block, label, target in zip(arrived, labels, targets):
        step_of = (target - 1) ^ here
        for step in range(mic_count):
            chosen = (target > 0) & (step_of == step)

            @pl.when(chosen)
            def _(block=block, label=label, step=step, slot=counts[step]):
                outs[step][slot] = block[0:side, :]
                label_outs[step][slot] = label

            counts[step] = counts[step] + chosen.astype(jnp.int32)


def middle_call(mic_count, capacity, arrived):
    side = arrived[0].shape[1]
    outs = pl.pallas_call(
        functools.partial(middle_kernel, mic_count, capacity),
        out_shape=[jax.ShapeDtypeStruct((capacity, side, side), BF16)] * mic_count
        + [jax.ShapeDtypeStruct((capacity, LABEL_ROWS, 128), F32)] * mic_count,
        in_specs=[VMEM] * len(arrived),
        out_specs=[VMEM] * (2 * mic_count),
        compiler_params=pltpu.CompilerParams(vmem_limit_bytes=VMEM_BYTES),
        name="middle",
    )(*arrived)
    return outs[:mic_count], outs[mic_count:]


def fold(values):
    return jnp.sum(values.reshape(values.shape[0] // 8, 8, values.shape[1]), axis=0)


def chunks_of(side):
    return [slice(c, c + CHUNK) for c in range(0, side, CHUNK)]


def shares(ctf, weight, s, rows, values):
    table = ctf[s, rows, :]
    scaled = weight[pl.ds(s, 1), :] * table
    return (scaled * values).astype(BF16).astype(F32), scaled * table, table


def renew(previous, numerator, denominator):
    return (
        (numerator + PRIOR_WEIGHT * previous.astype(F32)) / (denominator + PRIOR_WEIGHT)
    ).astype(BF16)


def update_shared(info, spectra, ctf, weight, number, source, target):
    chunks = chunks_of(source.shape[1])

    @pl.loop(0, source.shape[0])
    def _(p):
        @pl.when(info[MEMBERS, p] > 1)
        def _():
            number[...] = jnp.zeros(number.shape, F32)

            @pl.loop(0, spectra.shape[0])
            def _(s):
                @pl.when((info[ACTIVE, s] > 0) & (info[PLACE, s] == p))
                def _():
                    for rows in chunks:
                        values = spectra[s, rows, :].astype(F32)
                        term, power, _ = shares(ctf, weight, s, rows, values)
                        number[0, rows, :] += term
                        number[1, rows, :] += power

            for rows in chunks:
                target[p, rows, :] = renew(
                    source[p, rows, :], number[0, rows, :], number[1, rows, :]
                )


def ready_kernel(
    bin_count, mic_count, capacity, focus_ref, damping_ref, current_ref, *rest
):
    labels, near = rest[:mic_count], rest[mic_count:-3]
    info, ctf, sums = rest[-3:]
    own_bins, side, _ = current_ref.shape
    slots = mic_count * capacity
    here = lax.axis_index("mic")
    zero = jnp.zeros((8, side), F32)

    codes = []
    for s in range(slots):
        block = labels[s // capacity][s % capacity]
        code = block[1:2] + 256.0 * block[2:3] + 65536.0 * block[3:4]
        codes.append(jnp.max(jnp.where(block[0:1] > 0, code, -1.0)).astype(jnp.int32))
    row = lax.broadcasted_iota(jnp.int32, (slots, side), 0)
    focus = jnp.zeros((slots, side), F32)
    damping = jnp.zeros((slots, side), F32)
    for p in range(own_bins):
        info[MEMBERS, p] = jnp.int32(0)
    for s in range(slots):
        active = (codes[s] >= 0).astype(jnp.int32)
        code = jnp.maximum(codes[s], 0)
        group = (code >> 8) & 255
        sender = code >> 16
        place = code & 255
        info[ACTIVE, s] = active
        info[PLACE, s] = place
        info[HOME, s] = (here ^ (s // capacity)) * bin_count + lax.rem(sender, bin_count)
        info[PARTICLE, s] = sender // bin_count
        info[MEMBERS, place] = info[MEMBERS, place] + active
        focus = jnp.where(row == s, focus_ref[group], focus)
        damping = jnp.where(row == s, damping_ref[group], damping)
    for s in range(slots):
        single = (info[ACTIVE, s] > 0) & (info[MEMBERS, info[PLACE, s]] == 1)
        info[ALONE, s] = single.astype(jnp.int32)

    frequency = lax.broadcasted_iota(jnp.int32, (slots, side), 1)
    folded = jnp.minimum(frequency, side - frequency).astype(F32) / (side / 2.0)
    square = folded * folded
    envelope = jnp.exp(-damping * square)
    sine = jnp.sin(focus * square) * envelope
    cosine = jnp.cos(focus * square) * envelope
    by_sine = jnp.transpose(CONTRAST * sine - AMPLITUDE * cosine)
    by_cosine = jnp.transpose(-(AMPLITUDE * sine + CONTRAST * cosine))
    sums[...] = jnp.zeros(sums.shape, F32)

    for s in range(slots):

        @pl.when(info[ACTIVE, s] > 0)
        def _(s=s):
            cross, model, data = zero, zero, zero
            p = info[PLACE, s]
            for rows in chunks_of(side):
                table = (
                    by_sine[rows, s : s + 1] * sine[s : s + 1, :]
                    + by_cosine[rows, s : s + 1] * cosine[s : s + 1, :]
                )
                ctf[s, rows, :] = table
                predicted = table * current_ref[p, rows, :].astype(F32)
                model = model + fold(predicted * predicted)
                if s < len(near) * capacity:
                    values = near[s // capacity][s % capacity, rows, :].astype(F32)
                    cross = cross + fold(predicted * values)
                    data = data + fold(values * values)
            for k, total in enumerate((cross, model, data)):
                sums[k, s : s + 1, :] = jnp.sum(total, axis=0, keepdims=True)


def ready_call(bin_count, mic_count, capacity, defocus, bfactor, references, labels, near):
    own_bins, side, _ = references.shape
    slots = mic_count * capacity
    return pl.pallas_call(
        functools.partial(ready_kernel, bin_count, mic_count, capacity),
        out_shape=[
            jax.ShapeDtypeStruct((INFOS, max(slots, own_bins)), jnp.int32),
            jax.ShapeDtypeStruct((slots, side, side), F32),
            jax.ShapeDtypeStruct((3, slots, side), F32),
        ],
        in_specs=[SMEM] * 2 + [VMEM] * (1 + len(labels) + len(near)),
        out_specs=[SMEM, VMEM, VMEM],
        compiler_params=pltpu.CompilerParams(vmem_limit_bytes=VMEM_BYTES),
        cost_estimate=pl.CostEstimate(flops=4 << 20, bytes_accessed=4 << 20, transcendentals=0),
        name="ready",
    )(defocus, bfactor, references, *labels, *near)


def owner_kernel(capacity, near, info, current_ref, ctf, known, *rest):
    arrived, (spectra, middle, weight, score_ref, sums, number) = rest[:-6], rest[-6:]
    arrived = arrived[::-1]
    slots, side, _ = ctf.shape
    pixels = float(side * side)
    chunks = chunks_of(side)
    zero = jnp.zeros((8, side), F32)
    sums[...] = known[...]

    def keep(k, s, total):
        sums[k, pl.ds(s, 1), :] = jnp.sum(total, axis=0, keepdims=True)

    def correlate():
        cross, model, data = (
            jnp.sum(sums[k], axis=1, keepdims=True) / pixels for k in range(3)
        )
        correlation = cross / jnp.sqrt((model + EPSILON) * (data + EPSILON))
        weights = 1.0 / (1.0 + jnp.exp(-float(side) * correlation))
        weight[...] = jnp.broadcast_to(weights.astype(BF16).astype(F32), (slots, side))
        return correlation

    for s in range(slots):

        @pl.when(info[ACTIVE, s] > 0)
        def _(s=s):
            block = arrived[s // capacity]
            if s < near * capacity:
                spectra[s] = block[s % capacity]
            else:
                cross, data = zero, zero
                p = info[PLACE, s]
                for rows in chunks:
                    held = block[s % capacity, rows, :]
                    spectra[s, rows, :] = held
                    values = held.astype(F32)
                    predicted = ctf[s, rows, :] * current_ref[p, rows, :].astype(F32)
                    cross = cross + fold(predicted * values)
                    data = data + fold(values * values)
                keep(0, s, cross)
                keep(2, s, data)

    correlate()
    update_shared(info, spectra, ctf, weight, number, current_ref, middle)

    @pl.loop(0, slots)
    def _(s):
        p = info[PLACE, s]

        def compare(values, table, reference, cross, model):
            predicted = table * reference.astype(F32)
            return cross + fold(predicted * values), model + fold(predicted * predicted)

        @pl.when(info[ALONE, s] > 0)
        def _():
            cross, model = zero, zero
            for rows in chunks:
                values = spectra[s, rows, :].astype(F32)
                term, power, table = shares(ctf, weight, s, rows, values)
                reference = renew(current_ref[p, rows, :], term, power)
                middle[p, rows, :] = reference
                cross, model = compare(values, table, reference, cross, model)
            keep(0, s, cross)
            keep(1, s, model)

        @pl.when((info[ACTIVE, s] > 0) & (info[ALONE, s] == 0))
        def _():
            cross, model = zero, zero
            for rows in chunks:
                values = spectra[s, rows, :].astype(F32)
                cross, model = compare(values, ctf[s, rows, :], middle[p, rows, :], cross, model)
            keep(0, s, cross)
            keep(1, s, model)

    correlation = correlate()
    devices = score_ref.shape[0]
    device = lax.broadcasted_iota(jnp.int32, (devices, 1, 128), 0)
    lane = lax.broadcasted_iota(jnp.int32, (devices, 1, 128), 2)
    board = jnp.zeros((devices, 1, 128), F32)
    for s in range(slots):
        hit = (info[ACTIVE, s] > 0) & (device == info[HOME, s]) & (lane == info[PARTICLE, s])
        board = jnp.where(hit, correlation[s : s + 1, :].reshape(1, 1, 1), board)
    score_ref[...] = board


def owner_call(devices, capacity, near, info, references, ctf, known, arrived):
    slots, side, _ = ctf.shape
    return pl.pallas_call(
        functools.partial(owner_kernel, capacity, near),
        out_shape=[
            jax.ShapeDtypeStruct((slots, side, side), BF16),
            jax.ShapeDtypeStruct(references.shape, BF16),
            jax.ShapeDtypeStruct((slots, side), F32),
            jax.ShapeDtypeStruct((devices, 1, 128), F32),
        ],
        in_specs=[SMEM] + [VMEM] * (3 + len(arrived)),
        out_specs=[VMEM] * 4,
        scratch_shapes=[
            pltpu.VMEM((3, slots, side), F32),
            pltpu.VMEM((2, side, side), F32),
        ],
        compiler_params=pltpu.CompilerParams(vmem_limit_bytes=VMEM_BYTES),
        name="owner",
    )(info, references, ctf, known, *arrived[::-1])


def last_kernel(info, current_ref, spectra, ctf, middle, weight, refined_ref, number):
    slots, side, _ = ctf.shape
    update_shared(info, spectra, ctf, weight, number, middle, refined_ref)

    @pl.loop(0, slots)
    def _(s):
        @pl.when(info[ALONE, s] > 0)
        def _():
            p = info[PLACE, s]
            for rows in chunks_of(side):
                values = spectra[s, rows, :].astype(F32)
                term, power, _ = shares(ctf, weight, s, rows, values)
                refined_ref[p, rows, :] = renew(middle[p, rows, :], term, power)

    @pl.loop(0, current_ref.shape[0])
    def _(p):
        @pl.when(info[MEMBERS, p] == 0)
        def _():
            refined_ref[p] = current_ref[p]


def last_call(info, references, spectra, ctf, middle, weight):
    side = ctf.shape[1]
    return pl.pallas_call(
        last_kernel,
        out_shape=jax.ShapeDtypeStruct(references.shape, BF16),
        in_specs=[SMEM] + [VMEM] * 5,
        out_specs=VMEM,
        scratch_shapes=[pltpu.VMEM((2, side, side), F32)],
        compiler_params=pltpu.CompilerParams(vmem_limit_bytes=VMEM_BYTES),
        name="last",
    )(info, references, spectra, ctf, middle, weight)


def exchange(blocks, axis):
    size = lax.axis_size(axis)
    return [blocks[0]] + [
        lax.ppermute(blocks[k], axis, [(i, i ^ k) for i in range(size)]) for k in range(1, size)
    ]


def body(images, offsets, ctf_group, particle_bin, bin_place, defocus, bfactor, references):
    mic_count = lax.axis_size("mic")
    bin_count = lax.axis_size("bin")
    particles, side, _ = images.shape
    own_bins = references.shape[0]
    capacity = (3 * particles + 2 * mic_count - 1) // (2 * mic_count)
    near = 2

    basis = jnp.asarray(hartley(side), BF16)
    operands = (bin_place, particle_bin, ctf_group, offsets, images, basis)
    operands = tuple(map(in_hbm, operands))
    far = max(1, bin_count // 4)
    rest = bin_count - far
    sent_far = home_call(bin_count, own_bins, rest, far, operands)
    sent_near = home_call(bin_count, own_bins, 0, rest, operands, after=(sent_far[-1],))
    arrived = exchange(list(sent_near) + list(sent_far), "bin")

    sent, labels = middle_call(mic_count, capacity, arrived[::-1])
    arrived = exchange(sent, "mic")
    labels = exchange(labels, "mic")

    info, ctf, known = ready_call(
        bin_count, mic_count, capacity, defocus, bfactor, references, labels, arrived[:near]
    )
    spectra, middle, weight, board = owner_call(
        mic_count * bin_count, capacity, near, info, references, ctf, known, arrived
    )
    back = lax.all_to_all(board, ("mic", "bin"), split_axis=0, concat_axis=0, tiled=True)
    refined = last_call(info, references, spectra, ctf, middle, weight)
    return (refined, jnp.sum(back, axis=(0, 1))[:particles])


def solution(mesh):
    in_specs = (
        P(("mic", "bin"), None, None),
        P(None, ("mic", "bin")),
        P(("mic", "bin")),
        P(("mic", "bin")),
        P(),
        P(),
        P(),
        P(("mic", "bin"), None, None),
    )
    out_specs = (P(("mic", "bin"), None, None), P(("mic", "bin")))
    return jax.shard_map(body, mesh=mesh, in_specs=in_specs, out_specs=out_specs, check_vma=False)
```

```python
import functools
import math

import jax
import jax.numpy as jnp
import numpy as np
from jax import lax
from jax.experimental import pallas as pl
from jax.experimental.pallas import tpu as pltpu
from jax.sharding import PartitionSpec as P

ITERS = 2
PRIOR_WEIGHT = 0.5
EPSILON = 1e-06
CONTRAST = 0.1
AMPLITUDE = math.sqrt(1.0 - CONTRAST * CONTRAST)

LABEL_ROWS = 8
CHUNK = 32
VMEM_BYTES = 24 * 1024 * 1024

ACTIVE, PLACE, ALONE, HOME, PARTICLE, MEMBERS = range(6)
INFOS = 6

F32 = jnp.float32
BF16 = jnp.bfloat16
VMEM = pl.BlockSpec(memory_space=pltpu.VMEM)
SMEM = pl.BlockSpec(memory_space=pltpu.SMEM)
HBM = pl.BlockSpec(memory_space=pltpu.HBM)
ANY = pl.BlockSpec(memory_space=pl.ANY)


def in_hbm(x):
    return pltpu.with_memory_space_constraint(x, pltpu.HBM)


def hartley(side):
    index = np.arange(side)
    angles = (np.outer(index, index) % side).astype(np.float32) * np.float32(2.0 * math.pi / side)
    return (np.cos(angles) + np.sin(angles)) / np.float32(math.sqrt(side))


def label_block(values, side):
    row = lax.broadcasted_iota(jnp.int32, (LABEL_ROWS, side), 0)
    block = jnp.zeros((LABEL_ROWS, side), jnp.int32)
    for number, value in enumerate(values):
        block = jnp.where(row == number, value, block)
    return block.astype(F32).astype(BF16)


def home_kernel(
    bin_count, own_bins, first, count, place_hbm, bin_hbm, group_hbm, offset_hbm, image_hbm, basis_hbm, *rest
):
    rest = rest[len(rest) - count - 9 :]
    outs, rest = rest[:count], rest[count:]
    spectra, image_ref, basis_ref, place_ref, bin_ref, group_ref, offset_ref, image_sem, sem = rest
    particles, side = image_ref.shape[0], image_ref.shape[1]
    here = lax.axis_index("bin")
    pairs = (
        (basis_hbm, basis_ref),
        (place_hbm, place_ref),
        (bin_hbm, bin_ref),
        (group_hbm, group_ref),
        (offset_hbm, offset_ref),
    )
    copies = [pltpu.make_async_copy(a, b, sem.at[k]) for k, (a, b) in enumerate(pairs)]
    for copy in copies:
        copy.start()

    def image_copy(i):
        return pltpu.make_async_copy(image_hbm.at[i], image_ref.at[i], image_sem.at[i])

    for i in range(particles):
        image_copy(i).start()
    empty = jnp.zeros((LABEL_ROWS, side), BF16)
    for out in outs:
        out[side : side + LABEL_ROWS, :] = empty
    for copy in copies:
        copy.wait()

    @pl.loop(0, particles)
    def _(i):
        image_copy(i).wait()
        place = place_ref[bin_ref[i]]
        owner = place // own_bins
        step_of = lax.rem(owner, bin_count) ^ here

        @pl.when((step_of >= first) & (step_of < first + count))
        def _():
            moved = pltpu.roll(image_ref[i].astype(F32), side - offset_ref[0, i], 0).astype(BF16)
            columns = pltpu.roll(basis_ref[...].astype(F32), offset_ref[1, i], 0).astype(BF16)
            half = jnp.dot(basis_ref[...], moved, preferred_element_type=F32).astype(BF16)
            spectra[...] = jnp.dot(half, columns, preferred_element_type=F32).astype(BF16)
            labels = label_block(
                (
                    1 + owner // bin_count,
                    lax.rem(place, own_bins),
                    group_ref[i],
                    i * bin_count + here,
                ),
                side,
            )
            for k in range(count):

                @pl.when(step_of == first + k)
                def _():
                    outs[k][0:side, :] = spectra[...]
                    outs[k][side : side + LABEL_ROWS, :] = labels


def home_call(bin_count, own_bins, first, count, operands, after=()):
    images, particles, side = operands[4], operands[4].shape[0], operands[4].shape[1]
    return pl.pallas_call(
        functools.partial(home_kernel, bin_count, own_bins, first, count),
        out_shape=[jax.ShapeDtypeStruct((side + LABEL_ROWS, side), BF16)] * count,
        in_specs=[HBM] * 6 + [ANY] * len(after),
        out_specs=[VMEM] * count,
        scratch_shapes=[
            pltpu.VMEM((side, side), BF16),
            pltpu.VMEM(images.shape, BF16),
            pltpu.VMEM((side, side), BF16),
        ]
        + [pltpu.SMEM(x.shape, jnp.int32) for x in operands[:4]]
        + [pltpu.SemaphoreType.DMA((particles,)), pltpu.SemaphoreType.DMA((5,))],
        compiler_params=pltpu.CompilerParams(vmem_limit_bytes=VMEM_BYTES),
        name="home",
    )(*operands, *after)


def middle_kernel(mic_count, capacity, *rest):
    arrived, outs = rest[: len(rest) - mic_count], rest[len(rest) - mic_count :]
    rows, side = arrived[0].shape
    here = lax.axis_index("mic")
    empty = jnp.zeros((LABEL_ROWS, side), BF16)
    for out in outs:
        for j in range(capacity):
            out[j, rows - LABEL_ROWS : rows, :] = empty
    targets = [
        jnp.max(block[rows - LABEL_ROWS : rows, :128].astype(F32)[0:1]).astype(jnp.int32)
        for block in arrived
    ]
    counts = [jnp.int32(0)] * mic_count
    for block, target in zip(arrived, targets):
        step_of = (target - 1) ^ here
        for step in range(mic_count):
            chosen = (target > 0) & (step_of == step)

            @pl.when(chosen)
            def _(block=block, step=step, slot=counts[step]):
                outs[step][slot] = block[...]

            counts[step] = counts[step] + chosen.astype(jnp.int32)


def middle_call(mic_count, capacity, arrived):
    return pl.pallas_call(
        functools.partial(middle_kernel, mic_count, capacity),
        out_shape=[jax.ShapeDtypeStruct((capacity, *arrived[0].shape), BF16)] * mic_count,
        in_specs=[VMEM] * len(arrived),
        out_specs=[VMEM] * mic_count,
        compiler_params=pltpu.CompilerParams(vmem_limit_bytes=VMEM_BYTES),
        name="middle",
    )(*arrived)


def fold(values):
    return jnp.sum(values.reshape(values.shape[0] // 8, 8, values.shape[1]), axis=0)


def chunks_of(side):
    return [slice(c, c + CHUNK) for c in range(0, side, CHUNK)]


def shares(ctf, weight, s, rows, values):
    table = ctf[s, rows, :]
    scaled = weight[pl.ds(s, 1), :] * table
    return (scaled * values).astype(BF16).astype(F32), scaled * table, table


def renew(previous, numerator, denominator):
    return (
        (numerator + PRIOR_WEIGHT * previous.astype(F32)) / (denominator + PRIOR_WEIGHT)
    ).astype(BF16)


def update_shared(info, spectra, ctf, weight, number, source, target):
    chunks = chunks_of(source.shape[1])

    @pl.loop(0, source.shape[0])
    def _(p):
        @pl.when(info[MEMBERS, p] > 1)
        def _():
            number[...] = jnp.zeros(number.shape, F32)

            @pl.loop(0, spectra.shape[0])
            def _(s):
                @pl.when((info[ACTIVE, s] > 0) & (info[PLACE, s] == p))
                def _():
                    for rows in chunks:
                        values = spectra[s, rows, :].astype(F32)
                        term, power, _ = shares(ctf, weight, s, rows, values)
                        number[0, rows, :] += term
                        number[1, rows, :] += power

            for rows in chunks:
                target[p, rows, :] = renew(
                    source[p, rows, :], number[0, rows, :], number[1, rows, :]
                )


def decode(labels, capacity, bin_count, own_bins, info, focus_ref, damping_ref):
    slots = len(labels)
    here = lax.axis_index("mic")
    codes = []
    for s in range(slots):
        block = labels[s]
        code = block[1:2] + 256.0 * block[2:3] + 65536.0 * block[3:4]
        codes.append(jnp.max(jnp.where(block[0:1] > 0, code, -1.0)).astype(jnp.int32))
    row = lax.broadcasted_iota(jnp.int32, (8, 128), 0)
    focus = jnp.zeros((8, 128), F32)
    damping = jnp.zeros((8, 128), F32)
    for p in range(own_bins):
        info[MEMBERS, p] = jnp.int32(0)
    for s in range(slots):
        active = (codes[s] >= 0).astype(jnp.int32)
        code = jnp.maximum(codes[s], 0)
        group = (code >> 8) & 255
        sender = code >> 16
        place = code & 255
        info[ACTIVE, s] = active
        info[PLACE, s] = place
        info[HOME, s] = (here ^ (s // capacity)) * bin_count + lax.rem(sender, bin_count)
        info[PARTICLE, s] = sender // bin_count
        info[MEMBERS, place] = info[MEMBERS, place] + active
        focus = jnp.where(row == s, focus_ref[group], focus)
        damping = jnp.where(row == s, damping_ref[group], damping)
    for s in range(slots):
        single = (info[ACTIVE, s] > 0) & (info[MEMBERS, info[PLACE, s]] == 1)
        info[ALONE, s] = single.astype(jnp.int32)
    return focus[:, :1], damping[:, :1]


def ctf_factors(focus, damping, side):
    frequency = lax.broadcasted_iota(jnp.int32, (8, side), 1)
    folded = jnp.minimum(frequency, side - frequency).astype(F32) / (side / 2.0)
    square = folded * folded
    envelope = jnp.exp(-damping * square)
    sine = jnp.sin(focus * square) * envelope
    cosine = jnp.cos(focus * square) * envelope
    by_sine = jnp.transpose(CONTRAST * sine - AMPLITUDE * cosine)
    by_cosine = jnp.transpose(-(AMPLITUDE * sine + CONTRAST * cosine))
    return by_sine, sine, by_cosine, cosine


def ctf_chunk(factors, s, rows):
    by_sine, sine, by_cosine, cosine = factors
    return (
        by_sine[rows, s : s + 1] * sine[s : s + 1, :]
        + by_cosine[rows, s : s + 1] * cosine[s : s + 1, :]
    )


def first_compare(info, factors, current_ref, spectra, ctf, sums, s, block):
    side = ctf.shape[1]
    p = info[PLACE, s]
    cross = model = data = jnp.zeros((8, side), F32)
    for rows in chunks_of(side):
        table = ctf_chunk(factors, s, rows)
        ctf[s, rows, :] = table
        held = block[rows, :]
        spectra[s, rows, :] = held
        values = held.astype(F32)
        predicted = table * current_ref[p, rows, :].astype(F32)
        cross = cross + fold(predicted * values)
        model = model + fold(predicted * predicted)
        data = data + fold(values * values)
    for k, total in enumerate((cross, model, data)):
        sums[k, s : s + 1, :] = jnp.sum(total, axis=0, keepdims=True)


def owner_kernel(
    bin_count, mic_count, focus_ref, damping_ref, current_ref, *rest
):
    arrived, rest = rest[:mic_count][::-1], rest[mic_count:]
    spectra_hbm, middle_hbm, weight, label_ref, score_ref = rest[:5]
    spectra, middle, ctf, sums, number, info, spectra_sem, middle_sem = rest[5:]
    own_bins, side, _ = current_ref.shape
    capacity = arrived[0].shape[0]
    slots = mic_count * capacity
    pixels = float(side * side)
    chunks = chunks_of(side)
    zero = jnp.zeros((8, side), F32)

    copies = [
        pltpu.make_async_copy(
            block.at[:, pl.ds(0, side)],
            spectra_hbm.at[pl.ds(step * capacity, capacity)],
            spectra_sem.at[step],
        )
        for step, block in enumerate(arrived)
    ]
    for copy in copies:
        copy.start()
    labels = [
        arrived[s // capacity][s % capacity, side : side + LABEL_ROWS, :128].astype(F32)
        for s in range(slots)
    ]
    for s in range(slots):
        label_ref[s] = labels[s]
    focus, damping = decode(labels, capacity, bin_count, own_bins, info, focus_ref, damping_ref)
    factors = ctf_factors(focus, damping, side)
    sums[...] = jnp.zeros(sums.shape, F32)

    def middle_copy(p):
        return pltpu.make_async_copy(middle.at[p], middle_hbm.at[p], middle_sem.at[p])

    def keep(k, s, total):
        sums[k, pl.ds(s, 1), :] = jnp.sum(total, axis=0, keepdims=True)

    def correlate():
        cross, model, data = (
            jnp.sum(sums[k], axis=1, keepdims=True) / pixels for k in range(3)
        )
        correlation = cross / jnp.sqrt((model + EPSILON) * (data + EPSILON))
        weights = 1.0 / (1.0 + jnp.exp(-float(side) * correlation))
        weight[...] = jnp.broadcast_to(weights.astype(BF16).astype(F32), (8, side))
        return correlation

    for s in range(slots):

        @pl.when(info[ACTIVE, s] > 0)
        def _(s=s):
            block = arrived[s // capacity].at[s % capacity]
            first_compare(info, factors, current_ref, spectra, ctf, sums, s, block)

    correlate()
    update_shared(info, spectra, ctf, weight, number, current_ref, middle)

    @pl.loop(0, slots)
    def _(s):
        p = info[PLACE, s]

        def compare(values, table, reference, cross, model):
            predicted = table * reference.astype(F32)
            return cross + fold(predicted * values), model + fold(predicted * predicted)

        @pl.when(info[ALONE, s] > 0)
        def _():
            cross, model = zero, zero
            for rows in chunks:
                values = spectra[s, rows, :].astype(F32)
                term, power, table = shares(ctf, weight, s, rows, values)
                reference = renew(current_ref[p, rows, :], term, power)
                middle[p, rows, :] = reference
                cross, model = compare(values, table, reference, cross, model)
            keep(0, s, cross)
            keep(1, s, model)
            middle_copy(p).start()

        @pl.when((info[ACTIVE, s] > 0) & (info[ALONE, s] == 0))
        def _():
            cross, model = zero, zero
            for rows in chunks:
                values = spectra[s, rows, :].astype(F32)
                cross, model = compare(values, ctf[s, rows, :], middle[p, rows, :], cross, model)
            keep(0, s, cross)
            keep(1, s, model)

    @pl.loop(0, own_bins)
    def _(p):
        @pl.when(info[MEMBERS, p] > 1)
        def _():
            middle_copy(p).start()

    correlation = correlate()
    devices = score_ref.shape[0]
    device = lax.broadcasted_iota(jnp.int32, (devices, 1, 128), 0)
    lane = lax.broadcasted_iota(jnp.int32, (devices, 1, 128), 2)
    board = jnp.zeros((devices, 1, 128), F32)
    for s in range(slots):
        hit = (info[ACTIVE, s] > 0) & (device == info[HOME, s]) & (lane == info[PARTICLE, s])
        board = jnp.where(hit, correlation[s : s + 1, :].reshape(1, 1, 1), board)
    score_ref[...] = board
    for copy in copies:
        copy.wait()

    @pl.loop(0, own_bins)
    def _(p):
        @pl.when(info[MEMBERS, p] > 0)
        def _():
            middle_copy(p).wait()


def owner_call(bin_count, mic_count, defocus, bfactor, references, arrived):
    own_bins, side, _ = references.shape
    slots = mic_count * arrived[0].shape[0]
    return pl.pallas_call(
        functools.partial(owner_kernel, bin_count, mic_count),
        out_shape=[
            pltpu.HBM((slots, side, side), BF16),
            pltpu.HBM(references.shape, BF16),
            jax.ShapeDtypeStruct((8, side), F32),
            jax.ShapeDtypeStruct((slots, LABEL_ROWS, 128), F32),
            jax.ShapeDtypeStruct((mic_count * bin_count, 1, 128), F32),
        ],
        in_specs=[SMEM] * 2 + [VMEM] * (1 + mic_count),
        out_specs=[HBM, HBM, VMEM, VMEM, VMEM],
        scratch_shapes=[
            pltpu.VMEM((slots, side, side), BF16),
            pltpu.VMEM(references.shape, BF16),
            pltpu.VMEM((slots, side, side), F32),
            pltpu.VMEM((3, 8, side), F32),
            pltpu.VMEM((2, side, side), F32),
            pltpu.SMEM((INFOS, max(8, own_bins)), jnp.int32),
            pltpu.SemaphoreType.DMA((mic_count,)),
            pltpu.SemaphoreType.DMA((own_bins,)),
        ],
        compiler_params=pltpu.CompilerParams(vmem_limit_bytes=VMEM_BYTES),
        name="owner",
    )(defocus, bfactor, references, *arrived[::-1])


def last_kernel(
    capacity, bin_count, focus_ref, damping_ref, current_ref, weight, spectra_hbm, middle_hbm, *rest
):
    label_ref, refined_ref, spectra, middle, ctf, number, info, spectra_sem, middle_sem = rest
    slots, side, _ = ctf.shape
    own_bins = current_ref.shape[0]
    copies = [
        pltpu.make_async_copy(spectra_hbm, spectra, spectra_sem),
        pltpu.make_async_copy(middle_hbm, middle, middle_sem),
    ]
    for copy in copies:
        copy.start()
    labels = [label_ref[s] for s in range(slots)]
    focus, damping = decode(labels, capacity, bin_count, own_bins, info, focus_ref, damping_ref)
    factors = ctf_factors(focus, damping, side)
    for s in range(slots):

        @pl.when(info[ACTIVE, s] > 0)
        def _(s=s):
            for rows in chunks_of(side):
                ctf[s, rows, :] = ctf_chunk(factors, s, rows)

    for copy in copies:
        copy.wait()
    update_shared(info, spectra, ctf, weight, number, middle, refined_ref)

    @pl.loop(0, slots)
    def _(s):
        @pl.when(info[ALONE, s] > 0)
        def _():
            p = info[PLACE, s]
            for rows in chunks_of(side):
                values = spectra[s, rows, :].astype(F32)
                term, power, _ = shares(ctf, weight, s, rows, values)
                refined_ref[p, rows, :] = renew(middle[p, rows, :], term, power)

    @pl.loop(0, own_bins)
    def _(p):
        @pl.when(info[MEMBERS, p] == 0)
        def _():
            refined_ref[p] = current_ref[p]


def last_call(
    capacity, bin_count, defocus, bfactor, references, weight, spectra, middle, labels
):
    slots, side, _ = spectra.shape
    own_bins = references.shape[0]
    return pl.pallas_call(
        functools.partial(last_kernel, capacity, bin_count),
        out_shape=jax.ShapeDtypeStruct(references.shape, BF16),
        in_specs=[SMEM] * 2 + [VMEM] * 2 + [HBM] * 2 + [VMEM],
        out_specs=VMEM,
        scratch_shapes=[
            pltpu.VMEM(spectra.shape, BF16),
            pltpu.VMEM(references.shape, BF16),
            pltpu.VMEM((slots, side, side), F32),
            pltpu.VMEM((2, side, side), F32),
            pltpu.SMEM((INFOS, max(8, own_bins)), jnp.int32),
            pltpu.SemaphoreType.DMA(()),
            pltpu.SemaphoreType.DMA(()),
        ],
        compiler_params=pltpu.CompilerParams(vmem_limit_bytes=VMEM_BYTES),
        cost_estimate=pl.CostEstimate(flops=4 << 20, bytes_accessed=4 << 20, transcendentals=0),
        name="last",
    )(defocus, bfactor, references, weight, in_hbm(spectra), in_hbm(middle), labels)


def exchange(blocks, axis):
    size = lax.axis_size(axis)
    return [blocks[0]] + [
        lax.ppermute(blocks[k], axis, [(i, i ^ k) for i in range(size)]) for k in range(1, size)
    ]


def body(images, offsets, ctf_group, particle_bin, bin_place, defocus, bfactor, references):
    mic_count = lax.axis_size("mic")
    bin_count = lax.axis_size("bin")
    particles, side, _ = images.shape
    own_bins = references.shape[0]
    capacity = (3 * particles + 2 * mic_count - 1) // (2 * mic_count)

    basis = jnp.asarray(hartley(side), BF16)
    operands = (bin_place, particle_bin, ctf_group, offsets, images, basis)
    operands = tuple(map(in_hbm, operands))
    far = max(1, bin_count // 4)
    rest = bin_count - far
    sent_far = home_call(bin_count, own_bins, rest, far, operands)
    sent_near = home_call(bin_count, own_bins, 0, rest, operands, after=(sent_far[-1],))
    arrived = exchange(list(sent_near) + list(sent_far), "bin")

    sent = middle_call(mic_count, capacity, arrived[::-1])
    arrived = exchange(sent, "mic")
    spectra, middle, weight, labels, board = owner_call(
        bin_count, mic_count, defocus, bfactor, references, arrived
    )
    back = lax.all_to_all(board, ("mic", "bin"), split_axis=0, concat_axis=0, tiled=True)
    refined = last_call(
        capacity, bin_count, defocus, bfactor, references, weight, spectra, middle, labels
    )
    return (refined, jnp.sum(back, axis=(0, 1))[:particles])


def solution(mesh):
    in_specs = (
        P(("mic", "bin"), None, None),
        P(None, ("mic", "bin")),
        P(("mic", "bin")),
        P(("mic", "bin")),
        P(),
        P(),
        P(),
        P(("mic", "bin"), None, None),
    )
    out_specs = (P(("mic", "bin"), None, None), P(("mic", "bin")))
    return jax.shard_map(body, mesh=mesh, in_specs=in_specs, out_specs=out_specs, check_vma=False)
```

```python
import functools
import math

import jax
import jax.numpy as jnp
import numpy as np
from jax import lax
from jax.experimental import pallas as pl
from jax.experimental.pallas import tpu as pltpu
from jax.sharding import PartitionSpec as P

ITERS = 2
PRIOR_WEIGHT = 0.5
EPSILON = 1e-06
CONTRAST = 0.1
AMPLITUDE = math.sqrt(1.0 - CONTRAST * CONTRAST)

LANES = 128
LABEL_ROWS = 8
CHUNK = 32
VMEM_BYTES = 24 * 1024 * 1024

ACTIVE, PLACE, ALONE, HOME, PARTICLE, MEMBERS, LATE = range(7)
INFOS = 7

F32 = jnp.float32
BF16 = jnp.bfloat16
VMEM = pl.BlockSpec(memory_space=pltpu.VMEM)
SMEM = pl.BlockSpec(memory_space=pltpu.SMEM)
HBM = pl.BlockSpec(memory_space=pltpu.HBM)
ANY = pl.BlockSpec(memory_space=pl.ANY)


def in_hbm(x):
    return pltpu.with_memory_space_constraint(x, pltpu.HBM)


def hartley(side):
    index = np.arange(side)
    angles = (np.outer(index, index) % side).astype(np.float32) * np.float32(2.0 * math.pi / side)
    return (np.cos(angles) + np.sin(angles)) / np.float32(math.sqrt(side))


def label_block(values):
    row = lax.broadcasted_iota(jnp.int32, (LABEL_ROWS, LANES), 0)
    block = jnp.zeros((LABEL_ROWS, LANES), jnp.int32)
    for number, value in enumerate(values):
        block = jnp.where(row == number, value, block)
    return block.astype(F32).astype(BF16)


def home_kernel(
    bin_count, own_bins, first, count, place_hbm, bin_hbm, group_hbm, offset_hbm, image_hbm, basis_hbm, *rest
):
    rest = rest[len(rest) - count - 9 :]
    outs, rest = rest[:count], rest[count:]
    spectra, image_ref, basis_ref, place_ref, bin_ref, group_ref, offset_ref, image_sem, sem = rest
    particles, side = image_ref.shape[0], image_ref.shape[1]
    here = lax.axis_index("bin")
    pairs = (
        (basis_hbm, basis_ref),
        (place_hbm, place_ref),
        (bin_hbm, bin_ref),
        (group_hbm, group_ref),
        (offset_hbm, offset_ref),
    )
    copies = [pltpu.make_async_copy(a, b, sem.at[k]) for k, (a, b) in enumerate(pairs)]
    for copy in copies:
        copy.start()

    def image_copy(i):
        return pltpu.make_async_copy(image_hbm.at[i], image_ref.at[i], image_sem.at[i])

    for i in range(particles):
        image_copy(i).start()
    pieces = side // LANES
    for out in outs:
        out[pieces * side :, :] = jnp.zeros((LABEL_ROWS, LANES), BF16)
    for copy in copies:
        copy.wait()

    @pl.loop(0, particles)
    def _(i):
        image_copy(i).wait()
        place = place_ref[bin_ref[i]]
        owner = place // own_bins
        step_of = lax.rem(owner, bin_count) ^ here

        @pl.when((step_of >= first) & (step_of < first + count))
        def _():
            moved = pltpu.roll(image_ref[i].astype(F32), side - offset_ref[0, i], 0).astype(BF16)
            columns = pltpu.roll(basis_ref[...].astype(F32), offset_ref[1, i], 0).astype(BF16)
            half = jnp.dot(basis_ref[...], moved, preferred_element_type=F32).astype(BF16)
            spectra[...] = jnp.dot(half, columns, preferred_element_type=F32).astype(BF16)
            labels = label_block(
                (
                    1 + owner // bin_count,
                    lax.rem(place, own_bins),
                    group_ref[i],
                    i * bin_count + here,
                )
            )
            for k in range(count):

                @pl.when(step_of == first + k)
                def _():
                    for n in range(pieces):
                        outs[k][n * side : (n + 1) * side, :] = spectra[
                            :, n * LANES : (n + 1) * LANES
                        ]
                    outs[k][pieces * side :, :] = labels


def home_call(bin_count, own_bins, first, count, operands, after=()):
    images, particles, side = operands[4], operands[4].shape[0], operands[4].shape[1]
    return pl.pallas_call(
        functools.partial(home_kernel, bin_count, own_bins, first, count),
        out_shape=[
            jax.ShapeDtypeStruct((side * side // LANES + LABEL_ROWS, LANES), BF16)
        ]
        * count,
        in_specs=[HBM] * 6 + [ANY] * len(after),
        out_specs=[VMEM] * count,
        scratch_shapes=[
            pltpu.VMEM((side, side), BF16),
            pltpu.VMEM(images.shape, BF16),
            pltpu.VMEM((side, side), BF16),
        ]
        + [pltpu.SMEM(x.shape, jnp.int32) for x in operands[:4]]
        + [pltpu.SemaphoreType.DMA((particles,)), pltpu.SemaphoreType.DMA((5,))],
        compiler_params=pltpu.CompilerParams(vmem_limit_bytes=VMEM_BYTES),
        name="home",
    )(*operands, *after)


def middle_kernel(mic_count, capacity, *rest):
    arrived, outs = rest[: len(rest) - mic_count], rest[len(rest) - mic_count :]
    rows = arrived[0].shape[0]
    here = lax.axis_index("mic")
    empty = jnp.zeros((LABEL_ROWS, LANES), BF16)
    for out in outs:
        for j in range(capacity):
            out[j, rows - LABEL_ROWS : rows, :] = empty
    targets = [
        jnp.max(block[rows - LABEL_ROWS : rows, :].astype(F32)[0:1]).astype(jnp.int32)
        for block in arrived
    ]
    counts = [jnp.int32(0)] * mic_count
    for block, target in zip(arrived, targets):
        step_of = (target - 1) ^ here
        for step in range(mic_count):
            chosen = (target > 0) & (step_of == step)

            @pl.when(chosen)
            def _(block=block, step=step, slot=counts[step]):
                outs[step][slot] = block[...]

            counts[step] = counts[step] + chosen.astype(jnp.int32)


def middle_call(mic_count, capacity, arrived):
    return pl.pallas_call(
        functools.partial(middle_kernel, mic_count, capacity),
        out_shape=[jax.ShapeDtypeStruct((capacity, *arrived[0].shape), BF16)] * mic_count,
        in_specs=[VMEM] * len(arrived),
        out_specs=[VMEM] * mic_count,
        compiler_params=pltpu.CompilerParams(vmem_limit_bytes=VMEM_BYTES),
        name="middle",
    )(*arrived)


def fold(values):
    return jnp.sum(values.reshape(values.shape[0] // 8, 8, values.shape[1]), axis=0)


def chunks_of(side):
    return [slice(c, c + CHUNK) for c in range(0, side, CHUNK)]


def shares(ctf, weight, s, rows, values):
    table = ctf[s, rows, :]
    scaled = weight * table
    return (scaled * values).astype(BF16).astype(F32), scaled * table, table


def renew(previous, numerator, denominator):
    return (
        (numerator + PRIOR_WEIGHT * previous.astype(F32)) / (denominator + PRIOR_WEIGHT)
    ).astype(BF16)


def update_shared(info, groups, weight, number, source, target, kind=MEMBERS):
    chunks = chunks_of(source.shape[1])

    @pl.loop(0, source.shape[0])
    def _(p):
        @pl.when((info[MEMBERS, p] > 1) & (info[kind, p] > 0))
        def _():
            number[...] = jnp.zeros(number.shape, F32)
            for ctf, spectra, first in groups:

                @pl.loop(0, spectra.shape[0])
                def _(k):
                    @pl.when((info[ACTIVE, first + k] > 0) & (info[PLACE, first + k] == p))
                    def _():
                        scale = weight[pl.ds(first + k, 1), :]
                        for rows in chunks:
                            values = spectra[k, rows, :].astype(F32)
                            term, power, _ = shares(ctf, scale, k, rows, values)
                            number[0, rows, :] += term
                            number[1, rows, :] += power

            for rows in chunks:
                target[p, rows, :] = renew(
                    source[p, rows, :], number[0, rows, :], number[1, rows, :]
                )


def decode(labels, steps, bin_count, own_bins, info, late=0):
    slots = len(labels)
    capacity = slots // len(steps)
    here = lax.axis_index("mic")
    codes = []
    for block in labels:
        code = block[1:2] + 256.0 * block[3:4]
        codes.append(jnp.max(jnp.where(block[0:1] > 0, code, -1.0)).astype(jnp.int32))
    for p in range(own_bins):
        info[MEMBERS, p] = jnp.int32(0)
        info[LATE, p] = jnp.int32(0)
    for s in range(slots):
        active = (codes[s] >= 0).astype(jnp.int32)
        code = jnp.maximum(codes[s], 0)
        sender = code >> 8
        place = code & 255
        info[ACTIVE, s] = active
        info[PLACE, s] = place
        info[HOME, s] = (here ^ steps[s // capacity]) * bin_count + lax.rem(sender, bin_count)
        info[PARTICLE, s] = sender // bin_count
        info[MEMBERS, place] = info[MEMBERS, place] + active
        if s >= slots - late * capacity:
            info[LATE, place] = info[LATE, place] + active
    for s in range(slots):
        single = (info[ACTIVE, s] > 0) & (info[MEMBERS, info[PLACE, s]] == 1)
        info[ALONE, s] = single.astype(jnp.int32)


def ctf_factors(labels, focus_ref, damping_ref, side):
    groups = focus_ref.shape[1]
    group = jnp.concatenate([x[2:3, :groups] for x in labels] + [labels[0][4:5, :groups]] * 8)[:8]
    chosen = group.astype(jnp.int32) == lax.broadcasted_iota(jnp.int32, (8, groups), 1)
    focus = jnp.sum(jnp.where(chosen, focus_ref[...], 0.0), axis=1, keepdims=True)
    damping = jnp.sum(jnp.where(chosen, damping_ref[...], 0.0), axis=1, keepdims=True)
    frequency = lax.broadcasted_iota(jnp.int32, (8, side), 1)
    folded = jnp.minimum(frequency, side - frequency).astype(F32) / (side / 2.0)
    square = folded * folded
    envelope = jnp.exp(-damping * square)
    sine = jnp.sin(focus * square) * envelope
    cosine = jnp.cos(focus * square) * envelope
    by_sine = jnp.transpose(CONTRAST * sine - AMPLITUDE * cosine)
    by_cosine = jnp.transpose(-(AMPLITUDE * sine + CONTRAST * cosine))
    return by_sine, sine, by_cosine, cosine


def ctf_chunk(factors, s, rows):
    by_sine, sine, by_cosine, cosine = factors
    return (
        by_sine[rows, s : s + 1] * sine[s : s + 1, :]
        + by_cosine[rows, s : s + 1] * cosine[s : s + 1, :]
    )


def labels_of(arrived):
    return [
        block[j, block.shape[1] - LABEL_ROWS :, :].astype(F32)
        for block in arrived
        for j in range(block.shape[0])
    ]


def first_compare(info, factors, current_ref, group, sums, s, block):
    ctf, spectra, first = group
    side = ctf.shape[1]
    p = info[PLACE, s]
    cross = model = data = jnp.zeros((8, side), F32)
    for rows in chunks_of(side):
        table = ctf_chunk(factors, s, rows)
        ctf[s - first, rows, :] = table
        held = jnp.concatenate(
            [block[n + rows.start : n + rows.stop, :] for n in range(0, side * side // LANES, side)],
            axis=1,
        )
        spectra[s - first, rows, :] = held
        values = held.astype(F32)
        predicted = table * current_ref[p, rows, :].astype(F32)
        cross = cross + fold(predicted * values)
        model = model + fold(predicted * predicted)
        data = data + fold(values * values)
    for k, total in enumerate((cross, model, data)):
        sums[k, s : s + 1, :] = jnp.sum(total, axis=0, keepdims=True)


def correlate(sums, side):
    pixels = float(side * side)
    cross, model, data = (jnp.sum(sums[k], axis=1, keepdims=True) / pixels for k in range(3))
    correlation = cross / jnp.sqrt((model + EPSILON) * (data + EPSILON))
    weights = 1.0 / (1.0 + jnp.exp(-float(side) * correlation))
    return correlation, jnp.broadcast_to(weights.astype(BF16).astype(F32), (8, side))


def second_compare(group, k, reference_of):
    ctf, spectra, _ = group
    side = ctf.shape[1]
    cross = model = jnp.zeros((8, side), F32)
    for rows in chunks_of(side):
        values = spectra[k, rows, :].astype(F32)
        reference = reference_of(rows, values)
        predicted = ctf[k, rows, :] * reference.astype(F32)
        cross = cross + fold(predicted * values)
        model = model + fold(predicted * predicted)
    return cross, model


def update_and_compare(info, group, weight, sums, source, target):
    ctf, spectra, first = group

    @pl.loop(0, spectra.shape[0])
    def _(k):
        s = first + k
        p = info[PLACE, s]

        def keep(cross, model):
            sums[0, pl.ds(s, 1), :] = jnp.sum(cross, axis=0, keepdims=True)
            sums[1, pl.ds(s, 1), :] = jnp.sum(model, axis=0, keepdims=True)

        @pl.when(info[ALONE, s] > 0)
        def _():
            scale = weight[pl.ds(s, 1), :]

            def new(rows, values):
                term, power, _ = shares(ctf, scale, k, rows, values)
                reference = renew(source[p, rows, :], term, power)
                target[p, rows, :] = reference
                return reference

            keep(*second_compare(group, k, new))

        @pl.when((info[ACTIVE, s] > 0) & (info[ALONE, s] == 0))
        def _():
            keep(*second_compare(group, k, lambda rows, _: target[p, rows, :]))


def ready_kernel(bin_count, steps, focus_ref, damping_ref, current_ref, *rest):
    arrived, rest = rest[: len(steps)], rest[len(steps) :]
    ctf, spectra, spectra_hbm, weight, middle, sums, number, info, sem = rest
    own_bins, side, _ = current_ref.shape
    labels = labels_of(arrived)
    decode(labels, steps, bin_count, own_bins, info)
    factors = ctf_factors(labels, focus_ref, damping_ref, side)
    sums[...] = jnp.zeros(sums.shape, F32)
    group = (ctf, spectra, 0)
    for s in range(len(labels)):

        @pl.when(info[ACTIVE, s] > 0)
        def _(s=s):
            capacity = len(labels) // len(steps)
            block = arrived[s // capacity].at[s % capacity]
            first_compare(info, factors, current_ref, group, sums, s, block)

    copy = pltpu.make_async_copy(spectra, spectra_hbm, sem)
    copy.start()
    weight[...] = correlate(sums, side)[1]
    update_shared(info, (group,), weight, number, current_ref, middle)
    update_and_compare(info, group, weight, sums, current_ref, middle)
    copy.wait()


def ready_call(bin_count, steps, defocus, bfactor, references, arrived):
    own_bins, side, _ = references.shape
    slots = len(steps) * arrived[0].shape[0]
    return pl.pallas_call(
        functools.partial(ready_kernel, bin_count, steps),
        out_shape=[
            jax.ShapeDtypeStruct((slots, side, side), F32),
            jax.ShapeDtypeStruct((slots, side, side), BF16),
            pltpu.HBM((slots, side, side), BF16),
            jax.ShapeDtypeStruct((8, side), F32),
            jax.ShapeDtypeStruct(references.shape, BF16),
            jax.ShapeDtypeStruct((3, 8, side), F32),
        ],
        in_specs=[VMEM] * (3 + len(steps)),
        out_specs=[VMEM, VMEM, HBM, VMEM, VMEM, VMEM],
        scratch_shapes=[
            pltpu.VMEM((2, side, side), F32),
            pltpu.SMEM((INFOS, max(8, own_bins)), jnp.int32),
            pltpu.SemaphoreType.DMA(()),
        ],
        compiler_params=pltpu.CompilerParams(vmem_limit_bytes=VMEM_BYTES),
        name="ready",
    )(defocus, bfactor, references, *arrived)


def owner_kernel(bin_count, steps, focus_ref, damping_ref, current_ref, *rest):
    arrived, rest = rest[: len(steps)], rest[len(steps) :]
    early_ctf, early_spectra, early_weight, early_middle, early_sums = rest[:5]
    spectra_hbm, middle_hbm, weight, label_ref, score_ref = rest[5:10]
    ctf, spectra, middle, sums, number, info, spectra_sem, middle_sem = rest[10:]
    own_bins, side, _ = current_ref.shape
    capacity = arrived[0].shape[0]
    early = early_ctf.shape[0]
    late = len(steps) - early // capacity
    late_block = arrived[-1]

    spectra_copy = pltpu.make_async_copy(spectra, spectra_hbm, spectra_sem)
    labels = labels_of(arrived)
    for s, label in enumerate(labels):
        label_ref[s] = label
    decode(labels, steps, bin_count, own_bins, info, late)

    def early_copy(p):
        return pltpu.make_async_copy(early_middle.at[p], middle_hbm.at[p], middle_sem.at[p])

    def late_copy(p):
        return pltpu.make_async_copy(middle.at[p], middle_hbm.at[p], middle_sem.at[p])

    @pl.loop(0, own_bins)
    def _(p):
        @pl.when((info[MEMBERS, p] > 0) & (info[LATE, p] == 0))
        def _():
            early_copy(p).start()

    factors = ctf_factors(labels, focus_ref, damping_ref, side)
    sums[...] = early_sums[...]
    early_group, late_group = (early_ctf, early_spectra, 0), (ctf, spectra, early)
    for s in range(early, len(labels)):

        @pl.when(info[ACTIVE, s] > 0)
        def _(s=s):
            block = late_block.at[s - early]
            first_compare(info, factors, current_ref, late_group, sums, s, block)

    spectra_copy.start()
    row = lax.broadcasted_iota(jnp.int32, (8, side), 0)
    weight[...] = jnp.where(row < early, early_weight[...], correlate(sums, side)[1])
    update_shared(
        info, (early_group, late_group), weight, number, current_ref, middle, kind=LATE
    )
    update_and_compare(info, late_group, weight, sums, current_ref, middle)

    @pl.loop(0, early)
    def _(s):
        p = info[PLACE, s]

        @pl.when((info[ACTIVE, s] > 0) & (info[LATE, p] > 0))
        def _():
            cross, model = second_compare(early_group, s, lambda rows, _: middle[p, rows, :])
            sums[0, pl.ds(s, 1), :] = jnp.sum(cross, axis=0, keepdims=True)
            sums[1, pl.ds(s, 1), :] = jnp.sum(model, axis=0, keepdims=True)

    @pl.loop(0, own_bins)
    def _(p):
        @pl.when(info[LATE, p] > 0)
        def _():
            late_copy(p).start()

    correlation, weight[...] = correlate(sums, side)
    score_ref[...] = jnp.zeros(score_ref.shape, F32)
    lane = lax.broadcasted_iota(jnp.int32, (1, 128), 1)
    for s in range(len(labels)):

        @pl.when(info[ACTIVE, s] > 0)
        def _(s=s):
            score = jnp.where(lane == info[PARTICLE, s], correlation[s : s + 1, :], 0.0)
            score_ref[info[HOME, s]] = score

    spectra_copy.wait()

    @pl.loop(0, own_bins)
    def _(p):
        @pl.when(info[MEMBERS, p] > 0)
        def _():
            late_copy(p).wait()


def owner_call(bin_count, steps, defocus, bfactor, references, arrived, early):
    own_bins, side, _ = references.shape
    capacity = arrived[0].shape[0]
    slots = len(steps) * capacity
    late = slots - early[0].shape[0]
    return pl.pallas_call(
        functools.partial(owner_kernel, bin_count, steps),
        out_shape=[
            pltpu.HBM((late, side, side), BF16),
            pltpu.HBM(references.shape, BF16),
            jax.ShapeDtypeStruct((8, side), F32),
            jax.ShapeDtypeStruct((slots, LABEL_ROWS, 128), F32),
            jax.ShapeDtypeStruct((len(steps) * bin_count, 1, 128), F32),
        ],
        in_specs=[VMEM] * (3 + len(steps) + len(early)),
        out_specs=[HBM, HBM, VMEM, VMEM, VMEM],
        scratch_shapes=[
            pltpu.VMEM((late, side, side), F32),
            pltpu.VMEM((late, side, side), BF16),
            pltpu.VMEM(references.shape, BF16),
            pltpu.VMEM((3, 8, side), F32),
            pltpu.VMEM((2, side, side), F32),
            pltpu.SMEM((INFOS, max(8, own_bins)), jnp.int32),
            pltpu.SemaphoreType.DMA(()),
            pltpu.SemaphoreType.DMA((own_bins,)),
        ],
        compiler_params=pltpu.CompilerParams(vmem_limit_bytes=VMEM_BYTES),
        name="owner",
    )(defocus, bfactor, references, *arrived, *early)


def last_kernel(
    bin_count,
    steps,
    focus_ref,
    damping_ref,
    current_ref,
    weight,
    label_ref,
    early_hbm,
    late_hbm,
    middle_hbm,
    refined_ref,
    spectra,
    middle,
    ctf,
    number,
    info,
    sem,
):
    slots, side, _ = ctf.shape
    own_bins = current_ref.shape[0]
    early = early_hbm.shape[0]
    copies = [
        pltpu.make_async_copy(early_hbm, spectra.at[pl.ds(0, early)], sem.at[0]),
        pltpu.make_async_copy(late_hbm, spectra.at[pl.ds(early, slots - early)], sem.at[1]),
        pltpu.make_async_copy(middle_hbm, middle, sem.at[2]),
    ]
    for copy in copies:
        copy.start()
    labels = [label_ref[s] for s in range(slots)]
    decode(labels, steps, bin_count, own_bins, info)
    factors = ctf_factors(labels, focus_ref, damping_ref, side)
    for s in range(slots):

        @pl.when(info[ACTIVE, s] > 0)
        def _(s=s):
            for rows in chunks_of(side):
                ctf[s, rows, :] = ctf_chunk(factors, s, rows)

    for copy in copies:
        copy.wait()
    update_shared(info, ((ctf, spectra, 0),), weight, number, middle, refined_ref)

    @pl.loop(0, slots)
    def _(s):
        @pl.when(info[ALONE, s] > 0)
        def _():
            p = info[PLACE, s]
            scale = weight[pl.ds(s, 1), :]
            for rows in chunks_of(side):
                values = spectra[s, rows, :].astype(F32)
                term, power, _ = shares(ctf, scale, s, rows, values)
                refined_ref[p, rows, :] = renew(middle[p, rows, :], term, power)

    @pl.loop(0, own_bins)
    def _(p):
        @pl.when(info[MEMBERS, p] == 0)
        def _():
            refined_ref[p] = current_ref[p]


def last_call(bin_count, steps, defocus, bfactor, references, weight, labels, kept):
    own_bins, side, _ = references.shape
    slots = labels.shape[0]
    return pl.pallas_call(
        functools.partial(last_kernel, bin_count, steps),
        out_shape=jax.ShapeDtypeStruct(references.shape, BF16),
        in_specs=[VMEM] * 5 + [HBM] * 3,
        out_specs=VMEM,
        scratch_shapes=[
            pltpu.VMEM((slots, side, side), BF16),
            pltpu.VMEM(references.shape, BF16),
            pltpu.VMEM((slots, side, side), F32),
            pltpu.VMEM((2, side, side), F32),
            pltpu.SMEM((INFOS, max(8, own_bins)), jnp.int32),
            pltpu.SemaphoreType.DMA((3,)),
        ],
        compiler_params=pltpu.CompilerParams(vmem_limit_bytes=VMEM_BYTES),
        cost_estimate=pl.CostEstimate(flops=4 << 20, bytes_accessed=4 << 20, transcendentals=0),
        name="last",
    )(defocus, bfactor, references, weight, labels, *map(in_hbm, kept))


def exchange(blocks, axis):
    size = lax.axis_size(axis)
    return [blocks[0]] + [
        lax.ppermute(blocks[k], axis, [(i, i ^ k) for i in range(size)]) for k in range(1, size)
    ]


def body(images, offsets, ctf_group, particle_bin, bin_place, defocus, bfactor, references):
    mic_count = lax.axis_size("mic")
    bin_count = lax.axis_size("bin")
    particles, side, _ = images.shape
    own_bins = references.shape[0]
    capacity = (3 * particles + 2 * mic_count - 1) // (2 * mic_count)

    basis = jnp.asarray(hartley(side), BF16)
    operands = (bin_place, particle_bin, ctf_group, offsets, images, basis)
    operands = tuple(map(in_hbm, operands))
    far = max(1, bin_count // 4)
    rest = bin_count - far
    sent_far = home_call(bin_count, own_bins, rest, far, operands)
    sent_near = home_call(bin_count, own_bins, 0, rest, operands, after=(sent_far[-1],))
    arrived = exchange(list(sent_near) + list(sent_far), "bin")

    sent = middle_call(mic_count, capacity, arrived[::-1])
    arrived = exchange(sent, "mic")
    steps = [t for t in range(mic_count) if t != mic_count // 2] + [mic_count // 2]
    arrived = [arrived[t] for t in steps]
    tables = (defocus.reshape(1, -1), bfactor.reshape(1, -1), references)
    ctf, spectra, kept, *known = ready_call(bin_count, steps[:-1], *tables, arrived[:-1])
    late, middle, weight, labels, board = owner_call(
        bin_count, steps, *tables, arrived, (ctf, spectra, *known)
    )
    back = lax.all_to_all(board, ("mic", "bin"), split_axis=0, concat_axis=0, tiled=True)
    refined = last_call(bin_count, steps, *tables, weight, labels, (kept, late, middle))
    return (refined, jnp.sum(back, axis=(0, 1))[:particles])


def solution(mesh):
    in_specs = (
        P(("mic", "bin"), None, None),
        P(None, ("mic", "bin")),
        P(("mic", "bin")),
        P(("mic", "bin")),
        P(),
        P(),
        P(),
        P(("mic", "bin"), None, None),
    )
    out_specs = (P(("mic", "bin"), None, None), P(("mic", "bin")))
    return jax.shard_map(body, mesh=mesh, in_specs=in_specs, out_specs=out_specs, check_vma=False)
```

```python
import functools
import math

import jax
import jax.numpy as jnp
import numpy as np
from jax import lax
from jax.experimental import pallas as pl
from jax.experimental.pallas import tpu as pltpu
from jax.sharding import PartitionSpec as P

ITERS = 2
PRIOR_WEIGHT = 0.5
EPSILON = 1e-06
CONTRAST = 0.1
AMPLITUDE = math.sqrt(1.0 - CONTRAST * CONTRAST)

LANES = 128
LABEL_ROWS = 8
CHUNK = 32
VMEM_BYTES = 24 * 1024 * 1024

ACTIVE, PLACE, ALONE, HOME, PARTICLE, MEMBERS, LATE = range(7)
INFOS = 7

F32 = jnp.float32
BF16 = jnp.bfloat16
VMEM = pl.BlockSpec(memory_space=pltpu.VMEM)
SMEM = pl.BlockSpec(memory_space=pltpu.SMEM)
HBM = pl.BlockSpec(memory_space=pltpu.HBM)
ANY = pl.BlockSpec(memory_space=pl.ANY)


def in_hbm(x):
    return pltpu.with_memory_space_constraint(x, pltpu.HBM)


def hartley(side):
    index = np.arange(side)
    angles = (np.outer(index, index) % side).astype(np.float32) * np.float32(2.0 * math.pi / side)
    return (np.cos(angles) + np.sin(angles)) / np.float32(math.sqrt(side))


def label_block(values):
    row = lax.broadcasted_iota(jnp.int32, (LABEL_ROWS, LANES), 0)
    block = jnp.zeros((LABEL_ROWS, LANES), jnp.int32)
    for number, value in enumerate(values):
        block = jnp.where(row == number, value, block)
    return block.astype(F32).astype(BF16)


def home_kernel(
    bin_count, own_bins, first, count, place_hbm, bin_hbm, group_hbm, offset_hbm, image_hbm, basis_hbm, *rest
):
    rest = rest[len(rest) - count - 9 :]
    outs, rest = rest[:count], rest[count:]
    spectra, image_ref, basis_ref, place_ref, bin_ref, group_ref, offset_ref, image_sem, sem = rest
    particles, side = image_ref.shape[0], image_ref.shape[1]
    here = lax.axis_index("bin")
    pairs = (
        (basis_hbm, basis_ref),
        (place_hbm, place_ref),
        (bin_hbm, bin_ref),
        (group_hbm, group_ref),
        (offset_hbm, offset_ref),
    )
    copies = [pltpu.make_async_copy(a, b, sem.at[k]) for k, (a, b) in enumerate(pairs)]
    for copy in copies:
        copy.start()

    def image_copy(i):
        return pltpu.make_async_copy(image_hbm.at[i], image_ref.at[i], image_sem.at[i])

    for i in range(particles):
        image_copy(i).start()
    pieces = side // LANES
    for out in outs:
        out[pieces * side :, :] = jnp.zeros((LABEL_ROWS, LANES), BF16)
    for copy in copies:
        copy.wait()

    @pl.loop(0, particles)
    def _(i):
        image_copy(i).wait()
        place = place_ref[bin_ref[i]]
        owner = place // own_bins
        step_of = lax.rem(owner, bin_count) ^ here

        @pl.when((step_of >= first) & (step_of < first + count))
        def _():
            moved = pltpu.roll(image_ref[i].astype(F32), side - offset_ref[0, i], 0).astype(BF16)
            columns = pltpu.roll(basis_ref[...].astype(F32), offset_ref[1, i], 0).astype(BF16)
            half = jnp.dot(basis_ref[...], moved, preferred_element_type=F32).astype(BF16)
            spectra[...] = jnp.dot(half, columns, preferred_element_type=F32).astype(BF16)
            labels = label_block(
                (
                    1 + owner // bin_count,
                    lax.rem(place, own_bins),
                    group_ref[i],
                    i * bin_count + here,
                )
            )
            for k in range(count):

                @pl.when(step_of == first + k)
                def _():
                    for n in range(pieces):
                        outs[k][n * side : (n + 1) * side, :] = spectra[
                            :, n * LANES : (n + 1) * LANES
                        ]
                    outs[k][pieces * side :, :] = labels


def home_call(bin_count, own_bins, first, count, operands, after=()):
    images, particles, side = operands[4], operands[4].shape[0], operands[4].shape[1]
    return pl.pallas_call(
        functools.partial(home_kernel, bin_count, own_bins, first, count),
        out_shape=[
            jax.ShapeDtypeStruct((side * side // LANES + LABEL_ROWS, LANES), BF16)
        ]
        * count,
        in_specs=[HBM] * 6 + [ANY] * len(after),
        out_specs=[VMEM] * count,
        scratch_shapes=[
            pltpu.VMEM((side, side), BF16),
            pltpu.VMEM(images.shape, BF16),
            pltpu.VMEM((side, side), BF16),
        ]
        + [pltpu.SMEM(x.shape, jnp.int32) for x in operands[:4]]
        + [pltpu.SemaphoreType.DMA((particles,)), pltpu.SemaphoreType.DMA((5,))],
        compiler_params=pltpu.CompilerParams(vmem_limit_bytes=VMEM_BYTES),
        name="home",
    )(*operands, *after)


def middle_kernel(mic_count, sizes, *rest):
    arrived, flat = rest[: len(rest) - sum(map(len, sizes))], list(rest[-sum(map(len, sizes)) :])
    outs = [[flat.pop(0) for _ in parts] for parts in sizes]
    rows = arrived[0].shape[0]
    here = lax.axis_index("mic")
    empty = jnp.zeros((LABEL_ROWS, LANES), BF16)
    for out in sum(outs, []):
        for j in range(out.shape[0]):
            out[j, rows - LABEL_ROWS : rows, :] = empty
    targets = [
        jnp.max(block[rows - LABEL_ROWS : rows, :].astype(F32)[0:1]).astype(jnp.int32)
        for block in arrived
    ]
    counts = [jnp.int32(0)] * mic_count
    for block, target in zip(arrived, targets):
        step_of = (target - 1) ^ here
        for step in range(mic_count):
            chosen = (target > 0) & (step_of == step)
            if len(outs[step]) == 1:

                @pl.when(chosen)
                def _(block=block, out=outs[step][0], slot=counts[step]):
                    out[slot] = block[...]

            else:
                for j, out in enumerate(outs[step]):

                    @pl.when(chosen & (counts[step] == j))
                    def _(block=block, out=out):
                        out[0] = block[...]

            counts[step] = counts[step] + chosen.astype(jnp.int32)


def middle_call(mic_count, sizes, arrived):
    flat = sum(sizes, [])
    outs = pl.pallas_call(
        functools.partial(middle_kernel, mic_count, sizes),
        out_shape=[jax.ShapeDtypeStruct((n, *arrived[0].shape), BF16) for n in flat],
        in_specs=[VMEM] * len(arrived),
        out_specs=[VMEM] * len(flat),
        compiler_params=pltpu.CompilerParams(vmem_limit_bytes=VMEM_BYTES),
        name="middle",
    )(*arrived)
    outs = list(outs)
    return [[outs.pop(0) for _ in parts] for parts in sizes]


def fold(values):
    return jnp.sum(values.reshape(values.shape[0] // 8, 8, values.shape[1]), axis=0)


def chunks_of(side):
    return [slice(c, c + CHUNK) for c in range(0, side, CHUNK)]


def shares(ctf, weight, s, rows, values):
    table = ctf[s, rows, :]
    scaled = weight * table
    return (scaled * values).astype(BF16).astype(F32), scaled * table, table


def renew(previous, numerator, denominator):
    return (
        (numerator + PRIOR_WEIGHT * previous.astype(F32)) / (denominator + PRIOR_WEIGHT)
    ).astype(BF16)


def update_shared(info, groups, weight, number, source, target, kind=MEMBERS):
    chunks = chunks_of(source.shape[1])

    @pl.loop(0, source.shape[0])
    def _(p):
        @pl.when((info[MEMBERS, p] > 1) & (info[kind, p] > 0))
        def _():
            number[...] = jnp.zeros(number.shape, F32)
            for ctf, spectra, first in groups:

                @pl.loop(0, spectra.shape[0])
                def _(k):
                    @pl.when((info[ACTIVE, first + k] > 0) & (info[PLACE, first + k] == p))
                    def _():
                        scale = weight[pl.ds(first + k, 1), :]
                        for rows in chunks:
                            values = spectra[k, rows, :].astype(F32)
                            term, power, _ = shares(ctf, scale, k, rows, values)
                            number[0, rows, :] += term
                            number[1, rows, :] += power

            for rows in chunks:
                target[p, rows, :] = renew(
                    source[p, rows, :], number[0, rows, :], number[1, rows, :]
                )


def decode(labels, steps, bin_count, own_bins, info, late=0):
    slots = len(labels)
    here = lax.axis_index("mic")
    codes = []
    for block in labels:
        code = block[1:2] + 256.0 * block[3:4]
        codes.append(jnp.max(jnp.where(block[0:1] > 0, code, -1.0)).astype(jnp.int32))
    for p in range(own_bins):
        info[MEMBERS, p] = jnp.int32(0)
        info[LATE, p] = jnp.int32(0)
    for s in range(slots):
        active = (codes[s] >= 0).astype(jnp.int32)
        code = jnp.maximum(codes[s], 0)
        sender = code >> 8
        place = code & 255
        info[ACTIVE, s] = active
        info[PLACE, s] = place
        info[HOME, s] = (here ^ steps[s]) * bin_count + lax.rem(sender, bin_count)
        info[PARTICLE, s] = sender // bin_count
        info[MEMBERS, place] = info[MEMBERS, place] + active
        if s >= slots - late:
            info[LATE, place] = info[LATE, place] + active
    for s in range(slots):
        single = (info[ACTIVE, s] > 0) & (info[MEMBERS, info[PLACE, s]] == 1)
        info[ALONE, s] = single.astype(jnp.int32)


def ctf_factors(labels, focus_ref, damping_ref, side):
    groups = focus_ref.shape[1]
    group = jnp.concatenate([x[2:3, :groups] for x in labels] + [labels[0][4:5, :groups]] * 8)[:8]
    chosen = group.astype(jnp.int32) == lax.broadcasted_iota(jnp.int32, (8, groups), 1)
    focus = jnp.sum(jnp.where(chosen, focus_ref[...], 0.0), axis=1, keepdims=True)
    damping = jnp.sum(jnp.where(chosen, damping_ref[...], 0.0), axis=1, keepdims=True)
    frequency = lax.broadcasted_iota(jnp.int32, (8, side), 1)
    folded = jnp.minimum(frequency, side - frequency).astype(F32) / (side / 2.0)
    square = folded * folded
    envelope = jnp.exp(-damping * square)
    sine = jnp.sin(focus * square) * envelope
    cosine = jnp.cos(focus * square) * envelope
    by_sine = jnp.transpose(CONTRAST * sine - AMPLITUDE * cosine)
    by_cosine = jnp.transpose(-(AMPLITUDE * sine + CONTRAST * cosine))
    return by_sine, sine, by_cosine, cosine


def ctf_chunk(factors, s, rows):
    by_sine, sine, by_cosine, cosine = factors
    return (
        by_sine[rows, s : s + 1] * sine[s : s + 1, :]
        + by_cosine[rows, s : s + 1] * cosine[s : s + 1, :]
    )


def blocks_of(arrived):
    return [block.at[j] for block in arrived for j in range(block.shape[0])]


def labels_of(blocks):
    return [block[block.shape[0] - LABEL_ROWS :, :].astype(F32) for block in blocks]


def first_compare(info, factors, current_ref, group, sums, s, block):
    ctf, spectra, first = group
    side = ctf.shape[1]
    p = info[PLACE, s]
    cross = model = data = jnp.zeros((8, side), F32)
    for rows in chunks_of(side):
        table = ctf_chunk(factors, s, rows)
        ctf[s - first, rows, :] = table
        held = jnp.concatenate(
            [block[n + rows.start : n + rows.stop, :] for n in range(0, side * side // LANES, side)],
            axis=1,
        )
        spectra[s - first, rows, :] = held
        values = held.astype(F32)
        predicted = table * current_ref[p, rows, :].astype(F32)
        cross = cross + fold(predicted * values)
        model = model + fold(predicted * predicted)
        data = data + fold(values * values)
    for k, total in enumerate((cross, model, data)):
        sums[k, s : s + 1, :] = jnp.sum(total, axis=0, keepdims=True)


def correlate(sums, side):
    pixels = float(side * side)
    cross, model, data = (jnp.sum(sums[k], axis=1, keepdims=True) / pixels for k in range(3))
    correlation = cross / jnp.sqrt((model + EPSILON) * (data + EPSILON))
    weights = 1.0 / (1.0 + jnp.exp(-float(side) * correlation))
    return correlation, jnp.broadcast_to(weights.astype(BF16).astype(F32), (8, side))


def second_compare(group, k, reference_of):
    ctf, spectra, _ = group
    side = ctf.shape[1]
    cross = model = jnp.zeros((8, side), F32)
    for rows in chunks_of(side):
        values = spectra[k, rows, :].astype(F32)
        reference = reference_of(rows, values)
        predicted = ctf[k, rows, :] * reference.astype(F32)
        cross = cross + fold(predicted * values)
        model = model + fold(predicted * predicted)
    return cross, model


def update_and_compare(info, group, weight, sums, source, target):
    ctf, spectra, first = group

    @pl.loop(0, spectra.shape[0])
    def _(k):
        s = first + k
        p = info[PLACE, s]

        def keep(cross, model):
            sums[0, pl.ds(s, 1), :] = jnp.sum(cross, axis=0, keepdims=True)
            sums[1, pl.ds(s, 1), :] = jnp.sum(model, axis=0, keepdims=True)

        @pl.when(info[ALONE, s] > 0)
        def _():
            scale = weight[pl.ds(s, 1), :]

            def new(rows, values):
                term, power, _ = shares(ctf, scale, k, rows, values)
                reference = renew(source[p, rows, :], term, power)
                target[p, rows, :] = reference
                return reference

            keep(*second_compare(group, k, new))

        @pl.when((info[ACTIVE, s] > 0) & (info[ALONE, s] == 0))
        def _():
            keep(*second_compare(group, k, lambda rows, _: target[p, rows, :]))


def ready_kernel(bin_count, steps, focus_ref, damping_ref, current_ref, *rest):
    blocks, rest = blocks_of(rest[:-9]), rest[-9:]
    ctf, spectra, spectra_hbm, weight, middle, sums, number, info, sem = rest
    own_bins, side, _ = current_ref.shape
    labels = labels_of(blocks)
    decode(labels, steps, bin_count, own_bins, info)
    factors = ctf_factors(labels, focus_ref, damping_ref, side)
    sums[...] = jnp.zeros(sums.shape, F32)
    group = (ctf, spectra, 0)
    for s in range(len(labels)):

        @pl.when(info[ACTIVE, s] > 0)
        def _(s=s):
            first_compare(info, factors, current_ref, group, sums, s, blocks[s])

    copy = pltpu.make_async_copy(spectra, spectra_hbm, sem)
    copy.start()
    weight[...] = correlate(sums, side)[1]
    update_shared(info, (group,), weight, number, current_ref, middle)
    update_and_compare(info, group, weight, sums, current_ref, middle)
    copy.wait()


def ready_call(bin_count, steps, defocus, bfactor, references, arrived):
    own_bins, side, _ = references.shape
    slots = len(steps)
    return pl.pallas_call(
        functools.partial(ready_kernel, bin_count, steps),
        out_shape=[
            jax.ShapeDtypeStruct((slots, side, side), F32),
            jax.ShapeDtypeStruct((slots, side, side), BF16),
            pltpu.HBM((slots, side, side), BF16),
            jax.ShapeDtypeStruct((8, side), F32),
            jax.ShapeDtypeStruct(references.shape, BF16),
            jax.ShapeDtypeStruct((3, 8, side), F32),
        ],
        in_specs=[VMEM] * (3 + len(arrived)),
        out_specs=[VMEM, VMEM, HBM, VMEM, VMEM, VMEM],
        scratch_shapes=[
            pltpu.VMEM((2, side, side), F32),
            pltpu.SMEM((INFOS, max(8, own_bins)), jnp.int32),
            pltpu.SemaphoreType.DMA(()),
        ],
        compiler_params=pltpu.CompilerParams(vmem_limit_bytes=VMEM_BYTES),
        name="ready",
    )(defocus, bfactor, references, *arrived)


def owner_kernel(bin_count, steps, focus_ref, damping_ref, current_ref, *rest):
    blocks, rest = blocks_of(rest[:-18]), rest[-18:]
    early_ctf, early_spectra, early_weight, early_middle, early_sums = rest[:5]
    spectra_hbm, middle_hbm, weight, label_ref, score_ref = rest[5:10]
    ctf, spectra, middle, sums, number, info, spectra_sem, middle_sem = rest[10:]
    own_bins, side, _ = current_ref.shape
    early = early_ctf.shape[0]

    spectra_copy = pltpu.make_async_copy(spectra, spectra_hbm, spectra_sem)
    labels = labels_of(blocks)
    for s, label in enumerate(labels):
        label_ref[s] = label
    decode(labels, steps, bin_count, own_bins, info, len(steps) - early)

    def early_copy(p):
        return pltpu.make_async_copy(early_middle.at[p], middle_hbm.at[p], middle_sem.at[p])

    def late_copy(p):
        return pltpu.make_async_copy(middle.at[p], middle_hbm.at[p], middle_sem.at[p])

    @pl.loop(0, own_bins)
    def _(p):
        @pl.when((info[MEMBERS, p] > 0) & (info[LATE, p] == 0))
        def _():
            early_copy(p).start()

    factors = ctf_factors(labels, focus_ref, damping_ref, side)
    sums[...] = early_sums[...]
    early_group, late_group = (early_ctf, early_spectra, 0), (ctf, spectra, early)
    for s in range(early, len(labels)):

        @pl.when(info[ACTIVE, s] > 0)
        def _(s=s):
            first_compare(info, factors, current_ref, late_group, sums, s, blocks[s])

    spectra_copy.start()
    row = lax.broadcasted_iota(jnp.int32, (8, side), 0)
    weight[...] = jnp.where(row < early, early_weight[...], correlate(sums, side)[1])
    update_shared(
        info, (early_group, late_group), weight, number, current_ref, middle, kind=LATE
    )
    update_and_compare(info, late_group, weight, sums, current_ref, middle)

    @pl.loop(0, early)
    def _(s):
        p = info[PLACE, s]

        @pl.when((info[ACTIVE, s] > 0) & (info[LATE, p] > 0))
        def _():
            cross, model = second_compare(early_group, s, lambda rows, _: middle[p, rows, :])
            sums[0, pl.ds(s, 1), :] = jnp.sum(cross, axis=0, keepdims=True)
            sums[1, pl.ds(s, 1), :] = jnp.sum(model, axis=0, keepdims=True)

    @pl.loop(0, own_bins)
    def _(p):
        @pl.when(info[LATE, p] > 0)
        def _():
            late_copy(p).start()

    correlation, weight[...] = correlate(sums, side)
    score_ref[...] = jnp.zeros(score_ref.shape, F32)
    lane = lax.broadcasted_iota(jnp.int32, (1, 128), 1)
    for s in range(len(labels)):

        @pl.when(info[ACTIVE, s] > 0)
        def _(s=s):
            score = jnp.where(lane == info[PARTICLE, s], correlation[s : s + 1, :], 0.0)
            score_ref[info[HOME, s]] = score

    spectra_copy.wait()

    @pl.loop(0, own_bins)
    def _(p):
        @pl.when(info[MEMBERS, p] > 0)
        def _():
            late_copy(p).wait()


def owner_call(devices, bin_count, steps, defocus, bfactor, references, arrived, early):
    own_bins, side, _ = references.shape
    slots = len(steps)
    late = slots - early[0].shape[0]
    return pl.pallas_call(
        functools.partial(owner_kernel, bin_count, steps),
        out_shape=[
            pltpu.HBM((late, side, side), BF16),
            pltpu.HBM(references.shape, BF16),
            jax.ShapeDtypeStruct((8, side), F32),
            jax.ShapeDtypeStruct((slots, LABEL_ROWS, 128), F32),
            jax.ShapeDtypeStruct((devices, 1, 128), F32),
        ],
        in_specs=[VMEM] * (3 + len(arrived) + len(early)),
        out_specs=[HBM, HBM, VMEM, VMEM, VMEM],
        scratch_shapes=[
            pltpu.VMEM((late, side, side), F32),
            pltpu.VMEM((late, side, side), BF16),
            pltpu.VMEM(references.shape, BF16),
            pltpu.VMEM((3, 8, side), F32),
            pltpu.VMEM((2, side, side), F32),
            pltpu.SMEM((INFOS, max(8, own_bins)), jnp.int32),
            pltpu.SemaphoreType.DMA(()),
            pltpu.SemaphoreType.DMA((own_bins,)),
        ],
        compiler_params=pltpu.CompilerParams(vmem_limit_bytes=VMEM_BYTES),
        name="owner",
    )(defocus, bfactor, references, *arrived, *early)


def last_kernel(
    bin_count,
    steps,
    focus_ref,
    damping_ref,
    current_ref,
    weight,
    label_ref,
    early_hbm,
    late_hbm,
    middle_hbm,
    refined_ref,
    spectra,
    middle,
    ctf,
    number,
    info,
    sem,
):
    slots, side, _ = ctf.shape
    own_bins = current_ref.shape[0]
    early = early_hbm.shape[0]
    copies = [
        pltpu.make_async_copy(early_hbm, spectra.at[pl.ds(0, early)], sem.at[0]),
        pltpu.make_async_copy(late_hbm, spectra.at[pl.ds(early, slots - early)], sem.at[1]),
        pltpu.make_async_copy(middle_hbm, middle, sem.at[2]),
    ]
    for copy in copies:
        copy.start()
    labels = [label_ref[s] for s in range(slots)]
    decode(labels, steps, bin_count, own_bins, info)
    factors = ctf_factors(labels, focus_ref, damping_ref, side)
    for s in range(slots):

        @pl.when(info[ACTIVE, s] > 0)
        def _(s=s):
            for rows in chunks_of(side):
                ctf[s, rows, :] = ctf_chunk(factors, s, rows)

    for copy in copies:
        copy.wait()
    update_shared(info, ((ctf, spectra, 0),), weight, number, middle, refined_ref)

    @pl.loop(0, slots)
    def _(s):
        @pl.when(info[ALONE, s] > 0)
        def _():
            p = info[PLACE, s]
            scale = weight[pl.ds(s, 1), :]
            for rows in chunks_of(side):
                values = spectra[s, rows, :].astype(F32)
                term, power, _ = shares(ctf, scale, s, rows, values)
                refined_ref[p, rows, :] = renew(middle[p, rows, :], term, power)

    @pl.loop(0, own_bins)
    def _(p):
        @pl.when(info[MEMBERS, p] == 0)
        def _():
            refined_ref[p] = current_ref[p]


def last_call(bin_count, steps, defocus, bfactor, references, weight, labels, kept):
    own_bins, side, _ = references.shape
    slots = labels.shape[0]
    return pl.pallas_call(
        functools.partial(last_kernel, bin_count, steps),
        out_shape=jax.ShapeDtypeStruct(references.shape, BF16),
        in_specs=[VMEM] * 5 + [HBM] * 3,
        out_specs=VMEM,
        scratch_shapes=[
            pltpu.VMEM((slots, side, side), BF16),
            pltpu.VMEM(references.shape, BF16),
            pltpu.VMEM((slots, side, side), F32),
            pltpu.VMEM((2, side, side), F32),
            pltpu.SMEM((INFOS, max(8, own_bins)), jnp.int32),
            pltpu.SemaphoreType.DMA((3,)),
        ],
        compiler_params=pltpu.CompilerParams(vmem_limit_bytes=VMEM_BYTES),
        cost_estimate=pl.CostEstimate(flops=4 << 20, bytes_accessed=4 << 20, transcendentals=0),
        name="last",
    )(defocus, bfactor, references, weight, labels, *map(in_hbm, kept))


def exchange(blocks, axis):
    size = lax.axis_size(axis)
    return [blocks[0]] + [
        lax.ppermute(blocks[k], axis, [(i, i ^ k) for i in range(size)]) for k in range(1, size)
    ]


def body(images, offsets, ctf_group, particle_bin, bin_place, defocus, bfactor, references):
    mic_count = lax.axis_size("mic")
    bin_count = lax.axis_size("bin")
    particles, side, _ = images.shape
    own_bins = references.shape[0]
    capacity = (3 * particles + 2 * mic_count - 1) // (2 * mic_count)

    basis = jnp.asarray(hartley(side), BF16)
    operands = (bin_place, particle_bin, ctf_group, offsets, images, basis)
    operands = tuple(map(in_hbm, operands))
    far = 3 * bin_count // 8
    rest = bin_count - far
    sent_far = home_call(bin_count, own_bins, rest, far, operands)
    sent_near = home_call(bin_count, own_bins, 0, rest, operands, after=(sent_far[-1],))
    arrived = exchange(list(sent_near) + list(sent_far), "bin")

    last = mic_count - 1
    sizes = [[1] * capacity if step == 1 else [capacity] for step in range(mic_count)]
    sent = middle_call(mic_count, sizes, arrived[::-1])
    blocks = [(0, block) for block in sent[0]]
    for step in [t for t in range(1, mic_count) if t != last] + [last]:
        pairs = [(i, i ^ step) for i in range(mic_count)]
        blocks += [(step, lax.ppermute(block, "mic", pairs)) for block in sent[step]]
    steps = [step for step, block in blocks for _ in range(block.shape[0])]
    arrived = [block for _, block in blocks]
    tables = (defocus.reshape(1, -1), bfactor.reshape(1, -1), references)
    ctf, spectra, kept, *known = ready_call(bin_count, steps[: -arrived[-1].shape[0]], *tables, arrived[:-1])
    late, middle, weight, labels, board = owner_call(
        mic_count * bin_count, bin_count, steps, *tables, arrived, (ctf, spectra, *known)
    )
    back = lax.all_to_all(board, ("mic", "bin"), split_axis=0, concat_axis=0, tiled=True)
    refined = last_call(bin_count, steps, *tables, weight, labels, (kept, late, middle))
    return (refined, jnp.sum(back, axis=(0, 1))[:particles])


def solution(mesh):
    in_specs = (
        P(("mic", "bin"), None, None),
        P(None, ("mic", "bin")),
        P(("mic", "bin")),
        P(("mic", "bin")),
        P(),
        P(),
        P(),
        P(("mic", "bin"), None, None),
    )
    out_specs = (P(("mic", "bin"), None, None), P(("mic", "bin")))
    return jax.shard_map(body, mesh=mesh, in_specs=in_specs, out_specs=out_specs, check_vma=False)
```

```python
import functools
import math

import jax
import jax.numpy as jnp
import numpy as np
from jax import lax
from jax.experimental import pallas as pl
from jax.experimental.pallas import tpu as pltpu
from jax.sharding import PartitionSpec as P

ITERS = 2
PRIOR_WEIGHT = 0.5
EPSILON = 1e-06
CONTRAST = 0.1
AMPLITUDE = math.sqrt(1.0 - CONTRAST * CONTRAST)

LANES = 128
LABEL_ROWS = 8
CHUNK = 32
VMEM_BYTES = 24 * 1024 * 1024

ACTIVE, PLACE, ALONE, MEMBERS, LATE = range(5)
INFOS = 5

F32 = jnp.float32
BF16 = jnp.bfloat16
VMEM = pl.BlockSpec(memory_space=pltpu.VMEM)
SMEM = pl.BlockSpec(memory_space=pltpu.SMEM)
HBM = pl.BlockSpec(memory_space=pltpu.HBM)
ANY = pl.BlockSpec(memory_space=pl.ANY)


def in_hbm(x):
    return pltpu.with_memory_space_constraint(x, pltpu.HBM)


def hartley(side):
    index = np.arange(side)
    angles = (np.outer(index, index) % side).astype(np.float32) * np.float32(2.0 * math.pi / side)
    return (np.cos(angles) + np.sin(angles)) / np.float32(math.sqrt(side))


def label_block(values):
    row = lax.broadcasted_iota(jnp.int32, (LABEL_ROWS, LANES), 0)
    block = jnp.zeros((LABEL_ROWS, LANES), jnp.int32)
    for number, value in enumerate(values):
        block = jnp.where(row == number, value, block)
    return block.astype(F32).astype(BF16)


def home_kernel(
    bin_count, own_bins, first, count, place_hbm, bin_hbm, group_hbm, offset_hbm, image_hbm, basis_hbm, *rest
):
    rest = rest[len(rest) - count - 9 :]
    outs, rest = rest[:count], rest[count:]
    spectra, image_ref, basis_ref, place_ref, bin_ref, group_ref, offset_ref, image_sem, sem = rest
    particles, side = image_ref.shape[0], image_ref.shape[1]
    here = lax.axis_index("bin")
    pairs = (
        (basis_hbm, basis_ref),
        (place_hbm, place_ref),
        (bin_hbm, bin_ref),
        (group_hbm, group_ref),
        (offset_hbm, offset_ref),
    )
    copies = [pltpu.make_async_copy(a, b, sem.at[k]) for k, (a, b) in enumerate(pairs)]
    for copy in copies:
        copy.start()

    def image_copy(i):
        return pltpu.make_async_copy(image_hbm.at[i], image_ref.at[i], image_sem.at[i])

    for i in range(particles):
        image_copy(i).start()
    pieces = side // LANES
    for out in outs:
        out[pieces * side :, :] = jnp.zeros((LABEL_ROWS, LANES), BF16)
    for copy in copies:
        copy.wait()

    @pl.loop(0, particles)
    def _(i):
        image_copy(i).wait()
        place = place_ref[bin_ref[i]]
        owner = place // own_bins
        step_of = lax.rem(owner, bin_count) ^ here

        @pl.when((step_of >= first) & (step_of < first + count))
        def _():
            moved = pltpu.roll(image_ref[i].astype(F32), side - offset_ref[0, i], 0).astype(BF16)
            columns = pltpu.roll(basis_ref[...].astype(F32), offset_ref[1, i], 0).astype(BF16)
            half = jnp.dot(basis_ref[...], moved, preferred_element_type=F32).astype(BF16)
            spectra[...] = jnp.dot(half, columns, preferred_element_type=F32).astype(BF16)
            labels = label_block(
                (
                    1 + owner // bin_count,
                    lax.rem(place, own_bins),
                    group_ref[i],
                    i * bin_count + here,
                )
            )
            for k in range(count):

                @pl.when(step_of == first + k)
                def _():
                    for n in range(pieces):
                        outs[k][n * side : (n + 1) * side, :] = spectra[
                            :, n * LANES : (n + 1) * LANES
                        ]
                    outs[k][pieces * side :, :] = labels


def home_call(bin_count, own_bins, first, count, operands, after=()):
    images, particles, side = operands[4], operands[4].shape[0], operands[4].shape[1]
    return pl.pallas_call(
        functools.partial(home_kernel, bin_count, own_bins, first, count),
        out_shape=[
            jax.ShapeDtypeStruct((side * side // LANES + LABEL_ROWS, LANES), BF16)
        ]
        * count,
        in_specs=[HBM] * 6 + [ANY] * len(after),
        out_specs=[VMEM] * count,
        scratch_shapes=[
            pltpu.VMEM((side, side), BF16),
            pltpu.VMEM(images.shape, BF16),
            pltpu.VMEM((side, side), BF16),
        ]
        + [pltpu.SMEM(x.shape, jnp.int32) for x in operands[:4]]
        + [pltpu.SemaphoreType.DMA((particles,)), pltpu.SemaphoreType.DMA((5,))],
        compiler_params=pltpu.CompilerParams(vmem_limit_bytes=VMEM_BYTES),
        name="home",
    )(*operands, *after)


def middle_kernel(mic_count, sizes, *rest):
    arrived, flat = rest[: len(rest) - sum(map(len, sizes))], list(rest[-sum(map(len, sizes)) :])
    outs = [[flat.pop(0) for _ in parts] for parts in sizes]
    rows = arrived[0].shape[0]
    here = lax.axis_index("mic")
    empty = jnp.zeros((LABEL_ROWS, LANES), BF16)
    for out in sum(outs, []):
        for j in range(out.shape[0]):
            out[j, rows - LABEL_ROWS : rows, :] = empty
    targets = [
        jnp.max(block[rows - LABEL_ROWS : rows, :].astype(F32)[0:1]).astype(jnp.int32)
        for block in arrived
    ]
    counts = [jnp.int32(0)] * mic_count
    for block, target in zip(arrived, targets):
        step_of = (target - 1) ^ here
        for step in range(mic_count):
            chosen = (target > 0) & (step_of == step)
            if len(outs[step]) == 1:

                @pl.when(chosen)
                def _(block=block, out=outs[step][0], slot=counts[step]):
                    out[slot] = block[...]

            else:
                for j, out in enumerate(outs[step]):

                    @pl.when(chosen & (counts[step] == j))
                    def _(block=block, out=out):
                        out[0] = block[...]

            counts[step] = counts[step] + chosen.astype(jnp.int32)


def middle_call(mic_count, sizes, arrived):
    flat = sum(sizes, [])
    outs = pl.pallas_call(
        functools.partial(middle_kernel, mic_count, sizes),
        out_shape=[jax.ShapeDtypeStruct((n, *arrived[0].shape), BF16) for n in flat],
        in_specs=[VMEM] * len(arrived),
        out_specs=[VMEM] * len(flat),
        compiler_params=pltpu.CompilerParams(vmem_limit_bytes=VMEM_BYTES),
        name="middle",
    )(*arrived)
    outs = list(outs)
    return [[outs.pop(0) for _ in parts] for parts in sizes]


def fold(values):
    return jnp.sum(values.reshape(values.shape[0] // 8, 8, values.shape[1]), axis=0)


def chunks_of(side):
    return [slice(c, c + CHUNK) for c in range(0, side, CHUNK)]


def shares(ctf, weight, s, rows, values):
    table = ctf[s, rows, :]
    scaled = weight * table
    return (scaled * values).astype(BF16).astype(F32), scaled * table, table


def renew(previous, numerator, denominator):
    return (
        (numerator + PRIOR_WEIGHT * previous.astype(F32)) / (denominator + PRIOR_WEIGHT)
    ).astype(BF16)


def update_shared(info, groups, weight, number, source, target, kind=MEMBERS):
    chunks = chunks_of(source.shape[1])

    @pl.loop(0, source.shape[0])
    def _(p):
        @pl.when((info[MEMBERS, p] > 1) & (info[kind, p] > 0))
        def _():
            number[...] = jnp.zeros(number.shape, F32)
            for ctf, spectra, first in groups:

                @pl.loop(0, spectra.shape[0])
                def _(k):
                    @pl.when((info[ACTIVE, first + k] > 0) & (info[PLACE, first + k] == p))
                    def _():
                        scale = weight[pl.ds(first + k, 1), :]
                        for rows in chunks:
                            values = spectra[k, rows, :].astype(F32)
                            term, power, _ = shares(ctf, scale, k, rows, values)
                            number[0, rows, :] += term
                            number[1, rows, :] += power

            for rows in chunks:
                target[p, rows, :] = renew(
                    source[p, rows, :], number[0, rows, :], number[1, rows, :]
                )


def read_labels(labels):
    places, senders = [], []
    for block in labels:
        code = block[1:2] + 256.0 * block[3:4]
        code = jnp.max(jnp.where(block[0:1] > 0, code, -1.0)).astype(jnp.int32)
        places.append(jnp.where(code < 0, -1, code & 255))
        senders.append(jnp.maximum(code, 0) >> 8)
    return places, senders


def fill_info(info, places, own_bins, late=0):
    for p in range(own_bins):
        info[MEMBERS, p] = jnp.int32(0)
        info[LATE, p] = jnp.int32(0)
    for s, place in enumerate(places):
        active = (place >= 0).astype(jnp.int32)
        place = jnp.maximum(place, 0)
        info[ACTIVE, s] = active
        info[PLACE, s] = place
        info[MEMBERS, place] = info[MEMBERS, place] + active
        if s >= len(places) - late:
            info[LATE, place] = info[LATE, place] + active
    for s, place in enumerate(places):
        single = (place >= 0) & (info[MEMBERS, jnp.maximum(place, 0)] == 1)
        info[ALONE, s] = single.astype(jnp.int32)


def ctf_factors(labels, focus_ref, damping_ref, side):
    groups = focus_ref.shape[1]
    group = jnp.concatenate([x[2:3, :groups] for x in labels] + [labels[0][4:5, :groups]] * 8)[:8]
    chosen = group.astype(jnp.int32) == lax.broadcasted_iota(jnp.int32, (8, groups), 1)
    focus = jnp.sum(jnp.where(chosen, focus_ref[...], 0.0), axis=1, keepdims=True)
    damping = jnp.sum(jnp.where(chosen, damping_ref[...], 0.0), axis=1, keepdims=True)
    frequency = lax.broadcasted_iota(jnp.int32, (8, side), 1)
    folded = jnp.minimum(frequency, side - frequency).astype(F32) / (side / 2.0)
    square = folded * folded
    envelope = jnp.exp(-damping * square)
    sine = jnp.sin(focus * square) * envelope
    cosine = jnp.cos(focus * square) * envelope
    by_sine = jnp.transpose(CONTRAST * sine - AMPLITUDE * cosine)
    by_cosine = jnp.transpose(-(AMPLITUDE * sine + CONTRAST * cosine))
    return by_sine, sine, by_cosine, cosine


def ctf_chunk(factors, s, rows):
    by_sine, sine, by_cosine, cosine = factors
    return (
        by_sine[rows, s : s + 1] * sine[s : s + 1, :]
        + by_cosine[rows, s : s + 1] * cosine[s : s + 1, :]
    )


def blocks_of(arrived):
    return [block.at[j] for block in arrived for j in range(block.shape[0])]


def image_of(block, rows, side):
    lefts = range(0, side * side // LANES, side)
    return jnp.concatenate([block[n + rows.start : n + rows.stop, :] for n in lefts], axis=1)


def labels_of(blocks):
    return [block[block.shape[0] - LABEL_ROWS :, :].astype(F32) for block in blocks]


def first_compare(p, factors, current_ref, group, sums, s, block):
    ctf, spectra, first = group
    side = ctf.shape[1]
    cross = model = data = jnp.zeros((8, side), F32)
    for rows in chunks_of(side):
        table = ctf_chunk(factors, s, rows)
        ctf[s - first, rows, :] = table
        held = image_of(block, rows, side)
        spectra[s - first, rows, :] = held
        values = held.astype(F32)
        predicted = table * current_ref[p, rows, :].astype(F32)
        cross = cross + fold(predicted * values)
        model = model + fold(predicted * predicted)
        data = data + fold(values * values)
    for k, total in enumerate((cross, model, data)):
        sums[k, s : s + 1, :] = jnp.sum(total, axis=0, keepdims=True)


def correlate(sums, side):
    pixels = float(side * side)
    cross, model, data = (jnp.sum(sums[k], axis=1, keepdims=True) / pixels for k in range(3))
    correlation = cross / jnp.sqrt((model + EPSILON) * (data + EPSILON))
    weights = 1.0 / (1.0 + jnp.exp(-float(side) * correlation))
    return correlation, jnp.broadcast_to(weights.astype(BF16).astype(F32), (8, side))


def second_compare(group, k, reference_of):
    ctf, spectra, _ = group
    side = ctf.shape[1]
    cross = model = jnp.zeros((8, side), F32)
    for rows in chunks_of(side):
        values = spectra[k, rows, :].astype(F32)
        reference = reference_of(rows, values)
        predicted = ctf[k, rows, :] * reference.astype(F32)
        cross = cross + fold(predicted * values)
        model = model + fold(predicted * predicted)
    return cross, model


def update_and_compare(s, p, alone, shared, group, weight, sums, source, target):
    ctf, spectra, first = group
    k = s - first

    def keep(cross, model):
        sums[0, pl.ds(s, 1), :] = jnp.sum(cross, axis=0, keepdims=True)
        sums[1, pl.ds(s, 1), :] = jnp.sum(model, axis=0, keepdims=True)

    @pl.when(alone)
    def _():
        scale = weight[pl.ds(s, 1), :]

        def new(rows, values):
            term, power, _ = shares(ctf, scale, k, rows, values)
            reference = renew(source[p, rows, :], term, power)
            target[p, rows, :] = reference
            return reference

        keep(*second_compare(group, k, new))

    @pl.when(shared)
    def _():
        keep(*second_compare(group, k, lambda rows, _: target[p, rows, :]))


def ready_kernel(bin_count, steps, focus_ref, damping_ref, current_ref, *rest):
    blocks, rest = blocks_of(rest[:-7]), rest[-7:]
    ctf, spectra, weight, middle, sums, number, info = rest
    own_bins, side, _ = current_ref.shape
    labels = labels_of(blocks)
    fill_info(info, read_labels(labels)[0], own_bins)
    factors = ctf_factors(labels, focus_ref, damping_ref, side)
    sums[...] = jnp.zeros(sums.shape, F32)
    group = (ctf, spectra, 0)
    for s in range(len(labels)):

        @pl.when(info[ACTIVE, s] > 0)
        def _(s=s):
            first_compare(info[PLACE, s], factors, current_ref, group, sums, s, blocks[s])

    weight[...] = correlate(sums, side)[1]
    update_shared(info, (group,), weight, number, current_ref, middle)

    @pl.loop(0, len(labels))
    def _(s):
        alone = info[ALONE, s] > 0
        shared = (info[ACTIVE, s] > 0) & (info[ALONE, s] == 0)
        p = info[PLACE, s]
        update_and_compare(s, p, alone, shared, group, weight, sums, current_ref, middle)


def ready_call(bin_count, steps, defocus, bfactor, references, arrived):
    own_bins, side, _ = references.shape
    slots = len(steps)
    return pl.pallas_call(
        functools.partial(ready_kernel, bin_count, steps),
        out_shape=[
            jax.ShapeDtypeStruct((slots, side, side), F32),
            jax.ShapeDtypeStruct((slots, side, side), BF16),
            jax.ShapeDtypeStruct((8, side), F32),
            jax.ShapeDtypeStruct(references.shape, BF16),
            jax.ShapeDtypeStruct((3, 8, side), F32),
        ],
        in_specs=[VMEM] * (3 + len(arrived)),
        out_specs=[VMEM] * 5,
        scratch_shapes=[
            pltpu.VMEM((2, side, side), F32),
            pltpu.SMEM((INFOS, max(8, own_bins)), jnp.int32),
        ],
        compiler_params=pltpu.CompilerParams(vmem_limit_bytes=VMEM_BYTES),
        name="ready",
    )(defocus, bfactor, references, *arrived)


def owner_kernel(bin_count, steps, focus_ref, damping_ref, current_ref, *rest):
    blocks, rest = blocks_of(rest[:-14]), rest[-14:]
    early_ctf, early_spectra, early_weight, early_sums = rest[:4]
    middle_ref, weight, label_ref, score_ref = rest[4:8]
    ctf, spectra, middle, sums, number, info = rest[8:]
    own_bins, side, _ = current_ref.shape
    early = early_ctf.shape[0]
    slots = len(steps)
    here = lax.axis_index("mic")

    labels = labels_of(blocks)
    for s, label in enumerate(labels):
        label_ref[s] = label
    places, senders = read_labels(labels)
    factors = ctf_factors(labels, focus_ref, damping_ref, side)
    sums[...] = early_sums[...]
    early_group, late_group = (early_ctf, early_spectra, 0), (ctf, spectra, early)
    shared = {}
    for s in range(early, slots):
        active = places[s] >= 0
        others = [places[t] == places[s] for t in range(slots) if t != s]
        shared[s] = active & functools.reduce(jnp.logical_or, others)

        @pl.when(active)
        def _(s=s):
            first_compare(places[s], factors, current_ref, late_group, sums, s, blocks[s])

    row = lax.broadcasted_iota(jnp.int32, (8, side), 0)
    weight[...] = jnp.where(row < early, early_weight[...], correlate(sums, side)[1])
    any_shared = functools.reduce(jnp.logical_or, shared.values())

    @pl.when(any_shared)
    def _():
        fill_info(info, places, own_bins, slots - early)
        update_shared(
            info, (early_group, late_group), weight, number, current_ref, middle, kind=LATE
        )

        @pl.loop(0, early)
        def _(s):
            p = info[PLACE, s]

            @pl.when((info[ACTIVE, s] > 0) & (info[LATE, p] > 0))
            def _():
                cross, model = second_compare(early_group, s, lambda rows, _: middle[p, rows, :])
                sums[0, pl.ds(s, 1), :] = jnp.sum(cross, axis=0, keepdims=True)
                sums[1, pl.ds(s, 1), :] = jnp.sum(model, axis=0, keepdims=True)

    for s in range(early, slots):
        alone = (places[s] >= 0) & jnp.logical_not(shared[s])
        update_and_compare(
            s, places[s], alone, shared[s], late_group, weight, sums, current_ref, middle
        )

    for s in range(early, slots):

        @pl.when(places[s] >= 0)
        def _(s=s):
            middle_ref[s - early] = middle[places[s]]

    correlation, weight[...] = correlate(sums, side)
    score_ref[...] = jnp.zeros(score_ref.shape, F32)
    lane = lax.broadcasted_iota(jnp.int32, (1, 128), 1)
    for s in range(slots):
        home = (here ^ steps[s]) * bin_count + lax.rem(senders[s], bin_count)
        hit = (lane == senders[s] // bin_count) & (places[s] >= 0)
        score_ref[home] = score_ref[home] + jnp.where(hit, correlation[s : s + 1, :], 0.0)

def owner_call(devices, bin_count, steps, defocus, bfactor, references, arrived, early):
    own_bins, side, _ = references.shape
    slots = len(steps)
    late = slots - early[0].shape[0]
    return pl.pallas_call(
        functools.partial(owner_kernel, bin_count, steps),
        out_shape=[
            jax.ShapeDtypeStruct((late, side, side), BF16),
            jax.ShapeDtypeStruct((8, side), F32),
            jax.ShapeDtypeStruct((slots, LABEL_ROWS, 128), F32),
            jax.ShapeDtypeStruct((devices, 1, 128), F32),
        ],
        in_specs=[VMEM] * (3 + len(arrived) + len(early)),
        out_specs=[VMEM] * 4,
        scratch_shapes=[
            pltpu.VMEM((late, side, side), F32),
            pltpu.VMEM((late, side, side), BF16),
            pltpu.VMEM(references.shape, BF16),
            pltpu.VMEM((3, 8, side), F32),
            pltpu.VMEM((2, side, side), F32),
            pltpu.SMEM((INFOS, max(8, own_bins)), jnp.int32),
        ],
        compiler_params=pltpu.CompilerParams(vmem_limit_bytes=VMEM_BYTES),
        name="owner",
    )(defocus, bfactor, references, *arrived, *early)


def last_kernel(
    focus_ref,
    damping_ref,
    weight,
    label_ref,
    early_spectra,
    early_middle,
    late_middle,
    late_ref,
    current_hbm,
    refined_ref,
    spectra,
    middle,
    ctf,
    number,
    info,
    sem,
):
    slots, side, _ = ctf.shape
    own_bins = refined_ref.shape[0]
    early = early_spectra.shape[0]
    labels = [label_ref[s] for s in range(slots)]
    places, _ = read_labels(labels)
    fill_info(info, places, own_bins)

    def unchanged(p):
        return pltpu.make_async_copy(current_hbm.at[p], refined_ref.at[p], sem.at[p])

    @pl.loop(0, own_bins)
    def _(p):
        @pl.when(info[MEMBERS, p] == 0)
        def _():
            unchanged(p).start()

    factors = ctf_factors(labels, focus_ref, damping_ref, side)
    for s in range(slots):

        @pl.when(places[s] >= 0)
        def _(s=s):
            for rows in chunks_of(side):
                ctf[s, rows, :] = ctf_chunk(factors, s, rows)
            if s < early:
                spectra[s] = early_spectra[s]
                middle[places[s]] = early_middle[places[s]]
            else:
                spectra[s] = image_of(late_ref.at[s - early], slice(0, side), side)
                middle[places[s]] = late_middle[s - early]

    update_shared(info, ((ctf, spectra, 0),), weight, number, middle, refined_ref)

    @pl.loop(0, slots)
    def _(s):
        @pl.when(info[ALONE, s] > 0)
        def _():
            p = info[PLACE, s]
            scale = weight[pl.ds(s, 1), :]
            for rows in chunks_of(side):
                values = spectra[s, rows, :].astype(F32)
                term, power, _ = shares(ctf, scale, s, rows, values)
                refined_ref[p, rows, :] = renew(middle[p, rows, :], term, power)

    @pl.loop(0, own_bins)
    def _(p):
        @pl.when(info[MEMBERS, p] == 0)
        def _():
            unchanged(p).wait()


def last_call(defocus, bfactor, references, weight, labels, kept):
    own_bins, side, _ = references.shape
    slots = labels.shape[0]
    return pl.pallas_call(
        last_kernel,
        out_shape=jax.ShapeDtypeStruct(references.shape, BF16),
        in_specs=[VMEM] * 8 + [HBM],
        out_specs=VMEM,
        scratch_shapes=[
            pltpu.VMEM((slots, side, side), BF16),
            pltpu.VMEM(references.shape, BF16),
            pltpu.VMEM((slots, side, side), F32),
            pltpu.VMEM((2, side, side), F32),
            pltpu.SMEM((INFOS, max(8, own_bins)), jnp.int32),
            pltpu.SemaphoreType.DMA((own_bins,)),
        ],
        compiler_params=pltpu.CompilerParams(vmem_limit_bytes=VMEM_BYTES),
        cost_estimate=pl.CostEstimate(flops=4 << 20, bytes_accessed=4 << 20, transcendentals=0),
        name="last",
    )(defocus, bfactor, weight, labels, *kept, in_hbm(references))


def exchange(blocks, axis):
    size = lax.axis_size(axis)
    return [blocks[0]] + [
        lax.ppermute(blocks[k], axis, [(i, i ^ k) for i in range(size)]) for k in range(1, size)
    ]


def body(images, offsets, ctf_group, particle_bin, bin_place, defocus, bfactor, references):
    mic_count = lax.axis_size("mic")
    bin_count = lax.axis_size("bin")
    particles, side, _ = images.shape
    own_bins = references.shape[0]
    capacity = (3 * particles + 2 * mic_count - 1) // (2 * mic_count)

    basis = jnp.asarray(hartley(side), BF16)
    operands = (bin_place, particle_bin, ctf_group, offsets, images, basis)
    operands = tuple(map(in_hbm, operands))
    far = 3 * bin_count // 8
    rest = bin_count - far
    sent_far = home_call(bin_count, own_bins, rest, far, operands)
    sent_near = home_call(bin_count, own_bins, 0, rest, operands, after=(sent_far[-1],))
    arrived = exchange(list(sent_near) + list(sent_far), "bin")

    last = mic_count - 1
    sizes = [[1] * capacity if step == 1 else [capacity] for step in range(mic_count)]
    sent = middle_call(mic_count, sizes, arrived[::-1])
    blocks = [(0, block) for block in sent[0]]
    for step in [t for t in range(1, mic_count) if t != last] + [last]:
        pairs = [(i, i ^ step) for i in range(mic_count)]
        blocks += [(step, lax.ppermute(block, "mic", pairs)) for block in sent[step]]
    steps = [step for step, block in blocks for _ in range(block.shape[0])]
    arrived = [block for _, block in blocks]
    tables = (defocus.reshape(1, -1), bfactor.reshape(1, -1), references)
    early = slice(0, -arrived[-1].shape[0])
    ctf, spectra, early_weight, middle, sums = ready_call(
        bin_count, steps[early], *tables, arrived[:-1]
    )
    late_middle, weight, labels, board = owner_call(
        mic_count * bin_count, bin_count, steps, *tables, arrived, (ctf, spectra, early_weight, sums)
    )
    back = lax.all_to_all(board, ("mic", "bin"), split_axis=0, concat_axis=0, tiled=True)
    refined = last_call(*tables, weight, labels, (spectra, middle, late_middle, arrived[-1]))
    return (refined, jnp.sum(back, axis=(0, 1))[:particles])


def solution(mesh):
    in_specs = (
        P(("mic", "bin"), None, None),
        P(None, ("mic", "bin")),
        P(("mic", "bin")),
        P(("mic", "bin")),
        P(),
        P(),
        P(),
        P(("mic", "bin"), None, None),
    )
    out_specs = (P(("mic", "bin"), None, None), P(("mic", "bin")))
    return jax.shard_map(body, mesh=mesh, in_specs=in_specs, out_specs=out_specs, check_vma=False)
```

```python
import functools
import math

import jax
import jax.numpy as jnp
import numpy as np
from jax import lax
from jax.experimental import pallas as pl
from jax.experimental.pallas import tpu as pltpu
from jax.sharding import PartitionSpec as P

ITERS = 2
PRIOR_WEIGHT = 0.5
EPSILON = 1e-06
CONTRAST = 0.1
AMPLITUDE = math.sqrt(1.0 - CONTRAST * CONTRAST)

LANES = 128
LABEL_ROWS = 16
CHUNK = 32
VMEM_BYTES = 24 * 1024 * 1024

ACTIVE, PLACE, ALONE, MEMBERS, LATE = range(5)
INFOS = 5

F32 = jnp.float32
BF16 = jnp.bfloat16
VMEM = pl.BlockSpec(memory_space=pltpu.VMEM)
SMEM = pl.BlockSpec(memory_space=pltpu.SMEM)
HBM = pl.BlockSpec(memory_space=pltpu.HBM)
ANY = pl.BlockSpec(memory_space=pl.ANY)


def in_hbm(x):
    return pltpu.with_memory_space_constraint(x, pltpu.HBM)


def hartley(side):
    index = np.arange(side)
    angles = (np.outer(index, index) % side).astype(np.float32) * np.float32(2.0 * math.pi / side)
    return (np.cos(angles) + np.sin(angles)) / np.float32(math.sqrt(side))


def label_block(values):
    row = lax.broadcasted_iota(jnp.int32, (LABEL_ROWS, LANES), 0)
    block = jnp.zeros((LABEL_ROWS, LANES), jnp.int32)
    for number, value in enumerate(values):
        block = jnp.where(row == number, value, block)
    return block.astype(F32).astype(BF16)


def home_kernel(
    bin_count, own_bins, first, count, place_hbm, bin_hbm, group_hbm, offset_hbm, image_hbm, basis_hbm, *rest
):
    rest = rest[len(rest) - count - 9 :]
    outs, rest = rest[:count], rest[count:]
    spectra, image_ref, basis_ref, place_ref, bin_ref, group_ref, offset_ref, image_sem, sem = rest
    particles, side = image_ref.shape[0], image_ref.shape[1]
    here = lax.axis_index("bin")
    pairs = (
        (basis_hbm, basis_ref),
        (place_hbm, place_ref),
        (bin_hbm, bin_ref),
        (group_hbm, group_ref),
        (offset_hbm, offset_ref),
    )
    copies = [pltpu.make_async_copy(a, b, sem.at[k]) for k, (a, b) in enumerate(pairs)]
    for copy in copies:
        copy.start()

    def image_copy(i):
        return pltpu.make_async_copy(image_hbm.at[i], image_ref.at[i], image_sem.at[i])

    for i in range(particles):
        image_copy(i).start()
    pieces = side // LANES
    for out in outs:
        out[pieces * side :, :] = jnp.zeros((LABEL_ROWS, LANES), BF16)
    for copy in copies:
        copy.wait()

    @pl.loop(0, particles)
    def _(i):
        image_copy(i).wait()
        place = place_ref[bin_ref[i]]
        owner = place // own_bins
        step_of = lax.rem(owner, bin_count) ^ here

        @pl.when((step_of >= first) & (step_of < first + count))
        def _():
            moved = pltpu.roll(
                image_ref[i].astype(F32), lax.rem(side - offset_ref[0, i], side), 0
            ).astype(BF16)
            columns = pltpu.roll(basis_ref[...].astype(F32), offset_ref[1, i], 0).astype(BF16)
            half = jnp.dot(basis_ref[...], moved, preferred_element_type=F32).astype(BF16)
            spectra[...] = jnp.dot(half, columns, preferred_element_type=F32).astype(BF16)
            labels = label_block(
                (
                    1 + owner // bin_count,
                    lax.rem(place, own_bins),
                    group_ref[i],
                    i * bin_count + here,
                )
            )
            for k in range(count):

                @pl.when(step_of == first + k)
                def _():
                    for n in range(pieces):
                        outs[k][n * side : (n + 1) * side, :] = spectra[
                            :, n * LANES : (n + 1) * LANES
                        ]
                    outs[k][pieces * side :, :] = labels


def home_call(bin_count, own_bins, first, count, operands, after=()):
    images, particles, side = operands[4], operands[4].shape[0], operands[4].shape[1]
    return pl.pallas_call(
        functools.partial(home_kernel, bin_count, own_bins, first, count),
        out_shape=[
            jax.ShapeDtypeStruct((side * side // LANES + LABEL_ROWS, LANES), BF16)
        ]
        * count,
        in_specs=[HBM] * 6 + [ANY] * len(after),
        out_specs=[VMEM] * count,
        scratch_shapes=[
            pltpu.VMEM((side, side), BF16),
            pltpu.VMEM(images.shape, BF16),
            pltpu.VMEM((side, side), BF16),
        ]
        + [pltpu.SMEM(x.shape, jnp.int32) for x in operands[:4]]
        + [pltpu.SemaphoreType.DMA((particles,)), pltpu.SemaphoreType.DMA((5,))],
        compiler_params=pltpu.CompilerParams(vmem_limit_bytes=VMEM_BYTES),
        name="home",
    )(*operands, *after)


def middle_kernel(mic_count, sizes, *rest):
    arrived, flat = rest[: len(rest) - sum(map(len, sizes))], list(rest[-sum(map(len, sizes)) :])
    outs = [[flat.pop(0) for _ in parts] for parts in sizes]
    rows = arrived[0].shape[0]
    here = lax.axis_index("mic")
    empty = jnp.zeros((LABEL_ROWS, LANES), BF16)
    for out in sum(outs, []):
        for j in range(out.shape[0]):
            out[j, rows - LABEL_ROWS : rows, :] = empty
    targets = [
        jnp.max(block[rows - LABEL_ROWS : rows, :].astype(F32)[0:1]).astype(jnp.int32)
        for block in arrived
    ]
    counts = [jnp.int32(0)] * mic_count
    for block, target in zip(arrived, targets):
        step_of = (target - 1) ^ here
        for step in range(mic_count):
            chosen = (target > 0) & (step_of == step)
            if len(outs[step]) == 1:

                @pl.when(chosen)
                def _(block=block, out=outs[step][0], slot=counts[step]):
                    out[slot] = block[...]

            else:
                for j, out in enumerate(outs[step]):

                    @pl.when(chosen & (counts[step] == j))
                    def _(block=block, out=out):
                        out[0] = block[...]

            counts[step] = counts[step] + chosen.astype(jnp.int32)


def middle_call(mic_count, sizes, arrived):
    flat = sum(sizes, [])
    outs = pl.pallas_call(
        functools.partial(middle_kernel, mic_count, sizes),
        out_shape=[jax.ShapeDtypeStruct((n, *arrived[0].shape), BF16) for n in flat],
        in_specs=[VMEM] * len(arrived),
        out_specs=[VMEM] * len(flat),
        compiler_params=pltpu.CompilerParams(vmem_limit_bytes=VMEM_BYTES),
        name="middle",
    )(*arrived)
    outs = list(outs)
    return [[outs.pop(0) for _ in parts] for parts in sizes]


def fold(values):
    return jnp.sum(values.reshape(values.shape[0] // 8, 8, values.shape[1]), axis=0)


def chunks_of(side):
    return [slice(c, c + CHUNK) for c in range(0, side, CHUNK)]


def shares(ctf, weight, s, rows, values):
    table = ctf[s, rows, :]
    scaled = weight * table
    return (scaled * values).astype(BF16).astype(F32), scaled * table, table


def renew(previous, numerator, denominator):
    return (
        (numerator + PRIOR_WEIGHT * previous.astype(F32)) / (denominator + PRIOR_WEIGHT)
    ).astype(BF16)


def update_shared(info, groups, weight, number, source, target, kind=MEMBERS):
    chunks = chunks_of(source.shape[1])

    @pl.loop(0, source.shape[0])
    def _(p):
        @pl.when((info[MEMBERS, p] > 1) & (info[kind, p] > 0))
        def _():
            number[...] = jnp.zeros(number.shape, F32)
            for ctf, spectra, first in groups:

                @pl.loop(0, spectra.shape[0])
                def _(k):
                    @pl.when((info[ACTIVE, first + k] > 0) & (info[PLACE, first + k] == p))
                    def _():
                        scale = weight[pl.ds(first + k, 1), :]
                        for rows in chunks:
                            values = spectra[k, rows, :].astype(F32)
                            term, power, _ = shares(ctf, scale, k, rows, values)
                            number[0, rows, :] += term
                            number[1, rows, :] += power

            for rows in chunks:
                target[p, rows, :] = renew(
                    source[p, rows, :], number[0, rows, :], number[1, rows, :]
                )


def read_labels(labels):
    places, senders = [], []
    for block in labels:
        code = block[1:2] + 256.0 * block[3:4]
        code = jnp.max(jnp.where(block[0:1] > 0, code, -1.0)).astype(jnp.int32)
        places.append(jnp.where(code < 0, -1, code & 255))
        senders.append(jnp.maximum(code, 0) >> 8)
    return places, senders


def fill_info(info, places, own_bins, late=0):
    for p in range(own_bins):
        info[MEMBERS, p] = jnp.int32(0)
        info[LATE, p] = jnp.int32(0)
    for s, place in enumerate(places):
        active = (place >= 0).astype(jnp.int32)
        place = jnp.maximum(place, 0)
        info[ACTIVE, s] = active
        info[PLACE, s] = place
        info[MEMBERS, place] = info[MEMBERS, place] + active
        if s >= len(places) - late:
            info[LATE, place] = info[LATE, place] + active
    for s, place in enumerate(places):
        single = (place >= 0) & (info[MEMBERS, jnp.maximum(place, 0)] == 1)
        info[ALONE, s] = single.astype(jnp.int32)


def ctf_factors(labels, focus_ref, damping_ref, side):
    groups = focus_ref.shape[1]
    group = jnp.concatenate([x[2:3, :groups] for x in labels] + [labels[0][4:5, :groups]] * 8)[:8]
    chosen = group.astype(jnp.int32) == lax.broadcasted_iota(jnp.int32, (8, groups), 1)
    focus = jnp.sum(jnp.where(chosen, focus_ref[...], 0.0), axis=1, keepdims=True)
    damping = jnp.sum(jnp.where(chosen, damping_ref[...], 0.0), axis=1, keepdims=True)
    frequency = lax.broadcasted_iota(jnp.int32, (8, side), 1)
    folded = jnp.minimum(frequency, side - frequency).astype(F32) / (side / 2.0)
    square = folded * folded
    envelope = jnp.exp(-damping * square)
    sine = jnp.sin(focus * square) * envelope
    cosine = jnp.cos(focus * square) * envelope
    by_sine = jnp.transpose(CONTRAST * sine - AMPLITUDE * cosine)
    by_cosine = jnp.transpose(-(AMPLITUDE * sine + CONTRAST * cosine))
    return by_sine, sine, by_cosine, cosine


def ctf_chunk(factors, s, rows):
    by_sine, sine, by_cosine, cosine = factors
    return (
        by_sine[rows, s : s + 1] * sine[s : s + 1, :]
        + by_cosine[rows, s : s + 1] * cosine[s : s + 1, :]
    )


def blocks_of(arrived):
    return [block.at[j] for block in arrived for j in range(block.shape[0])]


def image_of(block, rows, side):
    lefts = range(0, side * side // LANES, side)
    return jnp.concatenate([block[n + rows.start : n + rows.stop, :] for n in lefts], axis=1)


def labels_of(blocks):
    return [block[block.shape[0] - LABEL_ROWS :, :].astype(F32) for block in blocks]


def first_compare(p, factors, current_ref, group, sums, s, block):
    ctf, spectra, first = group
    side = ctf.shape[1]
    cross = model = data = jnp.zeros((8, side), F32)
    for rows in chunks_of(side):
        table = ctf_chunk(factors, s, rows)
        ctf[s - first, rows, :] = table
        held = image_of(block, rows, side)
        spectra[s - first, rows, :] = held
        values = held.astype(F32)
        predicted = table * current_ref[p, rows, :].astype(F32)
        cross = cross + fold(predicted * values)
        model = model + fold(predicted * predicted)
        data = data + fold(values * values)
    for k, total in enumerate((cross, model, data)):
        sums[k, s : s + 1, :] = jnp.sum(total, axis=0, keepdims=True)


def correlate(sums, side):
    pixels = float(side * side)
    cross, model, data = (jnp.sum(sums[k], axis=1, keepdims=True) / pixels for k in range(3))
    correlation = cross / jnp.sqrt((model + EPSILON) * (data + EPSILON))
    weights = 1.0 / (1.0 + jnp.exp(-float(side) * correlation))
    return correlation, jnp.broadcast_to(weights.astype(BF16).astype(F32), (8, side))


def second_compare(group, k, reference_of):
    ctf, spectra, _ = group
    side = ctf.shape[1]
    cross = model = jnp.zeros((8, side), F32)
    for rows in chunks_of(side):
        values = spectra[k, rows, :].astype(F32)
        reference = reference_of(rows, values)
        predicted = ctf[k, rows, :] * reference.astype(F32)
        cross = cross + fold(predicted * values)
        model = model + fold(predicted * predicted)
    return cross, model


def update_and_compare(s, p, alone, shared, group, weight, sums, source, target):
    ctf, spectra, first = group
    k = s - first

    def keep(cross, model):
        sums[0, pl.ds(s, 1), :] = jnp.sum(cross, axis=0, keepdims=True)
        sums[1, pl.ds(s, 1), :] = jnp.sum(model, axis=0, keepdims=True)

    @pl.when(alone)
    def _():
        scale = weight[pl.ds(s, 1), :]

        def new(rows, values):
            term, power, _ = shares(ctf, scale, k, rows, values)
            reference = renew(source[p, rows, :], term, power)
            target[p, rows, :] = reference
            return reference

        keep(*second_compare(group, k, new))

    @pl.when(shared)
    def _():
        keep(*second_compare(group, k, lambda rows, _: target[p, rows, :]))


def ready_kernel(bin_count, steps, focus_ref, damping_ref, current_ref, *rest):
    blocks, rest = blocks_of(rest[:-7]), rest[-7:]
    ctf, spectra, weight, middle, sums, number, info = rest
    own_bins, side, _ = current_ref.shape
    labels = labels_of(blocks)
    fill_info(info, read_labels(labels)[0], own_bins)
    factors = ctf_factors(labels, focus_ref, damping_ref, side)
    sums[...] = jnp.zeros(sums.shape, F32)
    group = (ctf, spectra, 0)
    for s in range(len(labels)):

        @pl.when(info[ACTIVE, s] > 0)
        def _(s=s):
            first_compare(info[PLACE, s], factors, current_ref, group, sums, s, blocks[s])

    weight[...] = correlate(sums, side)[1]
    update_shared(info, (group,), weight, number, current_ref, middle)

    @pl.loop(0, len(labels))
    def _(s):
        alone = info[ALONE, s] > 0
        shared = (info[ACTIVE, s] > 0) & (info[ALONE, s] == 0)
        p = info[PLACE, s]
        update_and_compare(s, p, alone, shared, group, weight, sums, current_ref, middle)


def ready_call(bin_count, steps, defocus, bfactor, references, arrived):
    own_bins, side, _ = references.shape
    slots = len(steps)
    return pl.pallas_call(
        functools.partial(ready_kernel, bin_count, steps),
        out_shape=[
            jax.ShapeDtypeStruct((slots, side, side), F32),
            jax.ShapeDtypeStruct((slots, side, side), BF16),
            jax.ShapeDtypeStruct((8, side), F32),
            jax.ShapeDtypeStruct(references.shape, BF16),
            jax.ShapeDtypeStruct((3, 8, side), F32),
        ],
        in_specs=[VMEM] * (3 + len(arrived)),
        out_specs=[VMEM] * 5,
        scratch_shapes=[
            pltpu.VMEM((2, side, side), F32),
            pltpu.SMEM((INFOS, max(8, own_bins)), jnp.int32),
        ],
        compiler_params=pltpu.CompilerParams(vmem_limit_bytes=VMEM_BYTES),
        name="ready",
    )(defocus, bfactor, references, *arrived)


def owner_kernel(bin_count, steps, focus_ref, damping_ref, current_ref, *rest):
    blocks, rest = blocks_of(rest[:-14]), rest[-14:]
    early_ctf, early_spectra, early_weight, early_sums = rest[:4]
    middle_ref, weight, label_ref, score_ref = rest[4:8]
    ctf, spectra, middle, sums, number, info = rest[8:]
    own_bins, side, _ = current_ref.shape
    early = early_ctf.shape[0]
    slots = len(steps)
    here = lax.axis_index("mic")

    labels = labels_of(blocks)
    for s, label in enumerate(labels):
        label_ref[s] = label
    places, senders = read_labels(labels)
    factors = ctf_factors(labels, focus_ref, damping_ref, side)
    sums[...] = early_sums[...]
    early_group, late_group = (early_ctf, early_spectra, 0), (ctf, spectra, early)
    shared = {}
    for s in range(early, slots):
        active = places[s] >= 0
        others = [places[t] == places[s] for t in range(slots) if t != s]
        shared[s] = active & functools.reduce(jnp.logical_or, others)

        @pl.when(active)
        def _(s=s):
            first_compare(places[s], factors, current_ref, late_group, sums, s, blocks[s])

    row = lax.broadcasted_iota(jnp.int32, (8, side), 0)
    weight[...] = jnp.where(row < early, early_weight[...], correlate(sums, side)[1])
    any_shared = functools.reduce(jnp.logical_or, shared.values())

    @pl.when(any_shared)
    def _():
        fill_info(info, places, own_bins, slots - early)
        update_shared(
            info, (early_group, late_group), weight, number, current_ref, middle, kind=LATE
        )

        @pl.loop(0, early)
        def _(s):
            p = info[PLACE, s]

            @pl.when((info[ACTIVE, s] > 0) & (info[LATE, p] > 0))
            def _():
                cross, model = second_compare(early_group, s, lambda rows, _: middle[p, rows, :])
                sums[0, pl.ds(s, 1), :] = jnp.sum(cross, axis=0, keepdims=True)
                sums[1, pl.ds(s, 1), :] = jnp.sum(model, axis=0, keepdims=True)

    for s in range(early, slots):
        alone = (places[s] >= 0) & jnp.logical_not(shared[s])
        update_and_compare(
            s, places[s], alone, shared[s], late_group, weight, sums, current_ref, middle
        )

    for s in range(early, slots):

        @pl.when(places[s] >= 0)
        def _(s=s):
            middle_ref[s - early] = middle[places[s]]

    correlation, weight[...] = correlate(sums, side)
    score_ref[...] = jnp.zeros(score_ref.shape, F32)
    lane = lax.broadcasted_iota(jnp.int32, (1, 128), 1)
    for s in range(slots):
        home = (here ^ steps[s]) * bin_count + lax.rem(senders[s], bin_count)
        hit = (lane == senders[s] // bin_count) & (places[s] >= 0)
        score_ref[home] = score_ref[home] + jnp.where(hit, correlation[s : s + 1, :], 0.0)

def owner_call(devices, bin_count, steps, defocus, bfactor, references, arrived, early):
    own_bins, side, _ = references.shape
    slots = len(steps)
    late = slots - early[0].shape[0]
    return pl.pallas_call(
        functools.partial(owner_kernel, bin_count, steps),
        out_shape=[
            jax.ShapeDtypeStruct((late, side, side), BF16),
            jax.ShapeDtypeStruct((8, side), F32),
            jax.ShapeDtypeStruct((slots, LABEL_ROWS, 128), F32),
            jax.ShapeDtypeStruct((devices, 1, 128), F32),
        ],
        in_specs=[VMEM] * (3 + len(arrived) + len(early)),
        out_specs=[VMEM] * 4,
        scratch_shapes=[
            pltpu.VMEM((late, side, side), F32),
            pltpu.VMEM((late, side, side), BF16),
            pltpu.VMEM(references.shape, BF16),
            pltpu.VMEM((3, 8, side), F32),
            pltpu.VMEM((2, side, side), F32),
            pltpu.SMEM((INFOS, max(8, own_bins)), jnp.int32),
        ],
        compiler_params=pltpu.CompilerParams(vmem_limit_bytes=VMEM_BYTES),
        name="owner",
    )(defocus, bfactor, references, *arrived, *early)


def last_kernel(
    focus_ref,
    damping_ref,
    weight,
    label_ref,
    early_spectra,
    early_middle,
    late_middle,
    late_ref,
    current_hbm,
    refined_ref,
    spectra,
    middle,
    ctf,
    number,
    info,
    sem,
):
    slots, side, _ = ctf.shape
    own_bins = refined_ref.shape[0]
    early = early_spectra.shape[0]
    labels = [label_ref[s] for s in range(slots)]
    places, _ = read_labels(labels)
    fill_info(info, places, own_bins)

    def unchanged(p):
        return pltpu.make_async_copy(current_hbm.at[p], refined_ref.at[p], sem.at[p])

    @pl.loop(0, own_bins)
    def _(p):
        @pl.when(info[MEMBERS, p] == 0)
        def _():
            unchanged(p).start()

    factors = ctf_factors(labels, focus_ref, damping_ref, side)
    for s in range(slots):

        @pl.when(places[s] >= 0)
        def _(s=s):
            for rows in chunks_of(side):
                ctf[s, rows, :] = ctf_chunk(factors, s, rows)
            if s < early:
                spectra[s] = early_spectra[s]
                middle[places[s]] = early_middle[places[s]]
            else:
                spectra[s] = image_of(late_ref.at[s - early], slice(0, side), side)
                middle[places[s]] = late_middle[s - early]

    update_shared(info, ((ctf, spectra, 0),), weight, number, middle, refined_ref)

    @pl.loop(0, slots)
    def _(s):
        @pl.when(info[ALONE, s] > 0)
        def _():
            p = info[PLACE, s]
            scale = weight[pl.ds(s, 1), :]
            for rows in chunks_of(side):
                values = spectra[s, rows, :].astype(F32)
                term, power, _ = shares(ctf, scale, s, rows, values)
                refined_ref[p, rows, :] = renew(middle[p, rows, :], term, power)

    @pl.loop(0, own_bins)
    def _(p):
        @pl.when(info[MEMBERS, p] == 0)
        def _():
            unchanged(p).wait()


def last_call(defocus, bfactor, references, weight, labels, kept):
    own_bins, side, _ = references.shape
    slots = labels.shape[0]
    return pl.pallas_call(
        last_kernel,
        out_shape=jax.ShapeDtypeStruct(references.shape, BF16),
        in_specs=[VMEM] * 8 + [HBM],
        out_specs=VMEM,
        scratch_shapes=[
            pltpu.VMEM((slots, side, side), BF16),
            pltpu.VMEM(references.shape, BF16),
            pltpu.VMEM((slots, side, side), F32),
            pltpu.VMEM((2, side, side), F32),
            pltpu.SMEM((INFOS, max(8, own_bins)), jnp.int32),
            pltpu.SemaphoreType.DMA((own_bins,)),
        ],
        compiler_params=pltpu.CompilerParams(vmem_limit_bytes=VMEM_BYTES),
        cost_estimate=pl.CostEstimate(flops=4 << 20, bytes_accessed=4 << 20, transcendentals=0),
        name="last",
    )(defocus, bfactor, weight, labels, *kept, in_hbm(references))


def exchange(blocks, axis):
    size = lax.axis_size(axis)
    return [blocks[0]] + [
        lax.ppermute(blocks[k], axis, [(i, i ^ k) for i in range(size)]) for k in range(1, size)
    ]


def body(images, offsets, ctf_group, particle_bin, bin_place, defocus, bfactor, references):
    mic_count = lax.axis_size("mic")
    bin_count = lax.axis_size("bin")
    particles, side, _ = images.shape
    own_bins = references.shape[0]
    capacity = (3 * particles + 2 * mic_count - 1) // (2 * mic_count)

    basis = jnp.asarray(hartley(side), BF16)
    operands = (bin_place, particle_bin, ctf_group, offsets, images, basis)
    operands = tuple(map(in_hbm, operands))
    far = 3 * bin_count // 8
    rest = bin_count - far
    sent_far = home_call(bin_count, own_bins, rest, far, operands)
    sent_near = home_call(bin_count, own_bins, 0, rest, operands, after=(sent_far[-1],))
    arrived = exchange(list(sent_near) + list(sent_far), "bin")

    last = mic_count - 1
    sizes = [[1] * capacity if step == 1 else [capacity] for step in range(mic_count)]
    sent = middle_call(mic_count, sizes, arrived[::-1])
    blocks = [(0, block) for block in sent[0]]
    for step in [t for t in range(1, mic_count) if t != last] + [last]:
        pairs = [(i, i ^ step) for i in range(mic_count)]
        blocks += [(step, lax.ppermute(block, "mic", pairs)) for block in sent[step]]
    steps = [step for step, block in blocks for _ in range(block.shape[0])]
    arrived = [block for _, block in blocks]
    tables = (defocus.reshape(1, -1), bfactor.reshape(1, -1), references)
    early = slice(0, -arrived[-1].shape[0])
    ctf, spectra, early_weight, middle, sums = ready_call(
        bin_count, steps[early], *tables, arrived[:-1]
    )
    late_middle, weight, labels, board = owner_call(
        mic_count * bin_count, bin_count, steps, *tables, arrived, (ctf, spectra, early_weight, sums)
    )
    back = lax.all_to_all(board, ("mic", "bin"), split_axis=0, concat_axis=0, tiled=True)
    refined = last_call(*tables, weight, labels, (spectra, middle, late_middle, arrived[-1]))
    return (refined, jnp.sum(back, axis=(0, 1))[:particles])


def solution(mesh):
    in_specs = (
        P(("mic", "bin"), None, None),
        P(None, ("mic", "bin")),
        P(("mic", "bin")),
        P(("mic", "bin")),
        P(),
        P(),
        P(),
        P(("mic", "bin"), None, None),
    )
    out_specs = (P(("mic", "bin"), None, None), P(("mic", "bin")))
    return jax.shard_map(body, mesh=mesh, in_specs=in_specs, out_specs=out_specs, check_vma=False)
```

```python
import functools
import math

import jax
import jax.numpy as jnp
import numpy as np
from jax import lax
from jax.experimental import pallas as pl
from jax.experimental.pallas import tpu as pltpu
from jax.sharding import PartitionSpec as P

ITERS = 2
PRIOR_WEIGHT = 0.5
EPSILON = 1e-06
CONTRAST = 0.1
AMPLITUDE = math.sqrt(1.0 - CONTRAST * CONTRAST)

LANES = 128
LABEL_ROWS = 8
CHUNK = 32
VMEM_BYTES = 24 * 1024 * 1024

ACTIVE, PLACE, ALONE, MEMBERS, LATE = range(5)
INFOS = 5

F32 = jnp.float32
BF16 = jnp.bfloat16
VMEM = pl.BlockSpec(memory_space=pltpu.VMEM)
SMEM = pl.BlockSpec(memory_space=pltpu.SMEM)
HBM = pl.BlockSpec(memory_space=pltpu.HBM)
ANY = pl.BlockSpec(memory_space=pl.ANY)


def in_hbm(x):
    return pltpu.with_memory_space_constraint(x, pltpu.HBM)


def hartley(side):
    index = np.arange(side)
    angles = (np.outer(index, index) % side).astype(np.float32) * np.float32(2.0 * math.pi / side)
    return (np.cos(angles) + np.sin(angles)) / np.float32(math.sqrt(side))


def label_block(values):
    row = lax.broadcasted_iota(jnp.int32, (LABEL_ROWS, LANES), 0)
    block = jnp.zeros((LABEL_ROWS, LANES), jnp.int32)
    for number, value in enumerate(values):
        block = jnp.where(row == number, value, block)
    return block.astype(F32).astype(BF16)


def home_kernel(
    bin_count, own_bins, first, count, place_hbm, bin_hbm, group_hbm, offset_hbm, image_hbm, basis_hbm, *rest
):
    rest = rest[len(rest) - count - 9 :]
    outs, rest = rest[:count], rest[count:]
    spectra, image_ref, basis_ref, place_ref, bin_ref, group_ref, offset_ref, image_sem, sem = rest
    particles, side = image_ref.shape[0], image_ref.shape[1]
    here = lax.axis_index("bin")
    pairs = (
        (basis_hbm, basis_ref),
        (place_hbm, place_ref),
        (bin_hbm, bin_ref),
        (group_hbm, group_ref),
        (offset_hbm, offset_ref),
    )
    copies = [pltpu.make_async_copy(a, b, sem.at[k]) for k, (a, b) in enumerate(pairs)]
    for copy in copies:
        copy.start()

    def image_copy(i):
        return pltpu.make_async_copy(image_hbm.at[i], image_ref.at[i], image_sem.at[i])

    for i in range(particles):
        image_copy(i).start()
    pieces = side // LANES
    for out in outs:
        out[pieces * side :, :] = jnp.zeros((LABEL_ROWS, LANES), BF16)
    for copy in copies:
        copy.wait()

    @pl.loop(0, particles)
    def _(i):
        image_copy(i).wait()
        place = place_ref[bin_ref[i]]
        owner = place // own_bins
        step_of = lax.rem(owner, bin_count) ^ here

        @pl.when((step_of >= first) & (step_of < first + count))
        def _():
            moved = pltpu.roll(image_ref[i].astype(F32), side - offset_ref[0, i], 0).astype(BF16)
            columns = pltpu.roll(basis_ref[...].astype(F32), offset_ref[1, i], 0).astype(BF16)
            half = jnp.dot(basis_ref[...], moved, preferred_element_type=F32).astype(BF16)
            spectra[...] = jnp.dot(half, columns, preferred_element_type=F32).astype(BF16)
            labels = label_block(
                (
                    1 + owner // bin_count,
                    lax.rem(place, own_bins),
                    group_ref[i],
                    i * bin_count + here,
                )
            )
            for k in range(count):

                @pl.when(step_of == first + k)
                def _():
                    for n in range(pieces):
                        outs[k][n * side : (n + 1) * side, :] = spectra[
                            :, n * LANES : (n + 1) * LANES
                        ]
                    outs[k][pieces * side :, :] = labels


def home_call(bin_count, own_bins, first, count, operands, after=()):
    images, particles, side = operands[4], operands[4].shape[0], operands[4].shape[1]
    return pl.pallas_call(
        functools.partial(home_kernel, bin_count, own_bins, first, count),
        out_shape=[
            jax.ShapeDtypeStruct((side * side // LANES + LABEL_ROWS, LANES), BF16)
        ]
        * count,
        in_specs=[HBM] * 6 + [ANY] * len(after),
        out_specs=[VMEM] * count,
        scratch_shapes=[
            pltpu.VMEM((side, side), BF16),
            pltpu.VMEM(images.shape, BF16),
            pltpu.VMEM((side, side), BF16),
        ]
        + [pltpu.SMEM(x.shape, jnp.int32) for x in operands[:4]]
        + [pltpu.SemaphoreType.DMA((particles,)), pltpu.SemaphoreType.DMA((5,))],
        compiler_params=pltpu.CompilerParams(vmem_limit_bytes=VMEM_BYTES),
        name="home",
    )(*operands, *after)


def middle_kernel(mic_count, sizes, *rest):
    arrived, flat = rest[: len(rest) - sum(map(len, sizes))], list(rest[-sum(map(len, sizes)) :])
    outs = [[flat.pop(0) for _ in parts] for parts in sizes]
    rows = arrived[0].shape[0]
    here = lax.axis_index("mic")
    empty = jnp.zeros((LABEL_ROWS, LANES), BF16)
    for out in sum(outs, []):
        for j in range(out.shape[0]):
            out[j, rows - LABEL_ROWS : rows, :] = empty
    targets = [
        jnp.max(block[rows - LABEL_ROWS : rows, :].astype(F32)[0:1]).astype(jnp.int32)
        for block in arrived
    ]
    counts = [jnp.int32(0)] * mic_count
    for block, target in zip(arrived, targets):
        step_of = (target - 1) ^ here
        for step in range(mic_count):
            chosen = (target > 0) & (step_of == step)
            if len(outs[step]) == 1:

                @pl.when(chosen)
                def _(block=block, out=outs[step][0], slot=counts[step]):
                    out[slot] = block[...]

            else:
                for j, out in enumerate(outs[step]):

                    @pl.when(chosen & (counts[step] == j))
                    def _(block=block, out=out):
                        out[0] = block[...]

            counts[step] = counts[step] + chosen.astype(jnp.int32)


def middle_call(mic_count, sizes, arrived):
    flat = sum(sizes, [])
    outs = pl.pallas_call(
        functools.partial(middle_kernel, mic_count, sizes),
        out_shape=[jax.ShapeDtypeStruct((n, *arrived[0].shape), BF16) for n in flat],
        in_specs=[VMEM] * len(arrived),
        out_specs=[VMEM] * len(flat),
        compiler_params=pltpu.CompilerParams(vmem_limit_bytes=VMEM_BYTES),
        name="middle",
    )(*arrived)
    outs = list(outs)
    return [[outs.pop(0) for _ in parts] for parts in sizes]


def fold(values):
    return jnp.sum(values.reshape(values.shape[0] // 8, 8, values.shape[1]), axis=0)


def chunks_of(side):
    return [slice(c, c + CHUNK) for c in range(0, side, CHUNK)]


def shares(ctf, weight, s, rows, values):
    table = ctf[s, rows, :]
    scaled = weight * table
    return (scaled * values).astype(BF16).astype(F32), scaled * table, table


def renew(previous, numerator, denominator):
    return (
        (numerator + PRIOR_WEIGHT * previous.astype(F32)) / (denominator + PRIOR_WEIGHT)
    ).astype(BF16)


def update_shared(info, groups, weight, number, source, target, kind=MEMBERS):
    chunks = chunks_of(source.shape[1])

    @pl.loop(0, source.shape[0])
    def _(p):
        @pl.when((info[MEMBERS, p] > 1) & (info[kind, p] > 0))
        def _():
            number[...] = jnp.zeros(number.shape, F32)
            for ctf, spectra, first in groups:

                @pl.loop(0, spectra.shape[0])
                def _(k):
                    @pl.when((info[ACTIVE, first + k] > 0) & (info[PLACE, first + k] == p))
                    def _():
                        scale = weight[pl.ds(first + k, 1), :]
                        for rows in chunks:
                            values = spectra[k, rows, :].astype(F32)
                            term, power, _ = shares(ctf, scale, k, rows, values)
                            number[0, rows, :] += term
                            number[1, rows, :] += power

            for rows in chunks:
                target[p, rows, :] = renew(
                    source[p, rows, :], number[0, rows, :], number[1, rows, :]
                )


def read_labels(labels):
    places, senders = [], []
    for block in labels:
        code = block[1:2] + 256.0 * block[3:4]
        code = jnp.max(jnp.where(block[0:1] > 0, code, -1.0)).astype(jnp.int32)
        places.append(jnp.where(code < 0, -1, code & 255))
        senders.append(jnp.maximum(code, 0) >> 8)
    return places, senders


def fill_info(info, places, own_bins, late=0):
    for p in range(own_bins):
        info[MEMBERS, p] = jnp.int32(0)
        info[LATE, p] = jnp.int32(0)
    for s, place in enumerate(places):
        active = (place >= 0).astype(jnp.int32)
        place = jnp.maximum(place, 0)
        info[ACTIVE, s] = active
        info[PLACE, s] = place
        info[MEMBERS, place] = info[MEMBERS, place] + active
        if s >= len(places) - late:
            info[LATE, place] = info[LATE, place] + active
    for s, place in enumerate(places):
        single = (place >= 0) & (info[MEMBERS, jnp.maximum(place, 0)] == 1)
        info[ALONE, s] = single.astype(jnp.int32)


def ctf_factors(labels, focus_ref, damping_ref, side):
    groups = focus_ref.shape[1]
    group = jnp.concatenate([x[2:3, :groups] for x in labels] + [labels[0][4:5, :groups]] * 8)[:8]
    chosen = group.astype(jnp.int32) == lax.broadcasted_iota(jnp.int32, (8, groups), 1)
    focus = jnp.sum(jnp.where(chosen, focus_ref[...], 0.0), axis=1, keepdims=True)
    damping = jnp.sum(jnp.where(chosen, damping_ref[...], 0.0), axis=1, keepdims=True)
    frequency = lax.broadcasted_iota(jnp.int32, (8, side), 1)
    folded = jnp.minimum(frequency, side - frequency).astype(F32) / (side / 2.0)
    square = folded * folded
    envelope = jnp.exp(-damping * square)
    sine = jnp.sin(focus * square) * envelope
    cosine = jnp.cos(focus * square) * envelope
    by_sine = jnp.transpose(CONTRAST * sine - AMPLITUDE * cosine)
    by_cosine = jnp.transpose(-(AMPLITUDE * sine + CONTRAST * cosine))
    return by_sine, sine, by_cosine, cosine


def ctf_chunk(factors, s, rows):
    by_sine, sine, by_cosine, cosine = factors
    return (
        by_sine[rows, s : s + 1] * sine[s : s + 1, :]
        + by_cosine[rows, s : s + 1] * cosine[s : s + 1, :]
    )


def blocks_of(arrived):
    return [block.at[j] for block in arrived for j in range(block.shape[0])]


def image_of(block, rows, side):
    lefts = range(0, side * side // LANES, side)
    return jnp.concatenate([block[n + rows.start : n + rows.stop, :] for n in lefts], axis=1)


def labels_of(blocks):
    return [block[block.shape[0] - LABEL_ROWS :, :].astype(F32) for block in blocks]


def first_compare(p, factors, current_ref, group, sums, s, block):
    ctf, spectra, first = group
    side = ctf.shape[1]
    cross = model = data = jnp.zeros((8, side), F32)
    for rows in chunks_of(side):
        table = ctf_chunk(factors, s, rows)
        ctf[s - first, rows, :] = table
        held = image_of(block, rows, side)
        spectra[s - first, rows, :] = held
        values = held.astype(F32)
        predicted = table * current_ref[p, rows, :].astype(F32)
        cross = cross + fold(predicted * values)
        model = model + fold(predicted * predicted)
        data = data + fold(values * values)
    for k, total in enumerate((cross, model, data)):
        sums[k, s : s + 1, :] = jnp.sum(total, axis=0, keepdims=True)


def correlate(sums, side):
    pixels = float(side * side)
    cross, model, data = (jnp.sum(sums[k], axis=1, keepdims=True) / pixels for k in range(3))
    correlation = cross / jnp.sqrt((model + EPSILON) * (data + EPSILON))
    weights = 1.0 / (1.0 + jnp.exp(-float(side) * correlation))
    return correlation, jnp.broadcast_to(weights.astype(BF16).astype(F32), (8, side))


def second_compare(group, k, reference_of):
    ctf, spectra, _ = group
    side = ctf.shape[1]
    cross = model = jnp.zeros((8, side), F32)
    for rows in chunks_of(side):
        values = spectra[k, rows, :].astype(F32)
        reference = reference_of(rows, values)
        predicted = ctf[k, rows, :] * reference.astype(F32)
        cross = cross + fold(predicted * values)
        model = model + fold(predicted * predicted)
    return cross, model


def update_and_compare(s, p, alone, shared, group, weight, sums, source, target):
    ctf, spectra, first = group
    k = s - first

    def keep(cross, model):
        sums[0, pl.ds(s, 1), :] = jnp.sum(cross, axis=0, keepdims=True)
        sums[1, pl.ds(s, 1), :] = jnp.sum(model, axis=0, keepdims=True)

    @pl.when(alone)
    def _():
        scale = weight[pl.ds(s, 1), :]

        def new(rows, values):
            term, power, _ = shares(ctf, scale, k, rows, values)
            reference = renew(source[p, rows, :], term, power)
            target[p, rows, :] = reference
            return reference

        keep(*second_compare(group, k, new))

    @pl.when(shared)
    def _():
        keep(*second_compare(group, k, lambda rows, _: target[p, rows, :]))


def ready_kernel(bin_count, steps, focus_ref, damping_ref, current_ref, *rest):
    blocks, rest = blocks_of(rest[:-7]), rest[-7:]
    ctf, spectra, weight, middle, sums, number, info = rest
    own_bins, side, _ = current_ref.shape
    labels = labels_of(blocks)
    fill_info(info, read_labels(labels)[0], own_bins)
    factors = ctf_factors(labels, focus_ref, damping_ref, side)
    sums[...] = jnp.zeros(sums.shape, F32)
    group = (ctf, spectra, 0)
    for s in range(len(labels)):

        @pl.when(info[ACTIVE, s] > 0)
        def _(s=s):
            first_compare(info[PLACE, s], factors, current_ref, group, sums, s, blocks[s])

    weight[...] = correlate(sums, side)[1]
    update_shared(info, (group,), weight, number, current_ref, middle)

    @pl.loop(0, len(labels))
    def _(s):
        alone = info[ALONE, s] > 0
        shared = (info[ACTIVE, s] > 0) & (info[ALONE, s] == 0)
        p = info[PLACE, s]
        update_and_compare(s, p, alone, shared, group, weight, sums, current_ref, middle)


def ready_call(bin_count, steps, defocus, bfactor, references, arrived):
    own_bins, side, _ = references.shape
    slots = len(steps)
    return pl.pallas_call(
        functools.partial(ready_kernel, bin_count, steps),
        out_shape=[
            jax.ShapeDtypeStruct((slots, side, side), F32),
            jax.ShapeDtypeStruct((slots, side, side), BF16),
            jax.ShapeDtypeStruct((8, side), F32),
            jax.ShapeDtypeStruct(references.shape, BF16),
            jax.ShapeDtypeStruct((3, 8, side), F32),
        ],
        in_specs=[VMEM] * (3 + len(arrived)),
        out_specs=[VMEM] * 5,
        scratch_shapes=[
            pltpu.VMEM((2, side, side), F32),
            pltpu.SMEM((INFOS, max(8, own_bins)), jnp.int32),
        ],
        compiler_params=pltpu.CompilerParams(vmem_limit_bytes=VMEM_BYTES),
        name="ready",
    )(defocus, bfactor, references, *arrived)


def owner_kernel(bin_count, steps, focus_ref, damping_ref, current_ref, *rest):
    blocks, rest = blocks_of(rest[:-14]), rest[-14:]
    early_ctf, early_spectra, early_weight, early_sums = rest[:4]
    middle_ref, weight, label_ref, score_ref = rest[4:8]
    ctf, spectra, middle, sums, number, info = rest[8:]
    own_bins, side, _ = current_ref.shape
    early = early_ctf.shape[0]
    slots = len(steps)
    here = lax.axis_index("mic")

    labels = labels_of(blocks)
    for s, label in enumerate(labels):
        label_ref[s] = label
    places, senders = read_labels(labels)
    factors = ctf_factors(labels, focus_ref, damping_ref, side)
    sums[...] = early_sums[...]
    early_group, late_group = (early_ctf, early_spectra, 0), (ctf, spectra, early)
    shared = {}
    for s in range(early, slots):
        active = places[s] >= 0
        others = [places[t] == places[s] for t in range(slots) if t != s]
        shared[s] = active & functools.reduce(jnp.logical_or, others)

        @pl.when(active)
        def _(s=s):
            first_compare(places[s], factors, current_ref, late_group, sums, s, blocks[s])

    row = lax.broadcasted_iota(jnp.int32, (8, side), 0)
    weight[...] = jnp.where(row < early, early_weight[...], correlate(sums, side)[1])
    any_shared = functools.reduce(jnp.logical_or, shared.values())

    @pl.when(any_shared)
    def _():
        fill_info(info, places, own_bins, slots - early)
        update_shared(
            info, (early_group, late_group), weight, number, current_ref, middle, kind=LATE
        )

        @pl.loop(0, early)
        def _(s):
            p = info[PLACE, s]

            @pl.when((info[ACTIVE, s] > 0) & (info[LATE, p] > 0))
            def _():
                cross, model = second_compare(early_group, s, lambda rows, _: middle[p, rows, :])
                sums[0, pl.ds(s, 1), :] = jnp.sum(cross, axis=0, keepdims=True)
                sums[1, pl.ds(s, 1), :] = jnp.sum(model, axis=0, keepdims=True)

    for s in range(early, slots):
        alone = (places[s] >= 0) & jnp.logical_not(shared[s])
        update_and_compare(
            s, places[s], alone, shared[s], late_group, weight, sums, current_ref, middle
        )

    for s in range(early, slots):

        @pl.when(places[s] >= 0)
        def _(s=s):
            middle_ref[s - early] = middle[places[s]]

    correlation, weight[...] = correlate(sums, side)
    score_ref[...] = jnp.zeros(score_ref.shape, F32)
    lane = lax.broadcasted_iota(jnp.int32, (1, 128), 1)
    for s in range(slots):
        home = (here ^ steps[s]) * bin_count + lax.rem(senders[s], bin_count)
        hit = (lane == senders[s] // bin_count) & (places[s] >= 0)
        score_ref[home] = score_ref[home] + jnp.where(hit, correlation[s : s + 1, :], 0.0)

def owner_call(devices, bin_count, steps, defocus, bfactor, references, arrived, early):
    own_bins, side, _ = references.shape
    slots = len(steps)
    late = slots - early[0].shape[0]
    return pl.pallas_call(
        functools.partial(owner_kernel, bin_count, steps),
        out_shape=[
            jax.ShapeDtypeStruct((late, side, side), BF16),
            jax.ShapeDtypeStruct((8, side), F32),
            jax.ShapeDtypeStruct((slots, LABEL_ROWS, 128), F32),
            jax.ShapeDtypeStruct((devices, 1, 128), F32),
        ],
        in_specs=[VMEM] * (3 + len(arrived) + len(early)),
        out_specs=[VMEM] * 4,
        scratch_shapes=[
            pltpu.VMEM((late, side, side), F32),
            pltpu.VMEM((late, side, side), BF16),
            pltpu.VMEM(references.shape, BF16),
            pltpu.VMEM((3, 8, side), F32),
            pltpu.VMEM((2, side, side), F32),
            pltpu.SMEM((INFOS, max(8, own_bins)), jnp.int32),
        ],
        compiler_params=pltpu.CompilerParams(vmem_limit_bytes=VMEM_BYTES),
        name="owner",
    )(defocus, bfactor, references, *arrived, *early)


def last_kernel(
    focus_ref,
    damping_ref,
    weight,
    label_ref,
    early_spectra,
    early_middle,
    late_middle,
    late_ref,
    current_hbm,
    refined_ref,
    spectra,
    middle,
    ctf,
    number,
    info,
    sem,
):
    slots, side, _ = ctf.shape
    own_bins = refined_ref.shape[0]
    early = early_spectra.shape[0]
    labels = [label_ref[s] for s in range(slots)]
    places, _ = read_labels(labels)
    fill_info(info, places, own_bins)

    def unchanged(p):
        return pltpu.make_async_copy(current_hbm.at[p], refined_ref.at[p], sem.at[p])

    @pl.loop(0, own_bins)
    def _(p):
        @pl.when(info[MEMBERS, p] == 0)
        def _():
            unchanged(p).start()

    factors = ctf_factors(labels, focus_ref, damping_ref, side)
    for s in range(slots):

        @pl.when(places[s] >= 0)
        def _(s=s):
            for rows in chunks_of(side):
                ctf[s, rows, :] = ctf_chunk(factors, s, rows)
            if s < early:
                spectra[s] = early_spectra[s]
                middle[places[s]] = early_middle[places[s]]
            else:
                spectra[s] = image_of(late_ref.at[s - early], slice(0, side), side)
                middle[places[s]] = late_middle[s - early]

    update_shared(info, ((ctf, spectra, 0),), weight, number, middle, refined_ref)

    @pl.loop(0, slots)
    def _(s):
        @pl.when(info[ALONE, s] > 0)
        def _():
            p = info[PLACE, s]
            scale = weight[pl.ds(s, 1), :]
            for rows in chunks_of(side):
                values = spectra[s, rows, :].astype(F32)
                term, power, _ = shares(ctf, scale, s, rows, values)
                refined_ref[p, rows, :] = renew(middle[p, rows, :], term, power)

    @pl.loop(0, own_bins)
    def _(p):
        @pl.when(info[MEMBERS, p] == 0)
        def _():
            unchanged(p).wait()


def last_call(defocus, bfactor, references, weight, labels, kept):
    own_bins, side, _ = references.shape
    slots = labels.shape[0]
    return pl.pallas_call(
        last_kernel,
        out_shape=jax.ShapeDtypeStruct(references.shape, BF16),
        in_specs=[VMEM] * 8 + [HBM],
        out_specs=VMEM,
        scratch_shapes=[
            pltpu.VMEM((slots, side, side), BF16),
            pltpu.VMEM(references.shape, BF16),
            pltpu.VMEM((slots, side, side), F32),
            pltpu.VMEM((2, side, side), F32),
            pltpu.SMEM((INFOS, max(8, own_bins)), jnp.int32),
            pltpu.SemaphoreType.DMA((own_bins,)),
        ],
        compiler_params=pltpu.CompilerParams(vmem_limit_bytes=VMEM_BYTES),
        cost_estimate=pl.CostEstimate(flops=4 << 20, bytes_accessed=4 << 20, transcendentals=0),
        name="last",
    )(defocus, bfactor, weight, labels, *kept, in_hbm(references))


def exchange(blocks, axis):
    size = lax.axis_size(axis)
    return [blocks[0]] + [
        lax.ppermute(blocks[k], axis, [(i, i ^ k) for i in range(size)]) for k in range(1, size)
    ]


def body(images, offsets, ctf_group, particle_bin, bin_place, defocus, bfactor, references):
    mic_count = lax.axis_size("mic")
    bin_count = lax.axis_size("bin")
    particles, side, _ = images.shape
    own_bins = references.shape[0]
    capacity = (3 * particles + 2 * mic_count - 1) // (2 * mic_count)

    basis = jnp.asarray(hartley(side), BF16)
    operands = (bin_place, particle_bin, ctf_group, offsets, images, basis)
    operands = tuple(map(in_hbm, operands))
    far = bin_count // 4
    rest = bin_count - far
    sent_far = home_call(bin_count, own_bins, rest, far, operands)
    sent_near = home_call(bin_count, own_bins, 0, rest, operands, after=(sent_far[-1],))
    arrived = exchange(list(sent_near) + list(sent_far), "bin")

    last = mic_count - 1
    sizes = [[1] * capacity if step == 1 else [capacity] for step in range(mic_count)]
    sent = middle_call(mic_count, sizes, arrived[::-1])
    blocks = [(0, block) for block in sent[0]]
    for step in [t for t in range(1, mic_count) if t != last] + [last]:
        pairs = [(i, i ^ step) for i in range(mic_count)]
        blocks += [(step, lax.ppermute(block, "mic", pairs)) for block in sent[step]]
    steps = [step for step, block in blocks for _ in range(block.shape[0])]
    arrived = [block for _, block in blocks]
    tables = (defocus.reshape(1, -1), bfactor.reshape(1, -1), references)
    early = slice(0, -arrived[-1].shape[0])
    ctf, spectra, early_weight, middle, sums = ready_call(
        bin_count, steps[early], *tables, arrived[:-1]
    )
    late_middle, weight, labels, board = owner_call(
        mic_count * bin_count, bin_count, steps, *tables, arrived, (ctf, spectra, early_weight, sums)
    )
    back = lax.all_to_all(board, ("mic", "bin"), split_axis=0, concat_axis=0, tiled=True)
    refined = last_call(*tables, weight, labels, (spectra, middle, late_middle, arrived[-1]))
    return (refined, jnp.sum(back, axis=(0, 1))[:particles])


def solution(mesh):
    in_specs = (
        P(("mic", "bin"), None, None),
        P(None, ("mic", "bin")),
        P(("mic", "bin")),
        P(("mic", "bin")),
        P(),
        P(),
        P(),
        P(("mic", "bin"), None, None),
    )
    out_specs = (P(("mic", "bin"), None, None), P(("mic", "bin")))
    return jax.shard_map(body, mesh=mesh, in_specs=in_specs, out_specs=out_specs, check_vma=False)
```

```python
import functools
import math

import jax
import jax.numpy as jnp
import numpy as np
from jax import lax
from jax.experimental import pallas as pl
from jax.experimental.pallas import tpu as pltpu
from jax.sharding import PartitionSpec as P

ITERS = 2
PRIOR_WEIGHT = 0.5
EPSILON = 1e-06
CONTRAST = 0.1
AMPLITUDE = math.sqrt(1.0 - CONTRAST * CONTRAST)

LANES = 128
LABEL_ROWS = 8
CHUNK = 32
VMEM_BYTES = 24 * 1024 * 1024

ACTIVE, PLACE, ALONE, MEMBERS, LATE = range(5)
INFOS = 5

F32 = jnp.float32
BF16 = jnp.bfloat16
VMEM = pl.BlockSpec(memory_space=pltpu.VMEM)
SMEM = pl.BlockSpec(memory_space=pltpu.SMEM)
HBM = pl.BlockSpec(memory_space=pltpu.HBM)
ANY = pl.BlockSpec(memory_space=pl.ANY)


def in_hbm(x):
    return pltpu.with_memory_space_constraint(x, pltpu.HBM)


def hartley(side):
    index = np.arange(side)
    angles = (np.outer(index, index) % side).astype(np.float32) * np.float32(2.0 * math.pi / side)
    return (np.cos(angles) + np.sin(angles)) / np.float32(math.sqrt(side))


def label_block(values):
    row = lax.broadcasted_iota(jnp.int32, (LABEL_ROWS, LANES), 0)
    block = jnp.zeros((LABEL_ROWS, LANES), jnp.int32)
    for number, value in enumerate(values):
        block = jnp.where(row == number, value, block)
    return block.astype(F32).astype(BF16)


def home_kernel(
    bin_count, own_bins, first, count, place_hbm, bin_hbm, group_hbm, offset_hbm, image_hbm, basis_hbm, *rest
):
    rest = rest[len(rest) - count - 9 :]
    outs, rest = rest[:count], rest[count:]
    spectra, image_ref, basis_ref, place_ref, bin_ref, group_ref, offset_ref, image_sem, sem = rest
    particles, side = image_ref.shape[0], image_ref.shape[1]
    here = lax.axis_index("bin")
    pairs = (
        (basis_hbm, basis_ref),
        (place_hbm, place_ref),
        (bin_hbm, bin_ref),
        (group_hbm, group_ref),
        (offset_hbm, offset_ref),
    )
    copies = [pltpu.make_async_copy(a, b, sem.at[k]) for k, (a, b) in enumerate(pairs)]
    for copy in copies:
        copy.start()

    def image_copy(i):
        return pltpu.make_async_copy(image_hbm.at[i], image_ref.at[i], image_sem.at[i])

    for i in range(particles):
        image_copy(i).start()
    pieces = side // LANES
    for out in outs:
        out[pieces * side :, :] = jnp.zeros((LABEL_ROWS, LANES), BF16)
    for copy in copies:
        copy.wait()

    @pl.loop(0, particles)
    def _(i):
        image_copy(i).wait()
        place = place_ref[bin_ref[i]]
        owner = place // own_bins
        step_of = lax.rem(owner, bin_count) ^ here

        @pl.when((step_of >= first) & (step_of < first + count))
        def _():
            moved = pltpu.roll(image_ref[i].astype(F32), side - offset_ref[0, i], 0).astype(BF16)
            columns = pltpu.roll(basis_ref[...].astype(F32), offset_ref[1, i], 0).astype(BF16)
            half = jnp.dot(basis_ref[...], moved, preferred_element_type=F32).astype(BF16)
            spectra[...] = jnp.dot(half, columns, preferred_element_type=F32).astype(BF16)
            labels = label_block(
                (
                    1 + owner // bin_count,
                    lax.rem(place, own_bins),
                    group_ref[i],
                    i * bin_count + here,
                )
            )
            for k in range(count):

                @pl.when(step_of == first + k)
                def _():
                    for n in range(pieces):
                        outs[k][n * side : (n + 1) * side, :] = spectra[
                            :, n * LANES : (n + 1) * LANES
                        ]
                    outs[k][pieces * side :, :] = labels


def home_call(bin_count, own_bins, first, count, operands, after=()):
    images, particles, side = operands[4], operands[4].shape[0], operands[4].shape[1]
    return pl.pallas_call(
        functools.partial(home_kernel, bin_count, own_bins, first, count),
        out_shape=[
            jax.ShapeDtypeStruct((side * side // LANES + LABEL_ROWS, LANES), BF16)
        ]
        * count,
        in_specs=[HBM] * 6 + [ANY] * len(after),
        out_specs=[VMEM] * count,
        scratch_shapes=[
            pltpu.VMEM((side, side), BF16),
            pltpu.VMEM(images.shape, BF16),
            pltpu.VMEM((side, side), BF16),
        ]
        + [pltpu.SMEM(x.shape, jnp.int32) for x in operands[:4]]
        + [pltpu.SemaphoreType.DMA((particles,)), pltpu.SemaphoreType.DMA((5,))],
        compiler_params=pltpu.CompilerParams(vmem_limit_bytes=VMEM_BYTES),
        name="home",
    )(*operands, *after)


def middle_kernel(mic_count, sizes, *rest):
    arrived, flat = rest[: len(rest) - sum(map(len, sizes))], list(rest[-sum(map(len, sizes)) :])
    outs = [[flat.pop(0) for _ in parts] for parts in sizes]
    rows = arrived[0].shape[0]
    here = lax.axis_index("mic")
    empty = jnp.zeros((LABEL_ROWS, LANES), BF16)
    for out in sum(outs, []):
        for j in range(out.shape[0]):
            out[j, rows - LABEL_ROWS : rows, :] = empty
    targets = [
        jnp.max(block[rows - LABEL_ROWS : rows, :].astype(F32)[0:1]).astype(jnp.int32)
        for block in arrived
    ]
    counts = [jnp.int32(0)] * mic_count
    for block, target in zip(arrived, targets):
        step_of = (target - 1) ^ here

        @pl.when(target > 0)
        def _(block=block, step_of=step_of, counts=tuple(counts)):
            for step in range(mic_count):
                if len(outs[step]) == 1:

                    @pl.when(step_of == step)
                    def _(step=step):
                        outs[step][0][counts[step]] = block[...]

                else:
                    for j, out in enumerate(outs[step]):

                        @pl.when((step_of == step) & (counts[step] == j))
                        def _(out=out):
                            out[0] = block[...]

        for step in range(mic_count):
            chosen = (target > 0) & (step_of == step)
            counts[step] = counts[step] + chosen.astype(jnp.int32)


def middle_call(mic_count, sizes, arrived):
    flat = sum(sizes, [])
    outs = pl.pallas_call(
        functools.partial(middle_kernel, mic_count, sizes),
        out_shape=[jax.ShapeDtypeStruct((n, *arrived[0].shape), BF16) for n in flat],
        in_specs=[VMEM] * len(arrived),
        out_specs=[VMEM] * len(flat),
        compiler_params=pltpu.CompilerParams(vmem_limit_bytes=VMEM_BYTES),
        name="middle",
    )(*arrived)
    outs = list(outs)
    return [[outs.pop(0) for _ in parts] for parts in sizes]


def fold(values):
    return jnp.sum(values.reshape(values.shape[0] // 8, 8, values.shape[1]), axis=0)


def chunks_of(side):
    return [slice(c, c + CHUNK) for c in range(0, side, CHUNK)]


def shares(ctf, weight, s, rows, values):
    table = ctf[s, rows, :]
    scaled = weight * table
    return (scaled * values).astype(BF16).astype(F32), scaled * table, table


def renew(previous, numerator, denominator):
    return (
        (numerator + PRIOR_WEIGHT * previous.astype(F32)) / (denominator + PRIOR_WEIGHT)
    ).astype(BF16)


def update_shared(info, groups, weight, number, source, target, kind=MEMBERS):
    chunks = chunks_of(source.shape[1])

    @pl.loop(0, source.shape[0])
    def _(p):
        @pl.when((info[MEMBERS, p] > 1) & (info[kind, p] > 0))
        def _():
            number[...] = jnp.zeros(number.shape, F32)
            for ctf, spectra, first in groups:

                @pl.loop(0, spectra.shape[0])
                def _(k):
                    @pl.when((info[ACTIVE, first + k] > 0) & (info[PLACE, first + k] == p))
                    def _():
                        scale = weight[pl.ds(first + k, 1), :]
                        for rows in chunks:
                            values = spectra[k, rows, :].astype(F32)
                            term, power, _ = shares(ctf, scale, k, rows, values)
                            number[0, rows, :] += term
                            number[1, rows, :] += power

            for rows in chunks:
                target[p, rows, :] = renew(
                    source[p, rows, :], number[0, rows, :], number[1, rows, :]
                )


def read_labels(labels):
    places, senders = [], []
    for block in labels:
        code = block[1:2] + 256.0 * block[3:4]
        code = jnp.max(jnp.where(block[0:1] > 0, code, -1.0)).astype(jnp.int32)
        places.append(jnp.where(code < 0, -1, code & 255))
        senders.append(jnp.maximum(code, 0) >> 8)
    return places, senders


def fill_info(info, places, own_bins, late=0):
    for p in range(own_bins):
        info[MEMBERS, p] = jnp.int32(0)
        info[LATE, p] = jnp.int32(0)
    for s, place in enumerate(places):
        active = (place >= 0).astype(jnp.int32)
        place = jnp.maximum(place, 0)
        info[ACTIVE, s] = active
        info[PLACE, s] = place
        info[MEMBERS, place] = info[MEMBERS, place] + active
        if s >= len(places) - late:
            info[LATE, place] = info[LATE, place] + active
    for s, place in enumerate(places):
        single = (place >= 0) & (info[MEMBERS, jnp.maximum(place, 0)] == 1)
        info[ALONE, s] = single.astype(jnp.int32)


def ctf_factors(labels, focus_ref, damping_ref, side):
    groups = focus_ref.shape[1]
    group = jnp.concatenate([x[2:3, :groups] for x in labels] + [labels[0][4:5, :groups]] * 8)[:8]
    chosen = group.astype(jnp.int32) == lax.broadcasted_iota(jnp.int32, (8, groups), 1)
    focus = jnp.sum(jnp.where(chosen, focus_ref[...], 0.0), axis=1, keepdims=True)
    damping = jnp.sum(jnp.where(chosen, damping_ref[...], 0.0), axis=1, keepdims=True)
    frequency = lax.broadcasted_iota(jnp.int32, (8, side), 1)
    folded = jnp.minimum(frequency, side - frequency).astype(F32) / (side / 2.0)
    square = folded * folded
    envelope = jnp.exp(-damping * square)
    sine = jnp.sin(focus * square) * envelope
    cosine = jnp.cos(focus * square) * envelope
    by_sine = jnp.transpose(CONTRAST * sine - AMPLITUDE * cosine)
    by_cosine = jnp.transpose(-(AMPLITUDE * sine + CONTRAST * cosine))
    return by_sine, sine, by_cosine, cosine


def ctf_chunk(factors, s, rows):
    by_sine, sine, by_cosine, cosine = factors
    return (
        by_sine[rows, s : s + 1] * sine[s : s + 1, :]
        + by_cosine[rows, s : s + 1] * cosine[s : s + 1, :]
    )


def blocks_of(arrived):
    return [block.at[j] for block in arrived for j in range(block.shape[0])]


def image_of(block, rows, side):
    lefts = range(0, side * side // LANES, side)
    return jnp.concatenate([block[n + rows.start : n + rows.stop, :] for n in lefts], axis=1)


def labels_of(blocks):
    return [block[block.shape[0] - LABEL_ROWS :, :].astype(F32) for block in blocks]


def first_compare(p, factors, current_ref, group, sums, s, block):
    ctf, spectra, first = group
    side = ctf.shape[1]
    cross = model = data = jnp.zeros((8, side), F32)
    for rows in chunks_of(side):
        table = ctf_chunk(factors, s, rows)
        ctf[s - first, rows, :] = table
        held = image_of(block, rows, side)
        spectra[s - first, rows, :] = held
        values = held.astype(F32)
        predicted = table * current_ref[p, rows, :].astype(F32)
        cross = cross + fold(predicted * values)
        model = model + fold(predicted * predicted)
        data = data + fold(values * values)
    for k, total in enumerate((cross, model, data)):
        sums[k, s : s + 1, :] = jnp.sum(total, axis=0, keepdims=True)


def correlate(sums, side):
    pixels = float(side * side)
    cross, model, data = (jnp.sum(sums[k], axis=1, keepdims=True) / pixels for k in range(3))
    correlation = cross / jnp.sqrt((model + EPSILON) * (data + EPSILON))
    weights = 1.0 / (1.0 + jnp.exp(-float(side) * correlation))
    return correlation, jnp.broadcast_to(weights.astype(BF16).astype(F32), (8, side))


def second_compare(group, k, reference_of):
    ctf, spectra, _ = group
    side = ctf.shape[1]
    cross = model = jnp.zeros((8, side), F32)
    for rows in chunks_of(side):
        values = spectra[k, rows, :].astype(F32)
        reference = reference_of(rows, values)
        predicted = ctf[k, rows, :] * reference.astype(F32)
        cross = cross + fold(predicted * values)
        model = model + fold(predicted * predicted)
    return cross, model


def update_and_compare(s, p, alone, shared, group, weight, sums, source, target):
    ctf, spectra, first = group
    k = s - first

    def keep(cross, model):
        sums[0, pl.ds(s, 1), :] = jnp.sum(cross, axis=0, keepdims=True)
        sums[1, pl.ds(s, 1), :] = jnp.sum(model, axis=0, keepdims=True)

    @pl.when(alone)
    def _():
        scale = weight[pl.ds(s, 1), :]

        def new(rows, values):
            term, power, _ = shares(ctf, scale, k, rows, values)
            reference = renew(source[p, rows, :], term, power)
            target[p, rows, :] = reference
            return reference

        keep(*second_compare(group, k, new))

    @pl.when(shared)
    def _():
        keep(*second_compare(group, k, lambda rows, _: target[p, rows, :]))


def ready_kernel(bin_count, steps, focus_ref, damping_ref, current_ref, *rest):
    blocks, rest = blocks_of(rest[:-7]), rest[-7:]
    ctf, spectra, weight, middle, sums, number, info = rest
    own_bins, side, _ = current_ref.shape
    labels = labels_of(blocks)
    fill_info(info, read_labels(labels)[0], own_bins)
    factors = ctf_factors(labels, focus_ref, damping_ref, side)
    sums[...] = jnp.zeros(sums.shape, F32)
    group = (ctf, spectra, 0)
    for s in range(len(labels)):

        @pl.when(info[ACTIVE, s] > 0)
        def _(s=s):
            first_compare(info[PLACE, s], factors, current_ref, group, sums, s, blocks[s])

    weight[...] = correlate(sums, side)[1]
    update_shared(info, (group,), weight, number, current_ref, middle)

    @pl.loop(0, len(labels))
    def _(s):
        alone = info[ALONE, s] > 0
        shared = (info[ACTIVE, s] > 0) & (info[ALONE, s] == 0)
        p = info[PLACE, s]
        update_and_compare(s, p, alone, shared, group, weight, sums, current_ref, middle)


def ready_call(bin_count, steps, defocus, bfactor, references, arrived):
    own_bins, side, _ = references.shape
    slots = len(steps)
    return pl.pallas_call(
        functools.partial(ready_kernel, bin_count, steps),
        out_shape=[
            jax.ShapeDtypeStruct((slots, side, side), F32),
            jax.ShapeDtypeStruct((slots, side, side), BF16),
            jax.ShapeDtypeStruct((8, side), F32),
            jax.ShapeDtypeStruct(references.shape, BF16),
            jax.ShapeDtypeStruct((3, 8, side), F32),
        ],
        in_specs=[VMEM] * (3 + len(arrived)),
        out_specs=[VMEM] * 5,
        scratch_shapes=[
            pltpu.VMEM((2, side, side), F32),
            pltpu.SMEM((INFOS, max(8, own_bins)), jnp.int32),
        ],
        compiler_params=pltpu.CompilerParams(vmem_limit_bytes=VMEM_BYTES),
        name="ready",
    )(defocus, bfactor, references, *arrived)


def owner_kernel(bin_count, steps, focus_ref, damping_ref, current_ref, *rest):
    blocks, rest = blocks_of(rest[:-14]), rest[-14:]
    early_ctf, early_spectra, early_weight, early_sums = rest[:4]
    middle_ref, weight, label_ref, score_ref = rest[4:8]
    ctf, spectra, middle, sums, number, info = rest[8:]
    own_bins, side, _ = current_ref.shape
    early = early_ctf.shape[0]
    slots = len(steps)
    here = lax.axis_index("mic")

    labels = labels_of(blocks)
    for s, label in enumerate(labels):
        label_ref[s] = label
    places, senders = read_labels(labels)
    factors = ctf_factors(labels, focus_ref, damping_ref, side)
    sums[...] = early_sums[...]
    early_group, late_group = (early_ctf, early_spectra, 0), (ctf, spectra, early)
    shared = {}
    for s in range(early, slots):
        active = places[s] >= 0
        others = [places[t] == places[s] for t in range(slots) if t != s]
        shared[s] = active & functools.reduce(jnp.logical_or, others)

        @pl.when(active)
        def _(s=s):
            first_compare(places[s], factors, current_ref, late_group, sums, s, blocks[s])

    row = lax.broadcasted_iota(jnp.int32, (8, side), 0)
    weight[...] = jnp.where(row < early, early_weight[...], correlate(sums, side)[1])
    any_shared = functools.reduce(jnp.logical_or, shared.values())

    @pl.when(any_shared)
    def _():
        fill_info(info, places, own_bins, slots - early)
        update_shared(
            info, (early_group, late_group), weight, number, current_ref, middle, kind=LATE
        )

        @pl.loop(0, early)
        def _(s):
            p = info[PLACE, s]

            @pl.when((info[ACTIVE, s] > 0) & (info[LATE, p] > 0))
            def _():
                cross, model = second_compare(early_group, s, lambda rows, _: middle[p, rows, :])
                sums[0, pl.ds(s, 1), :] = jnp.sum(cross, axis=0, keepdims=True)
                sums[1, pl.ds(s, 1), :] = jnp.sum(model, axis=0, keepdims=True)

    for s in range(early, slots):
        alone = (places[s] >= 0) & jnp.logical_not(shared[s])
        update_and_compare(
            s, places[s], alone, shared[s], late_group, weight, sums, current_ref, middle
        )

    for s in range(early, slots):

        @pl.when(places[s] >= 0)
        def _(s=s):
            middle_ref[s - early] = middle[places[s]]

    correlation, weight[...] = correlate(sums, side)
    score_ref[...] = jnp.zeros(score_ref.shape, F32)
    lane = lax.broadcasted_iota(jnp.int32, (1, 128), 1)
    for s in range(slots):
        home = (here ^ steps[s]) * bin_count + lax.rem(senders[s], bin_count)
        hit = (lane == senders[s] // bin_count) & (places[s] >= 0)
        score_ref[home] = score_ref[home] + jnp.where(hit, correlation[s : s + 1, :], 0.0)

def owner_call(devices, bin_count, steps, defocus, bfactor, references, arrived, early):
    own_bins, side, _ = references.shape
    slots = len(steps)
    late = slots - early[0].shape[0]
    return pl.pallas_call(
        functools.partial(owner_kernel, bin_count, steps),
        out_shape=[
            jax.ShapeDtypeStruct((late, side, side), BF16),
            jax.ShapeDtypeStruct((8, side), F32),
            jax.ShapeDtypeStruct((slots, LABEL_ROWS, 128), F32),
            jax.ShapeDtypeStruct((devices, 1, 128), F32),
        ],
        in_specs=[VMEM] * (3 + len(arrived) + len(early)),
        out_specs=[VMEM] * 4,
        scratch_shapes=[
            pltpu.VMEM((late, side, side), F32),
            pltpu.VMEM((late, side, side), BF16),
            pltpu.VMEM(references.shape, BF16),
            pltpu.VMEM((3, 8, side), F32),
            pltpu.VMEM((2, side, side), F32),
            pltpu.SMEM((INFOS, max(8, own_bins)), jnp.int32),
        ],
        compiler_params=pltpu.CompilerParams(vmem_limit_bytes=VMEM_BYTES),
        name="owner",
    )(defocus, bfactor, references, *arrived, *early)


def last_kernel(
    focus_ref,
    damping_ref,
    weight,
    label_ref,
    early_spectra,
    early_middle,
    late_middle,
    late_ref,
    current_hbm,
    refined_ref,
    spectra,
    middle,
    ctf,
    number,
    info,
    sem,
):
    slots, side, _ = ctf.shape
    own_bins = refined_ref.shape[0]
    early = early_spectra.shape[0]
    labels = [label_ref[s] for s in range(slots)]
    places, _ = read_labels(labels)
    fill_info(info, places, own_bins)

    def unchanged(p):
        return pltpu.make_async_copy(current_hbm.at[p], refined_ref.at[p], sem.at[p])

    @pl.loop(0, own_bins)
    def _(p):
        @pl.when(info[MEMBERS, p] == 0)
        def _():
            unchanged(p).start()

    factors = ctf_factors(labels, focus_ref, damping_ref, side)
    for s in range(slots):

        @pl.when(places[s] >= 0)
        def _(s=s):
            for rows in chunks_of(side):
                ctf[s, rows, :] = ctf_chunk(factors, s, rows)
            if s < early:
                spectra[s] = early_spectra[s]
                middle[places[s]] = early_middle[places[s]]
            else:
                spectra[s] = image_of(late_ref.at[s - early], slice(0, side), side)
                middle[places[s]] = late_middle[s - early]

    update_shared(info, ((ctf, spectra, 0),), weight, number, middle, refined_ref)

    @pl.loop(0, slots)
    def _(s):
        @pl.when(info[ALONE, s] > 0)
        def _():
            p = info[PLACE, s]
            scale = weight[pl.ds(s, 1), :]
            for rows in chunks_of(side):
                values = spectra[s, rows, :].astype(F32)
                term, power, _ = shares(ctf, scale, s, rows, values)
                refined_ref[p, rows, :] = renew(middle[p, rows, :], term, power)

    @pl.loop(0, own_bins)
    def _(p):
        @pl.when(info[MEMBERS, p] == 0)
        def _():
            unchanged(p).wait()


def last_call(defocus, bfactor, references, weight, labels, kept):
    own_bins, side, _ = references.shape
    slots = labels.shape[0]
    return pl.pallas_call(
        last_kernel,
        out_shape=jax.ShapeDtypeStruct(references.shape, BF16),
        in_specs=[VMEM] * 8 + [HBM],
        out_specs=VMEM,
        scratch_shapes=[
            pltpu.VMEM((slots, side, side), BF16),
            pltpu.VMEM(references.shape, BF16),
            pltpu.VMEM((slots, side, side), F32),
            pltpu.VMEM((2, side, side), F32),
            pltpu.SMEM((INFOS, max(8, own_bins)), jnp.int32),
            pltpu.SemaphoreType.DMA((own_bins,)),
        ],
        compiler_params=pltpu.CompilerParams(vmem_limit_bytes=VMEM_BYTES),
        cost_estimate=pl.CostEstimate(flops=4 << 20, bytes_accessed=4 << 20, transcendentals=0),
        name="last",
    )(defocus, bfactor, weight, labels, *kept, in_hbm(references))


def exchange(blocks, axis):
    size = lax.axis_size(axis)
    return [blocks[0]] + [
        lax.ppermute(blocks[k], axis, [(i, i ^ k) for i in range(size)]) for k in range(1, size)
    ]


def body(images, offsets, ctf_group, particle_bin, bin_place, defocus, bfactor, references):
    mic_count = lax.axis_size("mic")
    bin_count = lax.axis_size("bin")
    particles, side, _ = images.shape
    own_bins = references.shape[0]
    capacity = (3 * particles + 2 * mic_count - 1) // (2 * mic_count)

    basis = jnp.asarray(hartley(side), BF16)
    operands = (bin_place, particle_bin, ctf_group, offsets, images, basis)
    operands = tuple(map(in_hbm, operands))
    far = 3 * bin_count // 8
    rest = bin_count - far
    sent_far = home_call(bin_count, own_bins, rest, far, operands)
    sent_near = home_call(bin_count, own_bins, 0, rest, operands, after=(sent_far[-1],))
    arrived = exchange(list(sent_near) + list(sent_far), "bin")

    last = mic_count - 1
    sizes = [[1] * capacity if step == 1 else [capacity] for step in range(mic_count)]
    sent = middle_call(mic_count, sizes, arrived[::-1])
    blocks = [(0, block) for block in sent[0]]
    for step in [t for t in range(1, mic_count) if t != last] + [last]:
        pairs = [(i, i ^ step) for i in range(mic_count)]
        blocks += [(step, lax.ppermute(block, "mic", pairs)) for block in sent[step]]
    steps = [step for step, block in blocks for _ in range(block.shape[0])]
    arrived = [block for _, block in blocks]
    tables = (defocus.reshape(1, -1), bfactor.reshape(1, -1), references)
    early = slice(0, -arrived[-1].shape[0])
    ctf, spectra, early_weight, middle, sums = ready_call(
        bin_count, steps[early], *tables, arrived[:-1]
    )
    late_middle, weight, labels, board = owner_call(
        mic_count * bin_count, bin_count, steps, *tables, arrived, (ctf, spectra, early_weight, sums)
    )
    back = lax.all_to_all(board, ("mic", "bin"), split_axis=0, concat_axis=0, tiled=True)
    refined = last_call(*tables, weight, labels, (spectra, middle, late_middle, arrived[-1]))
    return (refined, jnp.sum(back, axis=(0, 1))[:particles])


def solution(mesh):
    in_specs = (
        P(("mic", "bin"), None, None),
        P(None, ("mic", "bin")),
        P(("mic", "bin")),
        P(("mic", "bin")),
        P(),
        P(),
        P(),
        P(("mic", "bin"), None, None),
    )
    out_specs = (P(("mic", "bin"), None, None), P(("mic", "bin")))
    return jax.shard_map(body, mesh=mesh, in_specs=in_specs, out_specs=out_specs, check_vma=False)
```
